128 devices in a mesh: dp: 4 (over x_hi, core), seq: 32 (over z, x_lo, y).
Axes of the slice: x: 4 (x_hi: 2, x_lo: 2; x = x_hi * 2 + x_lo), y: 4, z: 4, core: 2. Of those that a mesh axis runs over, the one named last changes fastest.
Arguments:
- features: bfloat16 [4, 32768, 768], P('dp', 'seq'), may hold values from -24 to 24
- cotangent: bfloat16 [4, 32768, 768], P('dp', 'seq'), may hold values from -6 to 6
- strand_pairs: int32 [768], replicated, may hold values from 0 to 767, as said below
- dilations: int32 [2], replicated, may hold values from 1 to 64, as said below
- down_weight: bfloat16 [2, 768, 384], replicated, may hold values from -0.21875 to 0.21875
- conv_weight: bfloat16 [2, 3, 384, 384], replicated, may hold values from -0.1875 to 0.1875
- up_weight: bfloat16 [2, 384, 768], replicated, may hold values from -0.3125 to 0.3125
Outputs:
- block_out: bfloat16 [4, 32768, 768], P('dp', 'seq')
- input_grad: bfloat16 [4, 32768, 768], P('dp', 'seq')
- grad_down: float32 [2, 768, 384], replicated
- grad_conv: float32 [2, 3, 384, 384], replicated
- grad_up: float32 [2, 384, 768], replicated
The draws below stay inside these ranges and needn't reach their ends.
Inputs may be any that keep to these rules, and one draw needn't show every extreme that they name: strand_pairs is an involution without fixed points: strand_pairs[strand_pairs[c]] = c and strand_pairs[c] != c. `dilations`: every dilation is a power of two and some layer has dilation exactly 64.
All inputs are finite; a program needn't handle non-finite values.
Results may differ from the reference program's by a relative error of at most 0.02.
Values may be sent and summed in bfloat16 or wider, within the bound.
No kernel may reach another device: no remote copies, remote signals or barrier semaphores. Data moves between devices by JAX's collectives and lax.ppermute only.
A program may use at most 128 MiB of HBM per device.

```python
import math
import jax
import jax.numpy as jnp
from jax import lax

C = 768
B = 384
MAXDIL = 64
LAYERS = 2
POSITIONS = 32768
SEQS = 4


def draw_features(key, part):
    first, second, third = jax.random.split(key, 3)
    shape = (SEQS, POSITIONS, C)
    base = jax.random.truncated_normal(first, -4.0, 4.0, shape, jnp.float32)
    rows = jnp.exp(jax.random.uniform(second, (SEQS, POSITIONS, 1), jnp.float32, math.log(0.3), math.log(3.0)))
    cols = jnp.exp(jax.random.uniform(third, (1, 1, C), jnp.float32, math.log(0.5), math.log(2.0)))
    return (base * rows * cols).astype(jnp.bfloat16)


def draw_strand_pairs(key, part):
    order = jax.random.permutation(key, C).astype(jnp.int32)
    left = order[0::2]
    right = order[1::2]
    table = jnp.zeros((C,), jnp.int32)
    table = table.at[left].set(right)
    table = table.at[right].set(left)
    return table


def draw_dilations(key, part):
    first, second = jax.random.split(key, 2)
    levels = MAXDIL.bit_length() - 1
    powers = jax.random.randint(first, (LAYERS,), 0, levels)
    values = jnp.power(2, powers).astype(jnp.int32)
    chosen = jax.random.randint(second, (), 0, LAYERS)
    places = jnp.arange(LAYERS, dtype=jnp.int32)
    return jnp.where(places == chosen, MAXDIL, values).astype(jnp.int32)


def steps_of(own_key, dims, cuts, least, high):
    def one(position, blocks):
        heights = jax.random.uniform(jax.random.fold_in(jax.random.fold_in(own_key, 6), position), (blocks,), jnp.float32, least / len(cuts), high / len(cuts))
        return jnp.repeat(jnp.exp(heights), dims[position] // blocks).reshape((-1,) + (1,) * (len(dims) - position - 1))

    gain = one(*cuts[0])
    for cut in cuts[1:]:
        gain = gain * one(*cut)
    return gain


def gaussian(rng, extent, scale, most, pieces=(), kind=jnp.bfloat16):
    drawn = scale * jax.random.normal(rng, extent, jnp.float32)
    if pieces:
        drawn = drawn * steps_of(rng, extent, pieces, -0.22, 0.18)
    return jnp.clip(drawn, -most, most).astype(kind)


def setup_inputs(seed: int = 0) -> dict:
    streams_of = jax.random.split(jax.random.key(seed), 8)
    features = draw_features(jax.random.fold_in(streams_of[7], 71), 0)
    cotangent = gaussian(streams_of[1], (SEQS, POSITIONS, C), 1.0, 6.0, ((0, 4), (1, 32)))
    strand_pairs = draw_strand_pairs(jax.random.fold_in(streams_of[7], 71), 0)
    dilations = draw_dilations(jax.random.fold_in(streams_of[7], 71), 0)
    down_weight = gaussian(streams_of[4], (LAYERS, C, B), C ** -0.5, 0.21875)
    conv_weight = gaussian(streams_of[5], (LAYERS, 3, B, B), (3 * B) ** -0.5, 0.1875)
    up_weight = gaussian(streams_of[6], (LAYERS, B, C), B ** -0.5, 0.3125)
    return {"features": features, "cotangent": cotangent, "strand_pairs": strand_pairs, "dilations": dilations, "down_weight": down_weight, "conv_weight": conv_weight, "up_weight": up_weight}


eps = 1e-06

def complement(field, strand_pairs):
    return jnp.take(field[:, ::-1, :], strand_pairs, axis=2)

def product(form, left, right):
    return jnp.einsum(form, left.astype(jnp.float32), right.astype(jnp.float32))

def shifted(field, dilation, offset):
    padded = jnp.pad(field, ((0, 0), (MAXDIL, MAXDIL), (0, 0)))
    return lax.dynamic_slice_in_dim(padded, MAXDIL + offset * dilation, field.shape[1], 1)

def branch_forward(field, down, kernel, upward, dilation):
    wide = field.astype(jnp.float32)
    scale = lax.rsqrt(lax.optimization_barrier(jnp.mean(wide * wide, axis=-1, keepdims=True)) + eps)
    normed = (wide * scale).astype(jnp.bfloat16)
    inner = product('spc,cb->spb', normed, down).astype(jnp.bfloat16)
    pre = product('spi,ij->spj', shifted(inner, dilation, -1), kernel[0])
    pre = pre + product('spi,ij->spj', shifted(inner, dilation, 0), kernel[1])
    pre = pre + product('spi,ij->spj', shifted(inner, dilation, 1), kernel[2])
    act = jax.nn.gelu(pre).astype(jnp.bfloat16)
    result = product('spb,bc->spc', act, upward).astype(jnp.bfloat16)
    return (result, (field, scale, normed, inner, pre, act))

def branch_backward(saved, cot, down, kernel, upward, dilation):
    field, scale, normed, inner, pre, act = saved
    d_act = product('spc,bc->spb', cot, upward)
    g_up = product('spb,spc->bc', act, cot)
    d_pre = jax.vjp(jax.nn.gelu, pre)[1](d_act)[0].astype(jnp.bfloat16)
    d_inner = product('spj,ij->spi', shifted(d_pre, dilation, 1), kernel[0])
    d_inner = d_inner + product('spj,ij->spi', shifted(d_pre, dilation, 0), kernel[1])
    d_inner = d_inner + product('spj,ij->spi', shifted(d_pre, dilation, -1), kernel[2])
    d_inner = d_inner.astype(jnp.bfloat16)
    g_kernel = jnp.stack([product('spi,spj->ij', shifted(inner, dilation, k - 1), d_pre) for k in range(3)])
    d_norm = product('spb,cb->spc', d_inner, down)
    g_down = product('spc,spb->cb', normed, d_inner)
    wide = field.astype(jnp.float32)
    mixed = lax.optimization_barrier(jnp.mean(d_norm * wide, axis=-1, keepdims=True))
    d_field = (scale * d_norm - wide * scale ** 3 * mixed).astype(jnp.bfloat16)
    return (d_field, g_down, g_kernel, g_up)

def reference(features, cotangent, strand_pairs, dilations, down_weight, conv_weight, up_weight):
    stream = features
    saved = []
    for layer in range(LAYERS):
        down, kernel, upward, dilation = (down_weight[layer], conv_weight[layer], up_weight[layer], dilations[layer])
        out_a, keep_a = branch_forward(stream, down, kernel, upward, dilation)
        out_b, keep_b = branch_forward(complement(stream, strand_pairs), down, kernel, upward, dilation)
        saved.append((keep_a, keep_b))
        total = stream.astype(jnp.float32) + out_a.astype(jnp.float32)
        stream = (total + complement(out_b, strand_pairs).astype(jnp.float32)).astype(jnp.bfloat16)
    grad = cotangent.astype(jnp.float32)
    grads_down = [None] * LAYERS
    grads_conv = [None] * LAYERS
    grads_up = [None] * LAYERS
    for layer in reversed(range(LAYERS)):
        down, kernel, upward, dilation = (down_weight[layer], conv_weight[layer], up_weight[layer], dilations[layer])
        cot = grad.astype(jnp.bfloat16)
        d_a, ga_d, ga_k, ga_u = branch_backward(saved[layer][0], cot, down, kernel, upward, dilation)
        d_b, gb_d, gb_k, gb_u = branch_backward(saved[layer][1], complement(cot, strand_pairs), down, kernel, upward, dilation)
        grad = grad + d_a.astype(jnp.float32) + complement(d_b, strand_pairs).astype(jnp.float32)
        grads_down[layer] = ga_d + gb_d
        grads_conv[layer] = ga_k + gb_k
        grads_up[layer] = ga_u + gb_u
    factor = 1.0 / math.sqrt(features.shape[0] * features.shape[1])
    return (stream, grad.astype(jnp.bfloat16), jnp.stack(grads_down) * factor, jnp.stack(grads_conv) * factor, jnp.stack(grads_up) * factor)
```

```python
import functools
import math

import jax
import jax.numpy as jnp
from jax import lax
from jax.experimental import pallas as pl
from jax.experimental.pallas import tpu as pltpu
from jax.sharding import Mesh, PartitionSpec as P

C = 768
B = 384
PAD = 64
ROWS = 1024
TILE = 256
STEPS = ROWS // TILE
EPS = 1e-06
ROOT = math.sqrt(2.0 / math.pi)
CUBE = 0.044715
BF = jnp.bfloat16
F32 = jnp.float32
SEQ = ("z", "xl", "y")
CHIPS = ("xh", "z", "xl", "y")


def mm(left, right):
    return lax.dot_general(left, right, (((1,), (0,)), ((), ())), preferred_element_type=F32)


def mm_nt(left, right):
    return lax.dot_general(left, right, (((1,), (1,)), ((), ())), preferred_element_type=F32)


def mm_tn(left, right):
    return lax.dot_general(left, right, (((0,), (0,)), ((), ())), preferred_element_type=F32)


def swap(pairs_ref):
    cols = lax.broadcasted_iota(jnp.int32, (C, C), 1)
    return (cols == pairs_ref[...]).astype(F32).astype(BF)


def scale_of(wide):
    return lax.rsqrt(jnp.mean(wide * wide, axis=-1, keepdims=True) + EPS)


def fill(pad, mid_ref, top_ref, bot_ref):
    pad[0:PAD, :] = top_ref[...].astype(F32)
    pad[PAD : PAD + ROWS, :] = mid_ref[...].astype(F32)
    pad[PAD + ROWS :, :] = bot_ref[...].astype(F32)


def shift(pad, dil, step, before, after):
    base = pl.multiple_of(step * TILE + PAD, 8)

    @pl.when(dil >= 8)
    def _():
        for sign, ref in ((-1, before), (1, after)):
            ref[...] = pad[pl.ds(pl.multiple_of(base + sign * dil, 8), TILE), :].astype(BF)

    for small in (1, 2, 4):

        @pl.when(dil == small)
        def _():
            window = pad[pl.ds(pl.multiple_of(base - 8, 8), TILE + 16), :]
            before[...] = window[8 - small : 8 - small + TILE].astype(BF)
            after[...] = window[8 + small : 8 + small + TILE].astype(BF)


def centre(mid, step):
    return mid[pl.ds(pl.multiple_of(step * TILE, TILE), TILE), :]


def conv(first, last, mid, weight):
    rows_a = jnp.concatenate([first[:, :B], mid[:, :B], last[:, :B]], axis=1)
    rows_b = jnp.concatenate([last[:, B:], mid[:, B:], first[:, B:]], axis=1)
    both = mm(jnp.concatenate([rows_a, rows_b], axis=0), weight)
    return jnp.concatenate([both[:TILE], both[TILE:]], axis=1)


def gelu_both(pre):
    sq = pre * pre
    t = jnp.tanh(ROOT * (pre + CUBE * (pre * sq)))
    half = 0.5 + 0.5 * t
    slope = half + (0.5 * pre) * ((1.0 - t * t) * (ROOT + (3.0 * CUBE * ROOT) * sq))
    return pre * half, slope


def k_enter(pairs, down, x, dcat, normed, inner):
    @pl.when(pl.program_id(0) == 0)
    def _():
        dcat[:, :B] = down[...]
        dcat[:, B:] = mm(swap(pairs), down[...]).astype(BF)

    wide = x[...].astype(F32)
    n = (wide * scale_of(wide)).astype(BF)
    normed[...] = n
    inner[...] = mm(n, dcat[...]).astype(BF)


def k_prep(pairs, down1, up, kern, cot, dcat1, upcat, kern_t, d_act):
    @pl.when(pl.program_id(0) == 0)
    def _():
        s = swap(pairs)
        dcat1[:, :B] = down1[...]
        dcat1[:, B:] = mm(s, down1[...]).astype(BF)
        for layer in range(2):
            upcat[layer, :B, :] = up[layer]
            upcat[layer, B:, :] = mm(up[layer], s).astype(BF)
            for k in range(3):
                kern_t[layer, k * B : (k + 1) * B, :] = kern[layer, k].astype(F32).T.astype(BF)

    d_act[...] = mm_nt(cot[...], upcat[1]).astype(BF)


def k_middle(dil, mid, top, bot, weight, x, upcat, dcat, act, slope, tm, tp, stream, normed, inner, pad):
    step = pl.program_id(0)

    @pl.when(step == 0)
    def _():
        fill(pad, mid, top, bot)

    shift(pad, dil[0], step, tm, tp)
    g, s = gelu_both(conv(tm[...], tp[...], centre(mid, step), weight[...]))
    g = g.astype(BF)
    act[...] = g
    slope[...] = s.astype(BF)
    out = (x[...].astype(F32) + mm(g, upcat[...])).astype(BF)
    stream[...] = out
    wide = out.astype(F32)
    n = (wide * scale_of(wide)).astype(BF)
    normed[...] = n
    inner[...] = mm(n, dcat[...]).astype(BF)


def k_top(dil, mid, top, bot, weight, d_act, act, d_pre, tm, tp, pad):
    step = pl.program_id(0)

    @pl.when(step == 0)
    def _():
        fill(pad, mid, top, bot)

    shift(pad, dil[0], step, tm, tp)
    g, s = gelu_both(conv(tm[...], tp[...], centre(mid, step), weight[...]))
    act[...] = g.astype(BF)
    d_pre[...] = (d_act[...].astype(F32) * s).astype(BF)


def weight_sums(factor, pairs, act, cot, tm, mid, tp, d_pre, g_up, g_conv):
    up = mm_tn(act[...], cot[...]) * factor
    both = up[:B] + mm(up[B:].astype(BF), swap(pairs))
    g_up[0:B, :] = both[:, :B].astype(BF)
    g_up[B:, :] = both[:, B:].astype(BF)
    order = (tm, mid, tp)
    for k in range(3):
        total = mm_tn(order[k][:, :B], d_pre[:, :B]) + mm_tn(order[2 - k][:, B:], d_pre[:, B:])
        g_conv[k * B : (k + 1) * B, :] = (total * factor).astype(BF)


def k_sums_out(factor, pairs, act, cot, tm, mid, tp, d_pre, stream, upcat, g_up, g_conv, out):
    out[...] = (stream[...].astype(F32) + mm(act[...], upcat[...])).astype(BF)
    weight_sums(factor, pairs, act, cot, tm, mid, tp, d_pre, g_up, g_conv)


def k_sums(factor, pairs, act, cot, tm, mid, tp, d_pre, g_up, g_conv):
    weight_sums(factor, pairs, act, cot, tm, mid, tp, d_pre, g_up, g_conv)


def down_sum(factor, pairs, normed, d_inner, g_down):
    total = mm_tn(normed[...], d_inner[...]) * factor
    g_down[...] = (total[:, :B] + mm(swap(pairs), total[:, B:].astype(BF))).astype(BF)


def norm_back(v, d_norm):
    wide = v.astype(F32)
    scale = scale_of(wide)
    mixed = jnp.mean(d_norm * wide, axis=-1, keepdims=True)
    return scale * d_norm - wide * (scale * scale * scale * mixed)


def k_back(factor, dil, pairs, mid, top, bot, weight, normed, stream, cot, dcat, upcat, slope,
           grad, d_pre, g_down, pad, before, after, d_inner):
    step = pl.program_id(0)

    @pl.when(step == 0)
    def _():
        fill(pad, mid, top, bot)

    shift(pad, dil[0], step, before, after)
    di = conv(after[...], before[...], centre(mid, step), weight[...]).astype(BF)
    d_inner[pl.ds(pl.multiple_of(step * TILE, TILE), TILE), :] = di
    g = (cot[...].astype(F32) + norm_back(stream[...], mm_nt(di, dcat[...]))).astype(BF)
    grad[...] = g
    d_pre[...] = (mm_nt(g, upcat[...]) * slope[...].astype(F32)).astype(BF)

    @pl.when(step == STEPS - 1)
    def _():
        down_sum(factor, pairs, normed, d_inner, g_down)


def k_last(factor, dil, pairs, mid, top, bot, weight, normed, g_down, d_inner, pad, before, after):
    step = pl.program_id(0)

    @pl.when(step == 0)
    def _():
        fill(pad, mid, top, bot)

    shift(pad, dil[0], step, before, after)
    di = conv(after[...], before[...], centre(mid, step), weight[...]).astype(BF)
    d_inner[pl.ds(pl.multiple_of(step * TILE, TILE), TILE), :] = di

    @pl.when(step == STEPS - 1)
    def _():
        down_sum(factor, pairs, normed, d_inner, g_down)


def k_input(d_inner, x, cot, dcat, out):
    out[...] = (cot[...].astype(F32) + norm_back(x[...], mm_nt(d_inner[...], dcat[...]))).astype(BF)


def tile(width=C):
    return pl.BlockSpec((TILE, width), lambda i: (i, 0))


def whole(*shape):
    return pl.BlockSpec(shape, lambda i: (0,) * len(shape))


def scalar():
    return pl.BlockSpec(memory_space=pltpu.SMEM)


def shape(*dims):
    return jax.ShapeDtypeStruct(dims, BF)


def call(body, steps, ins, outs, scratch, flops, name):
    size = lambda s: 2 * math.prod(s.shape)
    return pl.pallas_call(
        body,
        grid=(steps,),
        in_specs=ins,
        out_specs=[spec for spec, _ in outs],
        out_shape=[form for _, form in outs],
        scratch_shapes=scratch,
        compiler_params=pltpu.CompilerParams(vmem_limit_bytes=48 * 1024 * 1024),
        cost_estimate=pl.CostEstimate(
            flops=int(flops), bytes_accessed=2 * sum(size(f) for _, f in outs), transcendentals=0
        ),
        name=name,
    )


UNIT = 2 * ROWS * C * C
FULL = (tile(), shape(ROWS, C))
PIECE = pltpu.VMEM((TILE, C), BF)
PADDED = pltpu.VMEM((ROWS + 2 * PAD, C), F32)


def edges(cells):
    count = 32
    top = lax.ppermute(cells[ROWS - PAD :], SEQ, [(i, i + 1) for i in range(count - 1)])
    bot = lax.ppermute(cells[:PAD], SEQ, [(i + 1, i) for i in range(count - 1)])
    return top, bot


def total(flat):
    rows = flat.shape[0]
    half = rows // 2
    core = lax.axis_index("core")
    mine = lax.dynamic_slice_in_dim(flat, core * half, half, 0)
    theirs = lax.dynamic_slice_in_dim(flat, (1 - core) * half, half, 0)
    got = lax.ppermute(theirs, "core", [(0, 1), (1, 0)])
    part = (mine.astype(F32) + got.astype(F32)).astype(BF)
    part = part.reshape(64, half // 64, flat.shape[1])
    part = lax.all_to_all(part, CHIPS, 0, 0, tiled=True)
    share = jnp.sum(part.astype(F32), axis=0).astype(BF)
    every = lax.all_to_all(jnp.broadcast_to(share[None], part.shape), CHIPS, 0, 0, tiled=True)
    every = every.reshape(half, flat.shape[1])
    other = lax.ppermute(every, "core", [(0, 1), (1, 0)])
    first = jnp.where(core == 0, every, other)
    second = jnp.where(core == 0, other, every)
    return jnp.concatenate([first, second], axis=0).astype(F32)


def split(flat):
    up = flat[: 2 * B]
    up = jnp.concatenate([up[:B], up[B:]], axis=1)
    return flat[2 * B + 3 * B :], flat[2 * B : 5 * B].reshape(3, B, B), up


def local(features, cotangent, strand_pairs, dilations, down_weight, conv_weight, up_weight):
    x = features[0]
    cot = cotangent[0]
    pairs = strand_pairs.reshape(C, 1)
    factor = 1.0 / math.sqrt(131072.0)
    dil = [dilations[layer : layer + 1] for layer in range(2)]
    kern = [conv_weight[layer].reshape(3 * B, B) for layer in range(2)]
    square = whole(C, C)
    halo = whole(PAD, C)
    resident = whole(ROWS, C)
    taps_w = whole(3 * B, B)

    dcat0, normed0, inner0 = call(
        k_enter, STEPS, [whole(C, 1), whole(C, B), tile()],
        [(square, shape(C, C)), FULL, FULL], [], UNIT, "enter",
    )(pairs, down_weight[0], x)
    top, bot = edges(inner0)
    dcat1, upcat, kern_t, d_act1 = call(
        k_prep, STEPS,
        [whole(C, 1), whole(C, B), whole(2, B, C), whole(2, 3, B, B), tile()],
        [(square, shape(C, C)), (whole(2, C, C), shape(2, C, C)), (whole(2, 3 * B, B), shape(2, 3 * B, B)), FULL],
        [], 2.5 * UNIT, "prep",
    )(pairs, down_weight[1], up_weight, conv_weight, cot)
    up0, up1 = upcat[0], upcat[1]
    act0, slope0, tm0, tp0, stream1, normed1, inner1 = call(
        k_middle, STEPS,
        [scalar(), resident, halo, halo, taps_w, tile(), square, square],
        [FULL] * 7, [PADDED], 4 * UNIT, "middle",
    )(dil[0], inner0, top, bot, kern[0], x, up0, dcat1)
    top, bot = edges(inner1)
    act1, d_pre1, tm1, tp1 = call(
        k_top, STEPS, [scalar(), resident, halo, halo, taps_w, tile()],
        [FULL] * 4, [PADDED], 2 * UNIT, "top",
    )(dil[1], inner1, top, bot, kern[1], d_act1)
    top, bot = edges(d_pre1)
    ups = (whole(2 * B, B), shape(2 * B, B))
    convs = (whole(3 * B, B), shape(3 * B, B))
    downs = (whole(C, B), shape(C, B))
    g_up1, g_conv1, out = call(
        functools.partial(k_sums_out, factor), 1, [whole(C, 1)] + [resident] * 7 + [square],
        [ups, convs, (resident, shape(ROWS, C))], [], 4 * UNIT, "sums_out",
    )(pairs, act1, cot, tm1, inner1, tp1, d_pre1, stream1, up1)
    grad, d_pre0, g_down1 = call(
        functools.partial(k_back, factor), STEPS,
        [scalar(), whole(C, 1), resident, halo, halo, taps_w, resident, tile(), tile(), square, square, tile()],
        [FULL, FULL, downs], [PADDED, PIECE, PIECE, pltpu.VMEM((ROWS, C), BF)], 5 * UNIT, "back",
    )(dil[1], pairs, d_pre1, top, bot, kern_t[1], normed1, stream1, cot, dcat1, up0, slope0)
    top, bot = edges(d_pre0)
    total1 = total(jnp.concatenate([g_up1, g_conv1, g_down1], axis=0))
    g_up0, g_conv0 = call(
        functools.partial(k_sums, factor), 1, [whole(C, 1)] + [resident] * 6,
        [ups, convs], [], 3 * UNIT, "sums",
    )(pairs, act0, grad, tm0, inner0, tp0, d_pre0)
    g_down0, d_inner0 = call(
        functools.partial(k_last, factor), STEPS,
        [scalar(), whole(C, 1), resident, halo, halo, taps_w, resident],
        [downs, (resident, shape(ROWS, C))], [PADDED, PIECE, PIECE], 3 * UNIT, "last",
    )(dil[0], pairs, d_pre0, top, bot, kern_t[0], normed0)
    total0 = total(jnp.concatenate([g_up0, g_conv0, g_down0], axis=0))
    (input_grad,) = call(
        k_input, STEPS, [tile(), tile(), tile(), square], [FULL], [], UNIT, "input",
    )(d_inner0, x, grad, dcat0)
    pieces = [split(total0), split(total1)]
    stacked = [jnp.stack([pieces[0][i], pieces[1][i]]) for i in range(3)]
    return (out[None], input_grad[None], *stacked)


def solution(mesh):
    fine = Mesh(mesh.devices.reshape(2, 2, 4, 2, 4), ("xh", "core", "z", "xl", "y"))
    rows = P(("xh", "core"), SEQ, None)
    in_specs = (rows, rows, P(), P(), P(), P(), P())
    out_specs = (rows, rows, P(), P(), P())
    return jax.shard_map(local, mesh=fine, in_specs=in_specs, out_specs=out_specs, check_vma=False)
```

```python
import functools
import math

import jax
import jax.numpy as jnp
from jax import lax
from jax.experimental import pallas as pl
from jax.experimental.pallas import tpu as pltpu
from jax.sharding import Mesh, PartitionSpec as P

C = 768
B = 384
PAD = 64
ROWS = 1024
TILE = 256
STEPS = ROWS // TILE
BLOCKS = 32
MID_ROWS, TOP_ROWS, BACK_ROWS = ROWS + 6 * PAD, ROWS + 4 * PAD, ROWS + 2 * PAD
MID_TILE, TOP_TILE, BACK_TILE = MID_ROWS // 4, TOP_ROWS // 4, BACK_ROWS // 3
EPS = 1e-06
ROOT = math.sqrt(2.0 / math.pi)
CUBE = 0.044715
BF = jnp.bfloat16
F32 = jnp.float32
SEQ = ("z", "xl", "y")
CHIPS = ("xh", "z", "xl", "y")


def mm(left, right):
    return lax.dot_general(left, right, (((1,), (0,)), ((), ())), preferred_element_type=F32)


def mm_nt(left, right):
    return lax.dot_general(left, right, (((1,), (1,)), ((), ())), preferred_element_type=F32)


def mm_tn(left, right):
    return lax.dot_general(left, right, (((0,), (0,)), ((), ())), preferred_element_type=F32)


def swap(pairs_ref):
    cols = lax.broadcasted_iota(jnp.int32, (C, C), 1)
    return (cols == pairs_ref[...]).astype(F32).astype(BF)


def scale_of(wide):
    return lax.rsqrt(jnp.mean(wide * wide, axis=-1, keepdims=True) + EPS)


def lay(dst, top, mid, bot):
    start = 0
    for piece in (top, mid, bot):
        rows = piece.shape[0]
        dst[start : start + rows, :] = piece.astype(dst.dtype)
        start += rows


def shift(pad, dil, start, before, after):
    rows = before.shape[0]
    base = pl.multiple_of(start + PAD, 8)

    @pl.when(dil >= 8)
    def _():
        for sign, ref in ((-1, before), (1, after)):
            ref[...] = pad[pl.ds(pl.multiple_of(base + sign * dil, 8), rows), :].astype(BF)

    for small in (1, 2, 4):

        @pl.when(dil == small)
        def _():
            window = pad[pl.ds(pl.multiple_of(base - 8, 8), rows + 16), :]
            before[...] = window[8 - small : 8 - small + rows].astype(BF)
            after[...] = window[8 + small : 8 + small + rows].astype(BF)


def centre(pad, start, rows):
    return pad[pl.ds(pl.multiple_of(start + PAD, 8), rows), :].astype(BF)


def conv(first, last, mid, weight):
    rows = mid.shape[0]
    rows_a = jnp.concatenate([first[:, :B], mid[:, :B], last[:, :B]], axis=1)
    rows_b = jnp.concatenate([last[:, B:], mid[:, B:], first[:, B:]], axis=1)
    both = mm(jnp.concatenate([rows_a, rows_b], axis=0), weight)
    return jnp.concatenate([both[:rows], both[rows:]], axis=1)


def inside(block, start, values):
    rows = lax.broadcasted_iota(jnp.int32, (values.shape[0], 1), 0) + (block * ROWS + start)
    return jnp.where((rows >= 0) & (rows < BLOCKS * ROWS), values, 0.0)


def gelu_both(pre):
    sq = pre * pre
    t = jnp.tanh(ROOT * (pre + CUBE * (pre * sq)))
    half = 0.5 + 0.5 * t
    slope = half + (0.5 * pre) * ((1.0 - t * t) * (ROOT + (3.0 * CUBE * ROOT) * sq))
    return pre * half, slope


def k_enter(pairs, down, x, dcat, normed, inner):
    @pl.when(pl.program_id(0) == 0)
    def _():
        dcat[:, :B] = down[...]
        dcat[:, B:] = mm(swap(pairs), down[...]).astype(BF)

    wide = x[...].astype(F32)
    n = (wide * scale_of(wide)).astype(BF)
    normed[...] = n
    inner[...] = mm(n, dcat[...]).astype(BF)


def k_prep(pairs, down1, up, kern, dcat1, upcat, kern_t):
    s = swap(pairs)
    dcat1[:, :B] = down1[...]
    dcat1[:, B:] = mm(s, down1[...]).astype(BF)
    for layer in range(2):
        upcat[layer, :B, :] = up[layer]
        upcat[layer, B:, :] = mm(up[layer], s).astype(BF)
        for k in range(3):
            kern_t[layer, k * B : (k + 1) * B, :] = kern[layer, k].astype(F32).T.astype(BF)


def k_middle(dil, block, mid, x, top, bot, dcat0, weight, upcat, dcat,
             act, slope, tm, tc, tp, stream, normed, inner, pad, field):
    start = pl.program_id(0) * MID_TILE

    @pl.when(pl.program_id(0) == 0)
    def _():
        lay(field, top[PAD:, :], x[...], bot[: 4 * PAD - PAD, :])
        ends = []
        for halo in (top, bot):
            wide = halo[...].astype(F32)
            ends.append(mm((wide * scale_of(wide)).astype(BF), dcat0[...]).astype(BF))
        lay(pad, ends[0], mid[...], ends[1])

    shift(pad, dil[0], start, tm, tp)
    m = centre(pad, start, MID_TILE)
    tc[...] = m
    g, s = gelu_both(conv(tm[...], tp[...], m, weight[...]))
    g = g.astype(BF)
    act[...] = g
    slope[...] = s.astype(BF)
    rows = pl.ds(pl.multiple_of(start, 16), MID_TILE)
    out = (field[rows, :].astype(F32) + mm(g, upcat[...])).astype(BF)
    stream[...] = out
    wide = out.astype(F32)
    n = (wide * scale_of(wide)).astype(BF)
    normed[...] = n
    inner[...] = inside(block[0], start - 3 * PAD, mm(n, dcat[...])).astype(BF)


def k_top(dil, mid, cot, ctop, cbot, weight, upcat, act, d_pre, tm, tc, tp, pad, grad):
    start = pl.program_id(0) * TOP_TILE

    @pl.when(pl.program_id(0) == 0)
    def _():
        pad[...] = mid[...].astype(F32)
        lay(grad, ctop[...], cot[...], cbot[...])

    shift(pad, dil[0], start, tm, tp)
    m = centre(pad, start, TOP_TILE)
    tc[...] = m
    rows = pl.ds(pl.multiple_of(start, 16), TOP_TILE)
    d_act = mm_nt(grad[rows, :], upcat[...])
    g, s = gelu_both(conv(tm[...], tp[...], m, weight[...]))
    act[...] = g.astype(BF)
    d_pre[...] = (d_act * s).astype(BF)


def put(ref, start, value):
    rows, cols = value.shape
    for i in range(cols // LANES):
        ref[start + i * rows : start + (i + 1) * rows, :] = value[:, i * LANES : (i + 1) * LANES].astype(BF)


def take(ref, start, rows, cols):
    pieces = [ref[start + i * rows : start + (i + 1) * rows, :] for i in range(cols // LANES)]
    return jnp.concatenate(pieces, axis=1).astype(F32)


def own(ref, before):
    return ref[before : before + ROWS, :]


def weight_sums(factor, pairs, act, cot, taps, d_pre, rest):
    up = mm_tn(act, cot) * factor
    put(rest, 0, up[:B] + mm(up[B:].astype(BF), swap(pairs)))
    for k in range(3):
        total = mm_tn(taps[k][:, :B], d_pre[:, :B]) + mm_tn(taps[2 - k][:, B:], d_pre[:, B:])
        put(rest, UP + k * 3 * B, total * factor)
    rest[REST - LANES :, :] = jnp.zeros((LANES, LANES), BF)


def sort_out(core, lower, upper, send, keep):
    @pl.when(core[0] == 0)
    def _():
        send[...] = upper[...]
        keep[...] = lower[...]

    @pl.when(core[0] != 0)
    def _():
        send[...] = lower[...]
        keep[...] = upper[...]


def k_sums_out(factor, pairs, act, cot, tm, tc, tp, d_pre, stream, upcat, rest, out):
    a = own(act, 2 * PAD)
    out[...] = (own(stream, 3 * PAD).astype(F32) + mm(a, upcat[...])).astype(BF)
    taps = [own(ref, 2 * PAD) for ref in (tm, tc, tp)]
    weight_sums(factor, pairs, a, cot[...], taps, own(d_pre, 2 * PAD), rest)


def k_sums(factor, core, pairs, act, cot, tm, tc, tp, d_pre, upper, send, keep, rest):
    taps = [own(ref, 3 * PAD) for ref in (tm, tc, tp)]
    weight_sums(factor, pairs, own(act, 3 * PAD), own(cot, PAD), taps, own(d_pre, PAD), rest)
    sort_out(core, rest, upper, send, keep)


def down_sum(factor, pairs, normed, d_inner, down):
    total = mm_tn(normed, d_inner) * factor
    put(down, 0, total[:, :B] + mm(swap(pairs), total[:, B:].astype(BF)))


def k_join(keep_a, got_a, keep_b, got_b, out):
    out[:REST, :] = (keep_a[...].astype(F32) + got_a[...].astype(F32)).astype(BF)
    out[REST:, :] = (keep_b[...].astype(F32) + got_b[...].astype(F32)).astype(BF)


def k_share(parts, out):
    share = jnp.sum(parts[...].astype(F32), axis=0).astype(BF)
    out[...] = jnp.broadcast_to(share[None], out.shape)


def k_finish(core, own, other, down, kern, up):
    layer = pl.program_id(0)
    for mine, ref in ((True, own), (False, other)):

        @pl.when((core[0] == layer) == mine)
        def _():
            up[0] = take(ref, 0, B, C)
            for k in range(3):
                kern[0, k] = take(ref, UP + k * 3 * B, B, B)
            down[0] = take(ref, REST, C, B)


def norm_back(v, d_norm):
    wide = v.astype(F32)
    scale = scale_of(wide)
    mixed = jnp.mean(d_norm * wide, axis=-1, keepdims=True)
    return scale * d_norm - wide * (scale * scale * scale * mixed)


def k_back(factor, dil, block, pairs, mid, weight, normed, stream, cot, ctop, cbot, dcat, upcat, slope,
           grad, d_pre, down, pad, before, after, d_inner, given):
    start = pl.program_id(0) * BACK_TILE

    @pl.when(pl.program_id(0) == 0)
    def _():
        pad[...] = mid[...].astype(F32)
        lay(given, ctop[PAD:, :], cot[...], cbot[:PAD, :])

    shift(pad, dil[0], start, before, after)
    di = conv(after[...], before[...], centre(pad, start, BACK_TILE), weight[...]).astype(BF)
    rows = pl.ds(pl.multiple_of(start, 16), BACK_TILE)
    saved = pl.ds(pl.multiple_of(start + 2 * PAD, 16), BACK_TILE)
    d_inner[rows, :] = di
    g = given[rows, :].astype(F32) + norm_back(stream[saved, :], mm_nt(di, dcat[...]))
    g = inside(block[0], start - PAD, g).astype(BF)
    grad[...] = g
    d_pre[...] = (mm_nt(g, upcat[...]) * slope[saved, :].astype(F32)).astype(BF)

    @pl.when(pl.program_id(0) == pl.num_programs(0) - 1)
    def _():
        down_sum(factor, pairs, own(normed, 3 * PAD), own(d_inner, PAD), down)


def k_last(factor, core, dil, pairs, mid, weight, normed, upper, send, keep, d_inner, pad, before, after, down):
    start = pl.program_id(0) * TILE

    @pl.when(pl.program_id(0) == 0)
    def _():
        pad[...] = mid[...].astype(F32)

    shift(pad, dil[0], start, before, after)
    di = conv(after[...], before[...], centre(pad, start, TILE), weight[...]).astype(BF)
    d_inner[pl.ds(pl.multiple_of(start, 16), TILE), :] = di

    @pl.when(pl.program_id(0) == pl.num_programs(0) - 1)
    def _():
        down_sum(factor, pairs, normed[...], d_inner[...], down)
        sort_out(core, down, upper, send, keep)


def k_input(d_inner, x, cot, dcat, out):
    rows = pl.ds(pl.multiple_of(pl.program_id(0) * TILE + PAD, 16), TILE)
    out[...] = (cot[rows, :].astype(F32) + norm_back(x[...], mm_nt(d_inner[...], dcat[...]))).astype(BF)


def tile(rows=TILE):
    return pl.BlockSpec((rows, C), lambda i: (i, 0))


def whole(*shape):
    return pl.BlockSpec(shape, lambda i: (0,) * len(shape))


def scalar():
    return pl.BlockSpec(memory_space=pltpu.SMEM)


def shape(*dims, kind=BF):
    return jax.ShapeDtypeStruct(dims, kind)


def call(body, steps, ins, outs, scratch, flops, name):
    size = lambda s: 2 * math.prod(s.shape)
    return pl.pallas_call(
        body,
        grid=(steps,),
        in_specs=ins,
        out_specs=[spec for spec, _ in outs],
        out_shape=[form for _, form in outs],
        scratch_shapes=scratch,
        compiler_params=pltpu.CompilerParams(vmem_limit_bytes=48 * 1024 * 1024),
        cost_estimate=pl.CostEstimate(
            flops=int(flops), bytes_accessed=2 * sum(size(f) for _, f in outs), transcendentals=0
        ),
        name=name,
    )


LANES = 128
UP = 6 * B
REST = UP + 9 * B + LANES
DOWN = 6 * B
UNIT = 2 * ROWS * C * C
FULL = (tile(), shape(ROWS, C))


def store(rows, kind=BF):
    return pltpu.VMEM((rows, C), kind)


def edges(cells, rows):
    top = lax.ppermute(cells[ROWS - rows :], SEQ, [(i, i + 1) for i in range(BLOCKS - 1)])
    bot = lax.ppermute(cells[:rows], SEQ, [(i + 1, i) for i in range(BLOCKS - 1)])
    return top, bot


SWAP = [(0, 1), (1, 0)]
SHARES = (64, (REST + DOWN) // 64, LANES)


def exchange(parts):
    return lax.all_to_all(parts, CHIPS, 0, 0, tiled=True)


def other_core(cells):
    return lax.ppermute(cells, "core", SWAP)


def local(features, cotangent, strand_pairs, dilations, down_weight, conv_weight, up_weight):
    x = features[0]
    cot = cotangent[0]
    pairs = strand_pairs.reshape(C, 1)
    factor = 1.0 / math.sqrt(131072.0)
    dil = [dilations[layer : layer + 1] for layer in range(2)]
    kern = [conv_weight[layer].reshape(3 * B, B) for layer in range(2)]
    block = lax.axis_index(SEQ).reshape(1)
    square = whole(C, C)
    resident = whole(ROWS, C)
    taps_w = whole(3 * B, B)

    top, bot = edges(x, 4 * PAD)
    ctop, cbot = edges(cot, 2 * PAD)
    dcat0, normed0, inner0 = call(
        k_enter, STEPS, [whole(C, 1), whole(C, B), tile()],
        [(square, shape(C, C)), FULL, FULL], [], UNIT, "enter",
    )(pairs, down_weight[0], x)
    dcat1, upcat, kern_t = call(
        k_prep, 1, [whole(C, 1), whole(C, B), whole(2, B, C), whole(2, 3, B, B)],
        [(square, shape(C, C)), (whole(2, C, C), shape(2, C, C)), (whole(2, 3 * B, B), shape(2, 3 * B, B))],
        [], 2.5 * UNIT, "prep",
    )(pairs, down_weight[1], up_weight, conv_weight)
    up0, up1 = upcat[0], upcat[1]
    mid = (tile(MID_TILE), shape(MID_ROWS, C))
    act0, slope0, tm0, tc0, tp0, stream1, normed1, inner1 = call(
        k_middle, 4,
        [scalar(), scalar(), resident, resident, whole(4 * PAD, C), whole(4 * PAD, C), square, taps_w, square, square],
        [mid] * 8, [store(ROWS + 8 * PAD, F32), store(MID_ROWS)], 6 * UNIT, "middle",
    )(dil[0], block, inner0, x, top, bot, dcat0, kern[0], up0, dcat1)
    upper = (tile(TOP_TILE), shape(TOP_ROWS, C))
    c_halo = whole(2 * PAD, C)
    act1, d_pre1, tm1, tc1, tp1 = call(
        k_top, 4, [scalar(), whole(MID_ROWS, C), resident, c_halo, c_halo, taps_w, square],
        [upper] * 5, [store(MID_ROWS, F32), store(TOP_ROWS)], 3 * UNIT, "top",
    )(dil[1], inner1, cot, ctop, cbot, kern[1], up1)
    core = lax.axis_index("core").reshape(1)
    sums = (whole(REST, LANES), shape(REST, LANES))
    downs = (whole(DOWN, LANES), shape(DOWN, LANES))
    joined = (whole(REST + DOWN, LANES), shape(REST + DOWN, LANES))
    shares = (whole(*SHARES), shape(*SHARES))
    wide_top, wide_mid, wide_back = whole(TOP_ROWS, C), whole(MID_ROWS, C), whole(BACK_ROWS, C)
    rest1, out = call(
        functools.partial(k_sums_out, factor), 1,
        [whole(C, 1), wide_top, resident] + [wide_top] * 4 + [wide_mid, square],
        [sums, (resident, shape(ROWS, C))], [], 4 * UNIT, "sums_out",
    )(pairs, act1, cot, tm1, tc1, tp1, d_pre1, stream1, up1)
    back = (tile(BACK_TILE), shape(BACK_ROWS, C))
    grad, d_pre0, down1 = call(
        functools.partial(k_back, factor), 3,
        [scalar(), scalar(), whole(C, 1), wide_top, taps_w, wide_mid, wide_mid, resident, c_halo, c_halo,
         square, square, wide_mid],
        [back, back, downs],
        [store(TOP_ROWS, F32), store(BACK_TILE), store(BACK_TILE), store(BACK_ROWS), store(BACK_ROWS)],
        5 * UNIT, "back",
    )(dil[1], block, pairs, d_pre1, kern_t[1], normed1, stream1, cot, ctop, cbot, dcat1, up0, slope0)
    send_a, keep_a = call(
        functools.partial(k_sums, factor), 1,
        [scalar(), whole(C, 1), wide_mid, wide_back, wide_mid, wide_mid, wide_mid, wide_back, sums[0]],
        [sums, sums], [pltpu.VMEM((REST, LANES), BF)], 3 * UNIT, "sums",
    )(core, pairs, act0, grad, tm0, tc0, tp0, d_pre0, rest1)
    send_b, keep_b, d_inner0 = call(
        functools.partial(k_last, factor), STEPS,
        [scalar(), scalar(), whole(C, 1), wide_back, taps_w, resident, downs[0]],
        [downs, downs, (resident, shape(ROWS, C))],
        [store(BACK_ROWS, F32), store(TILE), store(TILE), pltpu.VMEM((DOWN, LANES), BF)],
        3 * UNIT, "last",
    )(core, dil[0], pairs, d_pre0, kern_t[0], normed0, down1)
    (parts,) = call(
        k_join, 1, [sums[0], sums[0], downs[0], downs[0]], [joined], [], 0, "join",
    )(keep_a, other_core(send_a), keep_b, other_core(send_b))
    parts = exchange(parts.reshape(SHARES))
    (shared,) = call(k_share, 1, [shares[0]], [shares], [], 0, "share")(parts)
    (input_grad,) = call(
        k_input, STEPS, [tile(), tile(), wide_back, square], [FULL], [], UNIT, "input",
    )(d_inner0, x, grad, dcat0)
    own = exchange(shared).reshape(REST + DOWN, LANES)
    layered = lambda *dims: (
        pl.BlockSpec((1,) + dims, lambda i: (i,) + (0,) * len(dims)), shape(2, *dims, kind=F32)
    )
    grads = call(
        k_finish, 2, [scalar()] + [joined[0]] * 2,
        [layered(C, B), layered(3, B, B), layered(B, C)], [], 0, "finish",
    )(core, own, other_core(own))
    return (out[None], input_grad[None], *grads)


def solution(mesh):
    fine = Mesh(mesh.devices.reshape(2, 2, 4, 2, 4), ("xh", "core", "z", "xl", "y"))
    rows = P(("xh", "core"), SEQ, None)
    in_specs = (rows, rows, P(), P(), P(), P(), P())
    out_specs = (rows, rows, P(), P(), P())
    return jax.shard_map(local, mesh=fine, in_specs=in_specs, out_specs=out_specs, check_vma=False)
```

```python
import functools
import math

import jax
import jax.numpy as jnp
from jax import lax
from jax.experimental import pallas as pl
from jax.experimental.pallas import tpu as pltpu
from jax.sharding import Mesh, PartitionSpec as P

C = 768
B = 384
PAD = 64
ROWS = 1024
TILE = 256
STEPS = ROWS // TILE
BLOCKS = 32
MID_ROWS, TOP_ROWS, BACK_ROWS = ROWS + 6 * PAD, ROWS + 4 * PAD, ROWS + 2 * PAD
MID_TILE, TOP_TILE, BACK_TILE = MID_ROWS // 4, TOP_ROWS // 4, BACK_ROWS // 3
EPS = 1e-06
ROOT = math.sqrt(2.0 / math.pi)
CUBE = 0.044715
BF = jnp.bfloat16
F32 = jnp.float32
SEQ = ("z", "xl", "y")
CHIPS = ("xh", "z", "xl", "y")


def mm(left, right):
    return lax.dot_general(left, right, (((1,), (0,)), ((), ())), preferred_element_type=F32)


def mm_tn(left, right):
    return lax.dot_general(left, right, (((0,), (0,)), ((), ())), preferred_element_type=F32)


def swap(pairs_ref):
    rows = lax.broadcasted_iota(jnp.int32, (C, C), 0)
    return (rows == pairs_ref[...]).astype(F32).astype(BF)


def scale_of(wide):
    return lax.rsqrt(jnp.mean(wide * wide, axis=-1, keepdims=True) + EPS)


def lay(dst, top, mid, bot):
    start = 0
    for piece in (top, mid, bot):
        rows = piece.shape[0]
        dst[start : start + rows, :] = piece.astype(dst.dtype)
        start += rows


def shift(pad, dil, start, before, after):
    rows = before.shape[0]
    base = pl.multiple_of(start + PAD, 8)

    @pl.when(dil >= 8)
    def _():
        for sign, ref in ((-1, before), (1, after)):
            ref[...] = pad[pl.ds(pl.multiple_of(base + sign * dil, 8), rows), :].astype(BF)

    for small in (1, 2, 4):

        @pl.when(dil == small)
        def _():
            window = pad[pl.ds(pl.multiple_of(base - 8, 8), rows + 16), :]
            before[...] = window[8 - small : 8 - small + rows].astype(BF)
            after[...] = window[8 + small : 8 + small + rows].astype(BF)


def centre(pad, start, rows):
    return pad[pl.ds(pl.multiple_of(start + PAD, 8), rows), :].astype(BF)


def conv(first, last, mid, weight):
    rows = mid.shape[0]
    rows_a = jnp.concatenate([first[:, :B], mid[:, :B], last[:, :B]], axis=1)
    rows_b = jnp.concatenate([last[:, B:], mid[:, B:], first[:, B:]], axis=1)
    both = mm(jnp.concatenate([rows_a, rows_b], axis=0), weight)
    return jnp.concatenate([both[:rows], both[rows:]], axis=1)


def inside(block, start, values):
    rows = lax.broadcasted_iota(jnp.int32, (values.shape[0], 1), 0) + (block * ROWS + start)
    return jnp.where((rows >= 0) & (rows < BLOCKS * ROWS), values, 0.0)


def gelu_both(pre):
    sq = pre * pre
    t = jnp.tanh(ROOT * (pre + CUBE * (pre * sq)))
    half = 0.5 + 0.5 * t
    slope = half + (0.5 * pre) * ((1.0 - t * t) * (ROOT + (3.0 * CUBE * ROOT) * sq))
    return pre * half, slope


def k_enter(pairs, down, up, kern, x, dcat, dcat_t, upcat, upcat_t, kern_t, normed, inner):
    @pl.when(pl.program_id(0) == 0)
    def _():
        s = swap(pairs)
        for layer in range(2):
            other = mm(s, down[layer])
            dcat[layer, :, :B] = down[layer]
            dcat[layer, :, B:] = other.astype(BF)
            dcat_t[layer, :B, :] = down[layer].astype(F32).T.astype(BF)
            dcat_t[layer, B:, :] = other.T.astype(BF)
            other = mm(up[layer], s)
            upcat[layer, :B, :] = up[layer]
            upcat[layer, B:, :] = other.astype(BF)
            upcat_t[layer, :, :B] = up[layer].astype(F32).T.astype(BF)
            upcat_t[layer, :, B:] = other.T.astype(BF)
            for k in range(3):
                kern_t[layer, k] = kern[layer, k].astype(F32).T.astype(BF)

    wide = x[...].astype(F32)
    n = (wide * scale_of(wide)).astype(BF)
    normed[...] = n
    inner[...] = mm(n, dcat[0]).astype(BF)


def k_middle(dil, block, mid, x, top, bot, dcat0, weight, upcat, dcat,
             act, slope, tm, tc, tp, stream, normed, inner, pad, field):
    start = pl.program_id(0) * MID_TILE

    @pl.when(pl.program_id(0) == 0)
    def _():
        lay(field, top[PAD : 4 * PAD, :], x[...], bot[: 3 * PAD, :])
        ends = []
        for halo in (top, bot):
            wide = halo[: 4 * PAD, :].astype(F32)
            ends.append(mm((wide * scale_of(wide)).astype(BF), dcat0[...]).astype(BF))
        lay(pad, ends[0], mid[...], ends[1])

    shift(pad, dil[0], start, tm, tp)
    m = centre(pad, start, MID_TILE)
    tc[...] = m
    g, s = gelu_both(conv(tm[...], tp[...], m, weight[...].reshape(3 * B, B)))
    g = g.astype(BF)
    act[...] = g
    slope[...] = s.astype(BF)
    rows = pl.ds(pl.multiple_of(start, 16), MID_TILE)
    out = (field[rows, :].astype(F32) + mm(g, upcat[...])).astype(BF)
    stream[...] = out
    wide = out.astype(F32)
    n = (wide * scale_of(wide)).astype(BF)
    normed[...] = n
    inner[...] = inside(block[0], start - 3 * PAD, mm(n, dcat[...])).astype(BF)


def k_top(dil, mid, cot, top, bot, weight, upcat_t, act, d_pre, tm, tc, tp, pad, grad):
    start = pl.program_id(0) * TOP_TILE

    @pl.when(pl.program_id(0) == 0)
    def _():
        pad[...] = mid[...].astype(F32)
        lay(grad, top[4 * PAD :, :], cot[...], bot[4 * PAD :, :])

    shift(pad, dil[1], start, tm, tp)
    m = centre(pad, start, TOP_TILE)
    tc[...] = m
    rows = pl.ds(pl.multiple_of(start, 16), TOP_TILE)
    d_act = mm(grad[rows, :], upcat_t[...])
    g, s = gelu_both(conv(tm[...], tp[...], m, weight[...].reshape(3 * B, B)))
    act[...] = g.astype(BF)
    d_pre[...] = (d_act * s).astype(BF)


def put(ref, start, value):
    rows, cols = value.shape
    for i in range(cols // LANES):
        ref[start + i * rows : start + (i + 1) * rows, :] = value[:, i * LANES : (i + 1) * LANES].astype(BF)


def take(ref, start, rows, cols):
    pieces = [ref[start + i * rows : start + (i + 1) * rows, :] for i in range(cols // LANES)]
    return jnp.concatenate(pieces, axis=1).astype(F32)


def own(ref, before):
    return ref[before : before + ROWS, :]


def weight_sums(factor, pairs, act, cot, taps, d_pre, rest):
    up = mm_tn(act, cot) * factor
    put(rest, 0, up[:B] + mm(up[B:].astype(BF), swap(pairs)))
    rows_a = jnp.concatenate([tap[:, :B] for tap in taps], axis=1)
    rows_b = jnp.concatenate([tap[:, B:] for tap in taps[::-1]], axis=1)
    total = (mm_tn(d_pre[:, :B], rows_a) + mm_tn(d_pre[:, B:], rows_b)) * factor
    for k in range(3):
        put(rest, UP + k * 3 * B, total[:, k * B : (k + 1) * B].T)
    rest[REST - LANES :, :] = jnp.zeros((LANES, LANES), BF)


def sort_out(core, lower, upper, send, keep):
    @pl.when(core[0] == 0)
    def _():
        send[...] = upper[...]
        keep[...] = lower[...]

    @pl.when(core[0] != 0)
    def _():
        send[...] = lower[...]
        keep[...] = upper[...]


def k_sums_out(factor, pairs, act, cot, tm, tc, tp, d_pre, stream, upcat, rest, out):
    a = own(act, 2 * PAD)
    out[...] = (own(stream, 3 * PAD).astype(F32) + mm(a, upcat[...])).astype(BF)
    taps = [own(ref, 2 * PAD) for ref in (tm, tc, tp)]
    weight_sums(factor, pairs, a, cot[...], taps, own(d_pre, 2 * PAD), rest)


def k_sums(factor, core, pairs, act, cot, tm, tc, tp, d_pre, upper, send, keep, rest):
    taps = [own(ref, 3 * PAD) for ref in (tm, tc, tp)]
    weight_sums(factor, pairs, own(act, 3 * PAD), own(cot, PAD), taps, own(d_pre, PAD), rest)
    sort_out(core, rest, upper, send, keep)


def down_sum(factor, pairs, normed, d_inner, down):
    total = mm_tn(normed, d_inner) * factor
    put(down, 0, total[:, :B] + mm(swap(pairs), total[:, B:].astype(BF)))


def k_join(keep_a, got_a, keep_b, got_b, out):
    out[:REST, :] = (keep_a[...].astype(F32) + got_a[...].astype(F32)).astype(BF)
    out[REST:, :] = (keep_b[...].astype(F32) + got_b[...].astype(F32)).astype(BF)


def k_share(parts, out):
    share = jnp.sum(parts[...].astype(F32), axis=0).astype(BF)
    out[...] = jnp.broadcast_to(share[None], out.shape)


def k_finish(core, own, other, down, kern, up):
    layer = pl.program_id(0)
    for mine, ref in ((True, own), (False, other)):

        @pl.when((core[0] == layer) == mine)
        def _():
            up[0] = take(ref, 0, B, C)
            for k in range(3):
                kern[0, k] = take(ref, UP + k * 3 * B, B, B)
            down[0] = take(ref, REST, C, B)


def norm_back(v, d_norm):
    wide = v.astype(F32)
    scale = scale_of(wide)
    mixed = jnp.mean(d_norm * wide, axis=-1, keepdims=True)
    return scale * d_norm - wide * (scale * scale * scale * mixed)


def k_back(factor, dil, block, pairs, mid, weight, normed, stream, cot, top, bot, dcat_t, upcat_t, slope,
           grad, d_pre, down, pad, before, after, d_inner, given):
    start = pl.program_id(0) * BACK_TILE

    @pl.when(pl.program_id(0) == 0)
    def _():
        pad[...] = mid[...].astype(F32)
        lay(given, top[5 * PAD :, :], cot[...], bot[4 * PAD : 5 * PAD, :])

    shift(pad, dil[1], start, before, after)
    di = conv(after[...], before[...], centre(pad, start, BACK_TILE), weight[...].reshape(3 * B, B)).astype(BF)
    rows = pl.ds(pl.multiple_of(start, 16), BACK_TILE)
    saved = pl.ds(pl.multiple_of(start + 2 * PAD, 16), BACK_TILE)
    d_inner[rows, :] = di
    g = given[rows, :].astype(F32) + norm_back(stream[saved, :], mm(di, dcat_t[...]))
    g = inside(block[0], start - PAD, g).astype(BF)
    grad[...] = g
    d_pre[...] = (mm(g, upcat_t[...]) * slope[saved, :].astype(F32)).astype(BF)

    @pl.when(pl.program_id(0) == pl.num_programs(0) - 1)
    def _():
        down_sum(factor, pairs, own(normed, 3 * PAD), own(d_inner, PAD), down)


def k_last(factor, core, dil, pairs, mid, weight, normed, upper, send, keep, d_inner, pad, before, after, down):
    start = pl.program_id(0) * TILE

    @pl.when(pl.program_id(0) == 0)
    def _():
        pad[...] = mid[...].astype(F32)

    shift(pad, dil[0], start, before, after)
    di = conv(after[...], before[...], centre(pad, start, TILE), weight[...].reshape(3 * B, B)).astype(BF)
    d_inner[pl.ds(pl.multiple_of(start, 16), TILE), :] = di

    @pl.when(pl.program_id(0) == pl.num_programs(0) - 1)
    def _():
        down_sum(factor, pairs, normed[...], d_inner[...], down)
        sort_out(core, down, upper, send, keep)


def k_input(d_inner, x, cot, dcat_t, out):
    rows = pl.ds(pl.multiple_of(pl.program_id(0) * TILE + PAD, 16), TILE)
    out[...] = (cot[rows, :].astype(F32) + norm_back(x[...], mm(d_inner[...], dcat_t[...]))).astype(BF)


def tile(rows=TILE):
    return pl.BlockSpec((rows, C), lambda i: (i, 0))


def whole(*shape):
    return pl.BlockSpec(shape, lambda i: (0,) * len(shape))


def scalar():
    return pl.BlockSpec(memory_space=pltpu.SMEM)


def shape(*dims, kind=BF):
    return jax.ShapeDtypeStruct(dims, kind)


def call(body, steps, ins, outs, scratch, flops, name):
    size = lambda s: 2 * math.prod(s.shape)
    return pl.pallas_call(
        body,
        grid=(steps,),
        in_specs=ins,
        out_specs=[spec for spec, _ in outs],
        out_shape=[form for _, form in outs],
        scratch_shapes=scratch,
        compiler_params=pltpu.CompilerParams(vmem_limit_bytes=48 * 1024 * 1024),
        cost_estimate=pl.CostEstimate(
            flops=int(flops), bytes_accessed=2 * sum(size(f) for _, f in outs), transcendentals=0
        ),
        name=name,
    )


LANES = 128
UP = 6 * B
REST = UP + 9 * B + LANES
DOWN = 6 * B
UNIT = 2 * ROWS * C * C
FULL = (tile(), shape(ROWS, C))


def store(rows, kind=BF):
    return pltpu.VMEM((rows, C), kind)


def edges(x, cot):
    last = jnp.concatenate([x[ROWS - 4 * PAD :], cot[ROWS - 2 * PAD :]], axis=0)
    first = jnp.concatenate([x[: 4 * PAD], cot[: 2 * PAD]], axis=0)
    top = lax.ppermute(last, SEQ, [(i, i + 1) for i in range(BLOCKS - 1)])
    bot = lax.ppermute(first, SEQ, [(i + 1, i) for i in range(BLOCKS - 1)])
    return top, bot


SWAP = [(0, 1), (1, 0)]
SHARES = (64, (REST + DOWN) // 64, LANES)


def exchange(parts):
    return lax.all_to_all(parts, CHIPS, 0, 0, tiled=True)


def other_core(cells):
    return lax.ppermute(cells, "core", SWAP)


def local(features, cotangent, strand_pairs, dilations, down_weight, conv_weight, up_weight):
    x = features[0]
    cot = cotangent[0]
    pairs = strand_pairs.reshape(1, C)
    factor = 1.0 / math.sqrt(131072.0)
    block = lax.axis_index(SEQ).reshape(1)
    resident = whole(ROWS, C)
    taps_w = [pl.BlockSpec((None, 3, B, B), lambda i, n=n: (n, 0, 0, 0)) for n in range(2)]
    square_of = [pl.BlockSpec((None, C, C), lambda i, n=n: (n, 0, 0)) for n in range(2)]
    halo = whole(6 * PAD, C)

    top, bot = edges(x, cot)
    squares = (whole(2, C, C), shape(2, C, C))
    dcat, dcat_t, upcat, upcat_t, kern_t, normed0, inner0 = call(
        k_enter, STEPS, [whole(1, C), whole(2, C, B), whole(2, B, C), whole(2, 3, B, B), tile()],
        [squares] * 4 + [(whole(2, 3, B, B), shape(2, 3, B, B)), FULL, FULL], [], 3 * UNIT, "enter",
    )(pairs, down_weight, up_weight, conv_weight, x)
    mid = (tile(MID_TILE), shape(MID_ROWS, C))
    act0, slope0, tm0, tc0, tp0, stream1, normed1, inner1 = call(
        k_middle, 4,
        [scalar(), scalar(), resident, resident, halo, halo, square_of[0], taps_w[0], square_of[0], square_of[1]],
        [mid] * 8, [store(ROWS + 8 * PAD, F32), store(MID_ROWS)], 6 * UNIT, "middle",
    )(dilations, block, inner0, x, top, bot, dcat, conv_weight, upcat, dcat)
    upper = (tile(TOP_TILE), shape(TOP_ROWS, C))
    act1, d_pre1, tm1, tc1, tp1 = call(
        k_top, 4, [scalar(), whole(MID_ROWS, C), resident, halo, halo, taps_w[1], square_of[1]],
        [upper] * 5, [store(MID_ROWS, F32), store(TOP_ROWS)], 3 * UNIT, "top",
    )(dilations, inner1, cot, top, bot, conv_weight, upcat_t)
    core = lax.axis_index("core").reshape(1)
    sums = (whole(REST, LANES), shape(REST, LANES))
    downs = (whole(DOWN, LANES), shape(DOWN, LANES))
    joined = (whole(REST + DOWN, LANES), shape(REST + DOWN, LANES))
    shares = (whole(*SHARES), shape(*SHARES))
    wide_top, wide_mid, wide_back = whole(TOP_ROWS, C), whole(MID_ROWS, C), whole(BACK_ROWS, C)
    rest1, out = call(
        functools.partial(k_sums_out, factor), 1,
        [whole(1, C), wide_top, resident] + [wide_top] * 4 + [wide_mid, square_of[1]],
        [sums, (resident, shape(ROWS, C))], [], 4 * UNIT, "sums_out",
    )(pairs, act1, cot, tm1, tc1, tp1, d_pre1, stream1, upcat)
    back = (tile(BACK_TILE), shape(BACK_ROWS, C))
    grad, d_pre0, down1 = call(
        functools.partial(k_back, factor), 3,
        [scalar(), scalar(), whole(1, C), wide_top, taps_w[1], wide_mid, wide_mid, resident, halo, halo,
         square_of[1], square_of[0], wide_mid],
        [back, back, downs],
        [store(TOP_ROWS, F32), store(BACK_TILE), store(BACK_TILE), store(BACK_ROWS), store(BACK_ROWS)],
        5 * UNIT, "back",
    )(dilations, block, pairs, d_pre1, kern_t, normed1, stream1, cot, top, bot, dcat_t, upcat_t, slope0)
    send_a, keep_a = call(
        functools.partial(k_sums, factor), 1,
        [scalar(), whole(1, C), wide_mid, wide_back, wide_mid, wide_mid, wide_mid, wide_back, sums[0]],
        [sums, sums], [pltpu.VMEM((REST, LANES), BF)], 3 * UNIT, "sums",
    )(core, pairs, act0, grad, tm0, tc0, tp0, d_pre0, rest1)
    send_b, keep_b, d_inner0 = call(
        functools.partial(k_last, factor), STEPS,
        [scalar(), scalar(), whole(1, C), wide_back, taps_w[0], resident, downs[0]],
        [downs, downs, (resident, shape(ROWS, C))],
        [store(BACK_ROWS, F32), store(TILE), store(TILE), pltpu.VMEM((DOWN, LANES), BF)],
        3 * UNIT, "last",
    )(core, dilations, pairs, d_pre0, kern_t, normed0, down1)
    (parts,) = call(
        k_join, 1, [sums[0], sums[0], downs[0], downs[0]], [joined], [], 0, "join",
    )(keep_a, other_core(send_a), keep_b, other_core(send_b))
    parts = exchange(parts.reshape(SHARES))
    (shared,) = call(k_share, 1, [shares[0]], [shares], [], 0, "share")(parts)
    (input_grad,) = call(
        k_input, STEPS, [tile(), tile(), wide_back, square_of[0]], [FULL], [], UNIT, "input",
    )(d_inner0, x, grad, dcat_t)
    own = exchange(shared).reshape(REST + DOWN, LANES)
    layered = lambda *dims: (
        pl.BlockSpec((1,) + dims, lambda i: (i,) + (0,) * len(dims)), shape(2, *dims, kind=F32)
    )
    grads = call(
        k_finish, 2, [scalar()] + [joined[0]] * 2,
        [layered(C, B), layered(3, B, B), layered(B, C)], [], 0, "finish",
    )(core, own, other_core(own))
    return (out[None], input_grad[None], *grads)


def solution(mesh):
    fine = Mesh(mesh.devices.reshape(2, 2, 4, 2, 4), ("xh", "core", "z", "xl", "y"))
    rows = P(("xh", "core"), SEQ, None)
    in_specs = (rows, rows, P(), P(), P(), P(), P())
    out_specs = (rows, rows, P(), P(), P())
    return jax.shard_map(local, mesh=fine, in_specs=in_specs, out_specs=out_specs, check_vma=False)
```

```python
import functools
import math

import jax
import jax.numpy as jnp
from jax import lax
from jax.experimental import pallas as pl
from jax.experimental.pallas import tpu as pltpu
from jax.sharding import Mesh, PartitionSpec as P

C = 768
B = 384
PAD = 64
ROWS = 1024
TILE = 256
STEPS = ROWS // TILE
BLOCKS = 32
MID_ROWS, TOP_ROWS, BACK_ROWS = ROWS + 6 * PAD, ROWS + 4 * PAD, ROWS + 2 * PAD
MID_TILE, TOP_TILE, BACK_TILE = MID_ROWS // 4, TOP_ROWS // 4, BACK_ROWS // 3
EPS = 1e-06
ROOT = math.sqrt(2.0 / math.pi)
CUBE = 0.044715
BF = jnp.bfloat16
F32 = jnp.float32
SEQ = ("z", "xl", "y")
CHIPS = ("xh", "z", "xl", "y")


def mm(left, right):
    return lax.dot_general(left, right, (((1,), (0,)), ((), ())), preferred_element_type=F32)


def mm_tn(left, right):
    return lax.dot_general(left, right, (((0,), (0,)), ((), ())), preferred_element_type=F32)


def swap(pairs_ref):
    rows = lax.broadcasted_iota(jnp.int32, (C, C), 0)
    return (rows == pairs_ref[...]).astype(F32).astype(BF)


def scale_of(wide):
    return lax.rsqrt(jnp.mean(wide * wide, axis=-1, keepdims=True) + EPS)


def lay(dst, top, mid, bot):
    start = 0
    for piece in (top, mid, bot):
        rows = piece.shape[0]
        dst[start : start + rows, :] = piece.astype(dst.dtype)
        start += rows


def shift(cells, dil, start, before, after):
    rows = before.shape[0]
    base = pl.multiple_of(start + PAD, 16)

    @pl.when(dil >= 16)
    def _():
        for sign, ref in ((-1, before), (1, after)):
            ref[...] = cells[pl.ds(pl.multiple_of(base + sign * dil, 16), rows), :]

    for small in (1, 2, 4, 8):

        @pl.when(dil == small)
        def _():
            window = cells[pl.ds(pl.multiple_of(base - 16, 16), rows + 32), :].astype(F32)
            before[...] = window[16 - small : 16 - small + rows].astype(BF)
            after[...] = window[16 + small : 16 + small + rows].astype(BF)


def centre(cells, start, rows):
    return cells[pl.ds(pl.multiple_of(start + PAD, 16), rows), :]


def conv(first, last, mid, weight):
    rows = mid.shape[0]
    rows_a = jnp.concatenate([first[:, :B], mid[:, :B], last[:, :B]], axis=1)
    rows_b = jnp.concatenate([last[:, B:], mid[:, B:], first[:, B:]], axis=1)
    both = mm(jnp.concatenate([rows_a, rows_b], axis=0), weight)
    return jnp.concatenate([both[:rows], both[rows:]], axis=1)


def inside(block, start, values):
    rows = lax.broadcasted_iota(jnp.int32, (values.shape[0], 1), 0) + (block * ROWS + start)
    return jnp.where((rows >= 0) & (rows < BLOCKS * ROWS), values, 0.0)


def gelu_both(pre):
    sq = pre * pre
    t = jnp.tanh(pre * (ROOT + (ROOT * CUBE) * sq))
    half = 0.5 + 0.5 * t
    act = pre * half
    return act, half + (act * (1.0 - t)) * (ROOT + (3.0 * CUBE * ROOT) * sq)


def k_enter(pairs, down, up, kern, x, dcat, dcat_t, upcat, upcat_t, kern_t, normed, inner):
    @pl.when(pl.program_id(0) == 0)
    def _():
        s = swap(pairs)
        for layer in range(2):
            other = mm(s, down[layer])
            dcat[layer, :, :B] = down[layer]
            dcat[layer, :, B:] = other.astype(BF)
            dcat_t[layer, :B, :] = down[layer].astype(F32).T.astype(BF)
            dcat_t[layer, B:, :] = other.T.astype(BF)
            other = mm(up[layer], s)
            upcat[layer, :B, :] = up[layer]
            upcat[layer, B:, :] = other.astype(BF)
            upcat_t[layer, :, :B] = up[layer].astype(F32).T.astype(BF)
            upcat_t[layer, :, B:] = other.T.astype(BF)
            for k in range(3):
                kern_t[layer, k] = kern[layer, k].astype(F32).T.astype(BF)

    wide = x[...].astype(F32)
    n = (wide * scale_of(wide)).astype(BF)
    normed[...] = n
    inner[...] = mm(n, dcat[0]).astype(BF)


def k_middle(dil, block, mid, x, top, bot, dcat0, weight, upcat, dcat,
             act, slope, tm, tp, stream, normed, inner, pad, field):
    start = pl.program_id(0) * MID_TILE

    @pl.when(pl.program_id(0) == 0)
    def _():
        lay(field, top[PAD : 4 * PAD, :], x[...], bot[: 3 * PAD, :])
        ends = []
        for halo in (top, bot):
            wide = halo[: 4 * PAD, :].astype(F32)
            ends.append(mm((wide * scale_of(wide)).astype(BF), dcat0[...]).astype(BF))
        lay(pad, ends[0], mid[...], ends[1])

    shift(pad, dil[0], start, tm, tp)
    m = centre(pad, start, MID_TILE)
    g, s = gelu_both(conv(tm[...], tp[...], m, weight[...].reshape(3 * B, B)))
    g = g.astype(BF)
    act[...] = g
    slope[...] = s.astype(BF)
    rows = pl.ds(pl.multiple_of(start, 16), MID_TILE)
    out = (field[rows, :].astype(F32) + mm(g, upcat[...])).astype(BF)
    stream[...] = out
    wide = out.astype(F32)
    n = (wide * scale_of(wide)).astype(BF)
    normed[...] = n
    inner[...] = inside(block[0], start - 3 * PAD, mm(n, dcat[...])).astype(BF)


def k_top(dil, mid, cot, top, bot, weight, upcat_t, act, d_pre, tm, tp, grad):
    start = pl.program_id(0) * TOP_TILE

    @pl.when(pl.program_id(0) == 0)
    def _():
        lay(grad, top[4 * PAD :, :], cot[...], bot[4 * PAD :, :])

    shift(mid, dil[1], start, tm, tp)
    m = centre(mid, start, TOP_TILE)
    rows = pl.ds(pl.multiple_of(start, 16), TOP_TILE)
    d_act = mm(grad[rows, :], upcat_t[...])
    g, s = gelu_both(conv(tm[...], tp[...], m, weight[...].reshape(3 * B, B)))
    act[...] = g.astype(BF)
    d_pre[...] = (d_act * s).astype(BF)


def put(ref, start, value):
    rows, cols = value.shape
    for i in range(cols // LANES):
        ref[start + i * rows : start + (i + 1) * rows, :] = value[:, i * LANES : (i + 1) * LANES].astype(BF)


def take(ref, start, rows, cols):
    pieces = [ref[start + i * rows : start + (i + 1) * rows, :] for i in range(cols // LANES)]
    return jnp.concatenate(pieces, axis=1).astype(F32)


def own(ref, before):
    return ref[before : before + ROWS, :]


def weight_sums(factor, pairs, act, cot, taps, d_pre, rest):
    up = mm_tn(act, cot) * factor
    put(rest, 0, up[:B] + mm(up[B:].astype(BF), swap(pairs)))
    rows_a = jnp.concatenate([tap[:, :B] for tap in taps], axis=1)
    rows_b = jnp.concatenate([tap[:, B:] for tap in taps[::-1]], axis=1)
    total = (mm_tn(d_pre[:, :B], rows_a) + mm_tn(d_pre[:, B:], rows_b)) * factor
    for k in range(3):
        put(rest, UP + k * 3 * B, total[:, k * B : (k + 1) * B].T)
    rest[REST - LANES :, :] = jnp.zeros((LANES, LANES), BF)


def sort_out(core, lower, upper, send, keep):
    @pl.when(core[0] == 0)
    def _():
        send[...] = upper[...]
        keep[...] = lower[...]

    @pl.when(core[0] != 0)
    def _():
        send[...] = lower[...]
        keep[...] = upper[...]


def k_sums_out(factor, pairs, act, cot, tm, tc, tp, d_pre, stream, upcat, rest, out):
    a = own(act, 2 * PAD)
    out[...] = (own(stream, 3 * PAD).astype(F32) + mm(a, upcat[...])).astype(BF)
    taps = [own(tm, 2 * PAD), own(tc, 3 * PAD), own(tp, 2 * PAD)]
    weight_sums(factor, pairs, a, cot[...], taps, own(d_pre, 2 * PAD), rest)


def k_sums(factor, core, pairs, act, cot, tm, tc, tp, d_pre, upper, send, keep, rest):
    taps = [own(tm, 3 * PAD), tc[...], own(tp, 3 * PAD)]
    weight_sums(factor, pairs, own(act, 3 * PAD), own(cot, PAD), taps, own(d_pre, PAD), rest)
    sort_out(core, rest, upper, send, keep)


def down_sum(factor, pairs, normed, d_inner, down):
    total = mm_tn(normed, d_inner) * factor
    put(down, 0, total[:, :B] + mm(swap(pairs), total[:, B:].astype(BF)))


def k_join(keep_a, got_a, keep_b, got_b, out):
    out[:REST, :] = (keep_a[...].astype(F32) + got_a[...].astype(F32)).astype(BF)
    out[REST:, :] = (keep_b[...].astype(F32) + got_b[...].astype(F32)).astype(BF)


def k_share(parts, out):
    share = jnp.sum(parts[...].astype(F32), axis=0).astype(BF)
    out[...] = jnp.broadcast_to(share[None], out.shape)


def k_finish(core, own, other, down, kern, up):
    layer = pl.program_id(0)
    for mine, ref in ((True, own), (False, other)):

        @pl.when((core[0] == layer) == mine)
        def _():
            up[0] = take(ref, 0, B, C)
            for k in range(3):
                kern[0, k] = take(ref, UP + k * 3 * B, B, B)
            down[0] = take(ref, REST, C, B)


def norm_back(v, d_norm):
    wide = v.astype(F32)
    scale = scale_of(wide)
    mixed = jnp.mean(d_norm * wide, axis=-1, keepdims=True)
    return scale * d_norm - wide * (scale * scale * scale * mixed)


def k_back(factor, dil, block, pairs, mid, weight, normed, stream, cot, top, bot, dcat_t, upcat_t, slope,
           grad, d_pre, down, before, after, d_inner, given):
    start = pl.program_id(0) * BACK_TILE

    @pl.when(pl.program_id(0) == 0)
    def _():
        lay(given, top[5 * PAD :, :], cot[...], bot[4 * PAD : 5 * PAD, :])

    shift(mid, dil[1], start, before, after)
    di = conv(after[...], before[...], centre(mid, start, BACK_TILE), weight[...].reshape(3 * B, B)).astype(BF)
    rows = pl.ds(pl.multiple_of(start, 16), BACK_TILE)
    saved = pl.ds(pl.multiple_of(start + 2 * PAD, 16), BACK_TILE)
    d_inner[rows, :] = di
    g = given[rows, :].astype(F32) + norm_back(stream[saved, :], mm(di, dcat_t[...]))
    g = inside(block[0], start - PAD, g).astype(BF)
    grad[...] = g
    d_pre[...] = (mm(g, upcat_t[...]) * slope[saved, :].astype(F32)).astype(BF)

    @pl.when(pl.program_id(0) == pl.num_programs(0) - 1)
    def _():
        down_sum(factor, pairs, own(normed, 3 * PAD), own(d_inner, PAD), down)


def k_last(factor, core, dil, pairs, mid, weight, normed, upper, send, keep, d_inner, before, after, down):
    start = pl.program_id(0) * TILE

    shift(mid, dil[0], start, before, after)
    di = conv(after[...], before[...], centre(mid, start, TILE), weight[...].reshape(3 * B, B)).astype(BF)
    d_inner[pl.ds(pl.multiple_of(start, 16), TILE), :] = di

    @pl.when(pl.program_id(0) == pl.num_programs(0) - 1)
    def _():
        down_sum(factor, pairs, normed[...], d_inner[...], down)
        sort_out(core, down, upper, send, keep)


def k_input(d_inner, x, cot, dcat_t, out):
    rows = pl.ds(pl.multiple_of(pl.program_id(0) * TILE + PAD, 16), TILE)
    out[...] = (cot[rows, :].astype(F32) + norm_back(x[...], mm(d_inner[...], dcat_t[...]))).astype(BF)


def tile(rows=TILE):
    return pl.BlockSpec((rows, C), lambda i: (i, 0))


def whole(*shape):
    return pl.BlockSpec(shape, lambda i: (0,) * len(shape), pipeline_mode=pl.Buffered(1))


def scalar():
    return pl.BlockSpec(memory_space=pltpu.SMEM)


def shape(*dims, kind=BF):
    return jax.ShapeDtypeStruct(dims, kind)


def call(body, steps, ins, outs, scratch, flops, name):
    size = lambda s: 2 * math.prod(s.shape)
    return pl.pallas_call(
        body,
        grid=(steps,),
        in_specs=ins,
        out_specs=[spec for spec, _ in outs],
        out_shape=[form for _, form in outs],
        scratch_shapes=scratch,
        compiler_params=pltpu.CompilerParams(vmem_limit_bytes=20 * 1024 * 1024),
        cost_estimate=pl.CostEstimate(
            flops=int(flops), bytes_accessed=2 * sum(size(f) for _, f in outs), transcendentals=0
        ),
        name=name,
    )


LANES = 128
UP = 6 * B
REST = UP + 9 * B + LANES
DOWN = 6 * B
UNIT = 2 * ROWS * C * C
FULL = (tile(), shape(ROWS, C))


def store(rows, kind=BF):
    return pltpu.VMEM((rows, C), kind)


def edges(x, cot):
    last = jnp.concatenate([x[ROWS - 4 * PAD :], cot[ROWS - 2 * PAD :]], axis=0)
    first = jnp.concatenate([x[: 4 * PAD], cot[: 2 * PAD]], axis=0)
    top = lax.ppermute(last, SEQ, [(i, i + 1) for i in range(BLOCKS - 1)])
    bot = lax.ppermute(first, SEQ, [(i + 1, i) for i in range(BLOCKS - 1)])
    return top, bot


SWAP = [(0, 1), (1, 0)]
SHARES = (64, (REST + DOWN) // 64, LANES)


def exchange(parts):
    return lax.all_to_all(parts, CHIPS, 0, 0, tiled=True)


def other_core(cells):
    return lax.ppermute(cells, "core", SWAP)


def local(features, cotangent, strand_pairs, dilations, down_weight, conv_weight, up_weight):
    x = features[0]
    cot = cotangent[0]
    pairs = strand_pairs.reshape(1, C)
    factor = 1.0 / math.sqrt(131072.0)
    block = lax.axis_index(SEQ).reshape(1)
    resident = whole(ROWS, C)
    taps_w = [pl.BlockSpec((None, 3, B, B), lambda i, n=n: (n, 0, 0, 0), pipeline_mode=pl.Buffered(1)) for n in range(2)]
    square_of = [pl.BlockSpec((None, C, C), lambda i, n=n: (n, 0, 0), pipeline_mode=pl.Buffered(1)) for n in range(2)]
    halo = whole(6 * PAD, C)

    top, bot = edges(x, cot)
    squares = (whole(2, C, C), shape(2, C, C))
    dcat, dcat_t, upcat, upcat_t, kern_t, normed0, inner0 = call(
        k_enter, STEPS, [whole(1, C), whole(2, C, B), whole(2, B, C), whole(2, 3, B, B), tile()],
        [squares] * 4 + [(whole(2, 3, B, B), shape(2, 3, B, B)), FULL, FULL], [], 3 * UNIT, "enter",
    )(pairs, down_weight, up_weight, conv_weight, x)
    mid = (tile(MID_TILE), shape(MID_ROWS, C))
    act0, slope0, tm0, tp0, stream1, normed1, inner1 = call(
        k_middle, 4,
        [scalar(), scalar(), resident, resident, halo, halo, square_of[0], taps_w[0], square_of[0], square_of[1]],
        [mid] * 7, [store(ROWS + 8 * PAD), store(MID_ROWS)], 6 * UNIT, "middle",
    )(dilations, block, inner0, x, top, bot, dcat, conv_weight, upcat, dcat)
    upper = (tile(TOP_TILE), shape(TOP_ROWS, C))
    act1, d_pre1, tm1, tp1 = call(
        k_top, 4, [scalar(), whole(MID_ROWS, C), resident, halo, halo, taps_w[1], square_of[1]],
        [upper] * 4, [store(TOP_ROWS)], 3 * UNIT, "top",
    )(dilations, inner1, cot, top, bot, conv_weight, upcat_t)
    core = lax.axis_index("core").reshape(1)
    sums = (whole(REST, LANES), shape(REST, LANES))
    downs = (whole(DOWN, LANES), shape(DOWN, LANES))
    joined = (whole(REST + DOWN, LANES), shape(REST + DOWN, LANES))
    shares = (whole(*SHARES), shape(*SHARES))
    wide_top, wide_mid, wide_back = whole(TOP_ROWS, C), whole(MID_ROWS, C), whole(BACK_ROWS, C)
    rest1, out = call(
        functools.partial(k_sums_out, factor), 1,
        [whole(1, C), wide_top, resident, wide_top, wide_mid, wide_top, wide_top, wide_mid, square_of[1]],
        [sums, (resident, shape(ROWS, C))], [], 4 * UNIT, "sums_out",
    )(pairs, act1, cot, tm1, inner1, tp1, d_pre1, stream1, upcat)
    back = (tile(BACK_TILE), shape(BACK_ROWS, C))
    grad, d_pre0, down1 = call(
        functools.partial(k_back, factor), 3,
        [scalar(), scalar(), whole(1, C), wide_top, taps_w[1], wide_mid, wide_mid, resident, halo, halo,
         square_of[1], square_of[0], wide_mid],
        [back, back, downs],
        [store(BACK_TILE), store(BACK_TILE), store(BACK_ROWS), store(BACK_ROWS)],
        5 * UNIT, "back",
    )(dilations, block, pairs, d_pre1, kern_t, normed1, stream1, cot, top, bot, dcat_t, upcat_t, slope0)
    send_a, keep_a = call(
        functools.partial(k_sums, factor), 1,
        [scalar(), whole(1, C), wide_mid, wide_back, wide_mid, resident, wide_mid, wide_back, sums[0]],
        [sums, sums], [pltpu.VMEM((REST, LANES), BF)], 3 * UNIT, "sums",
    )(core, pairs, act0, grad, tm0, inner0, tp0, d_pre0, rest1)
    send_b, keep_b, d_inner0 = call(
        functools.partial(k_last, factor), STEPS,
        [scalar(), scalar(), whole(1, C), wide_back, taps_w[0], resident, downs[0]],
        [downs, downs, (resident, shape(ROWS, C))],
        [store(TILE), store(TILE), pltpu.VMEM((DOWN, LANES), BF)],
        3 * UNIT, "last",
    )(core, dilations, pairs, d_pre0, kern_t, normed0, down1)
    (parts,) = call(
        k_join, 1, [sums[0], sums[0], downs[0], downs[0]], [joined], [], 0, "join",
    )(keep_a, other_core(send_a), keep_b, other_core(send_b))
    parts = exchange(parts.reshape(SHARES))
    (shared,) = call(k_share, 1, [shares[0]], [shares], [], 0, "share")(parts)
    (input_grad,) = call(
        k_input, STEPS, [tile(), tile(), wide_back, square_of[0]], [FULL], [], UNIT, "input",
    )(d_inner0, x, grad, dcat_t)
    own = exchange(shared).reshape(REST + DOWN, LANES)
    layered = lambda *dims: (
        pl.BlockSpec((1,) + dims, lambda i: (i,) + (0,) * len(dims)), shape(2, *dims, kind=F32)
    )
    grads = call(
        k_finish, 2, [scalar()] + [joined[0]] * 2,
        [layered(C, B), layered(3, B, B), layered(B, C)], [], 0, "finish",
    )(core, own, other_core(own))
    return (out[None], input_grad[None], *grads)


def solution(mesh):
    fine = Mesh(mesh.devices.reshape(2, 2, 4, 2, 4), ("xh", "core", "z", "xl", "y"))
    rows = P(("xh", "core"), SEQ, None)
    in_specs = (rows, rows, P(), P(), P(), P(), P())
    out_specs = (rows, rows, P(), P(), P())
    return jax.shard_map(local, mesh=fine, in_specs=in_specs, out_specs=out_specs, check_vma=False)
```

```python
import functools
import math

import jax
import jax.numpy as jnp
from jax import lax
from jax.experimental import pallas as pl
from jax.experimental.pallas import tpu as pltpu
from jax.sharding import Mesh, PartitionSpec as P

C = 768
B = 384
PAD = 64
ROWS = 1024
TILE = 256
STEPS = ROWS // TILE
BLOCKS = 32
MID_ROWS, TOP_ROWS, BACK_ROWS = ROWS + 6 * PAD, ROWS + 4 * PAD, ROWS + 2 * PAD
MID_TILE, TOP_TILE, BACK_TILE = MID_ROWS // 4, TOP_ROWS // 4, BACK_ROWS // 3
EPS = 1e-06
ROOT = math.sqrt(2.0 / math.pi)
CUBE = 0.044715
BF = jnp.bfloat16
F32 = jnp.float32
SEQ = ("z", "xl", "y")
CHIPS = ("xh", "z", "xl", "y")


def mm(left, right):
    return lax.dot_general(left, right, (((1,), (0,)), ((), ())), preferred_element_type=F32)


def mm_tn(left, right):
    return lax.dot_general(left, right, (((0,), (0,)), ((), ())), preferred_element_type=F32)


def swap(pairs_ref):
    rows = lax.broadcasted_iota(jnp.int32, (C, C), 0)
    return (rows == pairs_ref[...]).astype(F32).astype(BF)


def scale_of(wide):
    return lax.rsqrt(jnp.mean(wide * wide, axis=-1, keepdims=True) + EPS)


def lay(dst, top, mid, bot):
    start = 0
    for piece in (top, mid, bot):
        rows = piece.shape[0]
        dst[start : start + rows, :] = piece.astype(dst.dtype)
        start += rows


def shift(cells, dil, start, before, after):
    rows = before.shape[0]
    base = pl.multiple_of(start + PAD, 16)

    @pl.when(dil >= 16)
    def _():
        for sign, ref in ((-1, before), (1, after)):
            ref[...] = cells[pl.ds(pl.multiple_of(base + sign * dil, 16), rows), :]

    for small in (1, 2, 4, 8):

        @pl.when(dil == small)
        def _():
            window = cells[pl.ds(pl.multiple_of(base - 16, 16), rows + 32), :].astype(F32)
            before[...] = window[16 - small : 16 - small + rows].astype(BF)
            after[...] = window[16 + small : 16 + small + rows].astype(BF)


def centre(cells, start, rows):
    return cells[pl.ds(pl.multiple_of(start + PAD, 16), rows), :]


def conv(first, last, mid, weight):
    rows = mid.shape[0]
    rows_a = jnp.concatenate([first[:, :B], mid[:, :B], last[:, :B]], axis=1)
    rows_b = jnp.concatenate([last[:, B:], mid[:, B:], first[:, B:]], axis=1)
    both = mm(jnp.concatenate([rows_a, rows_b], axis=0), weight)
    return jnp.concatenate([both[:rows], both[rows:]], axis=1)


def inside(block, start, values):
    rows = lax.broadcasted_iota(jnp.int32, (values.shape[0], 1), 0) + (block * ROWS + start)
    return jnp.where((rows >= 0) & (rows < BLOCKS * ROWS), values, 0.0)


def gelu_both(pre):
    sq = pre * pre
    t = jnp.tanh(pre * (ROOT + (ROOT * CUBE) * sq))
    half = 0.5 + 0.5 * t
    act = pre * half
    return act, half + (act * (1.0 - t)) * (ROOT + (3.0 * CUBE * ROOT) * sq)


def k_enter(pairs, down, up, kern, x, dcat, dcat_t, upcat, upcat_t, kern_t, normed, inner):
    @pl.when(pl.program_id(0) == 0)
    def _():
        s = swap(pairs)
        for layer in range(2):
            other = mm(s, down[layer])
            dcat[layer, :, :B] = down[layer]
            dcat[layer, :, B:] = other.astype(BF)
            dcat_t[layer, :B, :] = down[layer].astype(F32).T.astype(BF)
            dcat_t[layer, B:, :] = other.T.astype(BF)
            other = mm(up[layer], s)
            upcat[layer, :B, :] = up[layer]
            upcat[layer, B:, :] = other.astype(BF)
            upcat_t[layer, :, :B] = up[layer].astype(F32).T.astype(BF)
            upcat_t[layer, :, B:] = other.T.astype(BF)
            for k in range(3):
                kern_t[layer, k] = kern[layer, k].astype(F32).T.astype(BF)

    wide = x[...].astype(F32)
    n = (wide * scale_of(wide)).astype(BF)
    normed[...] = n
    inner[...] = mm(n, dcat[0]).astype(BF)


def k_middle(dil, block, mid, x, top, bot, dcat0, weight, upcat, dcat,
             act, slope, tm, tp, stream, normed, inner, pad, field):
    start = pl.program_id(0) * MID_TILE

    @pl.when(pl.program_id(0) == 0)
    def _():
        lay(field, top[PAD : 4 * PAD, :], x[...], bot[: 3 * PAD, :])
        ends = []
        for halo in (top, bot):
            wide = halo[...].astype(F32)
            ends.append(mm((wide * scale_of(wide)).astype(BF), dcat0[...]).astype(BF))
        lay(pad, ends[0], mid[...], ends[1])

    shift(pad, dil[0], start, tm, tp)
    m = centre(pad, start, MID_TILE)
    g, s = gelu_both(conv(tm[...], tp[...], m, weight[...].reshape(3 * B, B)))
    g = g.astype(BF)
    act[...] = g
    slope[...] = s.astype(BF)
    rows = pl.ds(pl.multiple_of(start, 16), MID_TILE)
    out = (field[rows, :].astype(F32) + mm(g, upcat[...])).astype(BF)
    stream[...] = out
    wide = out.astype(F32)
    n = (wide * scale_of(wide)).astype(BF)
    normed[...] = n
    inner[...] = inside(block[0], start - 3 * PAD, mm(n, dcat[...])).astype(BF)


def k_top(dil, mid, cot, top, bot, weight, upcat_t, act, d_pre, tm, tp, grad):
    start = pl.program_id(0) * TOP_TILE

    @pl.when(pl.program_id(0) == 0)
    def _():
        lay(grad, top[...], cot[...], bot[...])

    shift(mid, dil[1], start, tm, tp)
    m = centre(mid, start, TOP_TILE)
    rows = pl.ds(pl.multiple_of(start, 16), TOP_TILE)
    d_act = mm(grad[rows, :], upcat_t[...])
    g, s = gelu_both(conv(tm[...], tp[...], m, weight[...].reshape(3 * B, B)))
    act[...] = g.astype(BF)
    d_pre[...] = (d_act * s).astype(BF)


def put(ref, start, value):
    rows, cols = value.shape
    for i in range(cols // LANES):
        ref[start + i * rows : start + (i + 1) * rows, :] = value[:, i * LANES : (i + 1) * LANES].astype(BF)


def take(ref, start, rows, cols):
    pieces = [ref[start + i * rows : start + (i + 1) * rows, :] for i in range(cols // LANES)]
    return jnp.concatenate(pieces, axis=1).astype(F32)


def own(ref, before):
    return ref[before : before + ROWS, :]


def weight_sums(factor, pairs, act, cot, taps, d_pre, rest):
    up = mm_tn(act, cot) * factor
    put(rest, 0, up[:B] + mm(up[B:].astype(BF), swap(pairs)))
    rows_a = jnp.concatenate([tap[:, :B] for tap in taps], axis=1)
    rows_b = jnp.concatenate([tap[:, B:] for tap in taps[::-1]], axis=1)
    total = (mm_tn(d_pre[:, :B], rows_a) + mm_tn(d_pre[:, B:], rows_b)) * factor
    for k in range(3):
        put(rest, UP + k * 3 * B, total[:, k * B : (k + 1) * B].T)
    rest[REST - LANES :, :] = jnp.zeros((LANES, LANES), BF)


def sort_out(core, lower, upper, send, keep):
    @pl.when(core[0] == 0)
    def _():
        send[...] = upper[...]
        keep[...] = lower[...]

    @pl.when(core[0] != 0)
    def _():
        send[...] = lower[...]
        keep[...] = upper[...]


def k_sums_top(factor, pairs, act, cot, tm, tc, tp, d_pre, rest):
    taps = [own(tm, 2 * PAD), own(tc, 3 * PAD), own(tp, 2 * PAD)]
    weight_sums(factor, pairs, own(act, 2 * PAD), cot[...], taps, own(d_pre, 2 * PAD), rest)


def k_sums(factor, core, pairs, act, cot, tm, tc, tp, d_pre, upper, send, keep, rest):
    taps = [own(tm, 3 * PAD), tc[...], own(tp, 3 * PAD)]
    weight_sums(factor, pairs, own(act, 3 * PAD), own(cot, PAD), taps, own(d_pre, PAD), rest)
    sort_out(core, rest, upper, send, keep)


def down_sum(factor, pairs, normed, d_inner, down):
    total = mm_tn(normed, d_inner) * factor
    put(down, 0, total[:, :B] + mm(swap(pairs), total[:, B:].astype(BF)))


def k_join(keep_a, got_a, keep_b, got_b, out):
    out[:REST, :] = (keep_a[...].astype(F32) + got_a[...].astype(F32)).astype(BF)
    out[REST:, :] = (keep_b[...].astype(F32) + got_b[...].astype(F32)).astype(BF)


def k_share(parts, out):
    share = jnp.sum(parts[...].astype(F32), axis=0).astype(BF)
    out[...] = jnp.broadcast_to(share[None], out.shape)


def k_finish(layer, ref, *rest):
    down, kern, up = rest[-3:]
    up[0] = take(ref, 0, B, C)
    for k in range(3):
        kern[0, k] = take(ref, UP + k * 3 * B, B, B)
    down[0] = take(ref, REST, C, B)


def write_layer(layer, total, outs):
    dims = ((C, B), (3, B, B), (B, C))
    blocks = [pl.BlockSpec((1,) + d, lambda i, n, d=d: (n[0],) + (0,) * len(d)) for d in dims]
    return pl.pallas_call(
        k_finish,
        grid_spec=pltpu.PrefetchScalarGridSpec(
            num_scalar_prefetch=1,
            grid=(1,),
            in_specs=[pl.BlockSpec(total.shape, lambda i, n: (0, 0))] + [pl.BlockSpec(memory_space=pl.ANY)] * len(outs),
            out_specs=blocks,
        ),
        out_shape=[shape(2, *d, kind=F32) for d in dims],
        input_output_aliases={2 + i: i for i in range(len(outs))},
        compiler_params=pltpu.CompilerParams(vmem_limit_bytes=20 * 1024 * 1024),
        name="finish",
    )(layer, total, *outs)


def norm_back(v, d_norm):
    wide = v.astype(F32)
    scale = scale_of(wide)
    mixed = jnp.mean(d_norm * wide, axis=-1, keepdims=True)
    return scale * d_norm - wide * (scale * scale * scale * mixed)


def k_back(factor, dil, block, pairs, mid, weight, normed, stream, cot, top, bot, dcat_t, upcat_t, slope,
           grad, d_pre, down, before, after, d_inner, given):
    start = pl.program_id(0) * BACK_TILE

    @pl.when(pl.program_id(0) == 0)
    def _():
        lay(given, top[PAD:, :], cot[...], bot[:PAD, :])

    shift(mid, dil[1], start, before, after)
    di = conv(after[...], before[...], centre(mid, start, BACK_TILE), weight[...].reshape(3 * B, B)).astype(BF)
    rows = pl.ds(pl.multiple_of(start, 16), BACK_TILE)
    saved = pl.ds(pl.multiple_of(start + 2 * PAD, 16), BACK_TILE)
    d_inner[rows, :] = di
    g = given[rows, :].astype(F32) + norm_back(stream[saved, :], mm(di, dcat_t[...]))
    g = inside(block[0], start - PAD, g).astype(BF)
    grad[...] = g
    d_pre[...] = (mm(g, upcat_t[...]) * slope[saved, :].astype(F32)).astype(BF)

    @pl.when(pl.program_id(0) == pl.num_programs(0) - 1)
    def _():
        down_sum(factor, pairs, own(normed, 3 * PAD), own(d_inner, PAD), down)


def k_last(factor, core, dil, pairs, mid, weight, normed, upper, send, keep, d_inner, before, after, down):
    start = pl.program_id(0) * TILE

    shift(mid, dil[0], start, before, after)
    di = conv(after[...], before[...], centre(mid, start, TILE), weight[...].reshape(3 * B, B)).astype(BF)
    d_inner[pl.ds(pl.multiple_of(start, 16), TILE), :] = di

    @pl.when(pl.program_id(0) == pl.num_programs(0) - 1)
    def _():
        down_sum(factor, pairs, normed[...], d_inner[...], down)
        sort_out(core, down, upper, send, keep)


def k_out(act, stream, upcat, out):
    step = pl.program_id(0) * TILE
    rows = pl.ds(pl.multiple_of(step + 2 * PAD, 16), TILE)
    base = pl.ds(pl.multiple_of(step + 3 * PAD, 16), TILE)
    out[...] = (stream[base, :].astype(F32) + mm(act[rows, :], upcat[...])).astype(BF)


def k_input(d_inner, x, cot, dcat_t, out):
    rows = pl.ds(pl.multiple_of(pl.program_id(0) * TILE + PAD, 16), TILE)
    out[...] = (cot[rows, :].astype(F32) + norm_back(x[...], mm(d_inner[...], dcat_t[...]))).astype(BF)


def tile(rows=TILE):
    return pl.BlockSpec((rows, C), lambda i: (i, 0))


def whole(*shape):
    return pl.BlockSpec(shape, lambda i: (0,) * len(shape), pipeline_mode=pl.Buffered(1))


def scalar():
    return pl.BlockSpec(memory_space=pltpu.SMEM)


def shape(*dims, kind=BF):
    return jax.ShapeDtypeStruct(dims, kind)


def call(body, steps, ins, outs, scratch, flops, name):
    size = lambda s: 2 * math.prod(s.shape)
    return pl.pallas_call(
        body,
        grid=(steps,),
        in_specs=ins,
        out_specs=[spec for spec, _ in outs],
        out_shape=[form for _, form in outs],
        scratch_shapes=scratch,
        compiler_params=pltpu.CompilerParams(vmem_limit_bytes=20 * 1024 * 1024),
        cost_estimate=pl.CostEstimate(
            flops=int(flops), bytes_accessed=2 * sum(size(f) for _, f in outs), transcendentals=0
        ),
        name=name,
    )


LANES = 128
UP = 6 * B
REST = UP + 9 * B + LANES
DOWN = 6 * B
UNIT = 2 * ROWS * C * C
FULL = (tile(), shape(ROWS, C))


def store(rows, kind=BF):
    return pltpu.VMEM((rows, C), kind)


def edges(cells, rows):
    top = lax.ppermute(cells[ROWS - rows :], SEQ, [(i, i + 1) for i in range(BLOCKS - 1)])
    bot = lax.ppermute(cells[:rows], SEQ, [(i + 1, i) for i in range(BLOCKS - 1)])
    return top, bot


SWAP = [(0, 1), (1, 0)]
SHARES = (64, (REST + DOWN) // 64, LANES)


def exchange(parts):
    return lax.all_to_all(parts, CHIPS, 0, 0, tiled=True)


def other_core(cells):
    return lax.ppermute(cells, "core", SWAP)


def local(features, cotangent, strand_pairs, dilations, down_weight, conv_weight, up_weight):
    x = features[0]
    cot = cotangent[0]
    pairs = strand_pairs.reshape(1, C)
    factor = 1.0 / math.sqrt(131072.0)
    block = lax.axis_index(SEQ).reshape(1)
    resident = whole(ROWS, C)
    taps_w = [pl.BlockSpec((None, 3, B, B), lambda i, n=n: (n, 0, 0, 0), pipeline_mode=pl.Buffered(1)) for n in range(2)]
    square_of = [pl.BlockSpec((None, C, C), lambda i, n=n: (n, 0, 0), pipeline_mode=pl.Buffered(1)) for n in range(2)]
    halo, c_halo = whole(4 * PAD, C), whole(2 * PAD, C)

    top, bot = edges(x, 4 * PAD)
    ctop, cbot = edges(cot, 2 * PAD)
    squares = (whole(2, C, C), shape(2, C, C))
    dcat, dcat_t, upcat, upcat_t, kern_t, normed0, inner0 = call(
        k_enter, STEPS, [whole(1, C), whole(2, C, B), whole(2, B, C), whole(2, 3, B, B), tile()],
        [squares] * 4 + [(whole(2, 3, B, B), shape(2, 3, B, B)), FULL, FULL], [], 3 * UNIT, "enter",
    )(pairs, down_weight, up_weight, conv_weight, x)
    mid = (tile(MID_TILE), shape(MID_ROWS, C))
    act0, slope0, tm0, tp0, stream1, normed1, inner1 = call(
        k_middle, 4,
        [scalar(), scalar(), resident, resident, halo, halo, square_of[0], taps_w[0], square_of[0], square_of[1]],
        [mid] * 7, [store(ROWS + 8 * PAD), store(MID_ROWS)], 6 * UNIT, "middle",
    )(dilations, block, inner0, x, top, bot, dcat, conv_weight, upcat, dcat)
    upper = (tile(TOP_TILE), shape(TOP_ROWS, C))
    act1, d_pre1, tm1, tp1 = call(
        k_top, 4, [scalar(), whole(MID_ROWS, C), resident, c_halo, c_halo, taps_w[1], square_of[1]],
        [upper] * 4, [store(TOP_ROWS)], 3 * UNIT, "top",
    )(dilations, inner1, cot, ctop, cbot, conv_weight, upcat_t)
    core = lax.axis_index("core").reshape(1)
    sums = (whole(REST, LANES), shape(REST, LANES))
    downs = (whole(DOWN, LANES), shape(DOWN, LANES))
    joined = (whole(REST + DOWN, LANES), shape(REST + DOWN, LANES))
    shares = (whole(*SHARES), shape(*SHARES))
    wide_top, wide_mid, wide_back = whole(TOP_ROWS, C), whole(MID_ROWS, C), whole(BACK_ROWS, C)
    (rest1,) = call(
        functools.partial(k_sums_top, factor), 1,
        [whole(1, C), wide_top, resident, wide_top, wide_mid, wide_top, wide_top],
        [sums], [], 3 * UNIT, "sums_top",
    )(pairs, act1, cot, tm1, inner1, tp1, d_pre1)
    back = (tile(BACK_TILE), shape(BACK_ROWS, C))
    grad, d_pre0, down1 = call(
        functools.partial(k_back, factor), 3,
        [scalar(), scalar(), whole(1, C), wide_top, taps_w[1], wide_mid, wide_mid, resident, c_halo, c_halo,
         square_of[1], square_of[0], wide_mid],
        [back, back, downs],
        [store(BACK_TILE), store(BACK_TILE), store(BACK_ROWS), store(BACK_ROWS)],
        5 * UNIT, "back",
    )(dilations, block, pairs, d_pre1, kern_t, normed1, stream1, cot, ctop, cbot, dcat_t, upcat_t, slope0)
    send_a, keep_a = call(
        functools.partial(k_sums, factor), 1,
        [scalar(), whole(1, C), wide_mid, wide_back, wide_mid, resident, wide_mid, wide_back, sums[0]],
        [sums, sums], [pltpu.VMEM((REST, LANES), BF)], 3 * UNIT, "sums",
    )(core, pairs, act0, grad, tm0, inner0, tp0, d_pre0, rest1)
    send_b, keep_b, d_inner0 = call(
        functools.partial(k_last, factor), STEPS,
        [scalar(), scalar(), whole(1, C), wide_back, taps_w[0], resident, downs[0]],
        [downs, downs, (resident, shape(ROWS, C))],
        [store(TILE), store(TILE), pltpu.VMEM((DOWN, LANES), BF)],
        3 * UNIT, "last",
    )(core, dilations, pairs, d_pre0, kern_t, normed0, down1)
    (parts,) = call(
        k_join, 1, [sums[0], sums[0], downs[0], downs[0]], [joined], [], 0, "join",
    )(keep_a, other_core(send_a), keep_b, other_core(send_b))
    parts, act1, d_inner0 = lax.optimization_barrier((parts, act1, d_inner0))
    (out,) = call(
        k_out, STEPS, [wide_top, wide_mid, square_of[1]], [FULL], [], UNIT, "out",
    )(act1, stream1, upcat)
    (input_grad,) = call(
        k_input, STEPS, [tile(), tile(), wide_back, square_of[0]], [FULL], [], UNIT, "input",
    )(d_inner0, x, grad, dcat_t)
    parts = exchange(parts.reshape(SHARES))
    parts, out, input_grad = lax.optimization_barrier((parts, out, input_grad))
    (shared,) = call(k_share, 1, [shares[0]], [shares], [], 0, "share")(parts)
    mine = exchange(shared).reshape(REST + DOWN, LANES)
    other = other_core(mine)
    grads = write_layer(core, mine, ())
    grads = write_layer(1 - core, other, grads)
    return (out[None], input_grad[None], *grads)


def solution(mesh):
    fine = Mesh(mesh.devices.reshape(2, 2, 4, 2, 4), ("xh", "core", "z", "xl", "y"))
    rows = P(("xh", "core"), SEQ, None)
    in_specs = (rows, rows, P(), P(), P(), P(), P())
    out_specs = (rows, rows, P(), P(), P())
    return jax.shard_map(local, mesh=fine, in_specs=in_specs, out_specs=out_specs, check_vma=False)
```

```python
import functools
import math

import jax
import jax.numpy as jnp
from jax import lax
from jax.experimental import pallas as pl
from jax.experimental.pallas import tpu as pltpu
from jax.sharding import Mesh, PartitionSpec as P

C = 768
B = 384
PAD = 64
ROWS = 1024
TILE = 256
STEPS = ROWS // TILE
BLOCKS = 32
MID_ROWS, TOP_ROWS, BACK_ROWS = ROWS + 6 * PAD, ROWS + 4 * PAD, ROWS + 2 * PAD
MID_TILE, TOP_TILE, BACK_TILE = MID_ROWS // 4, TOP_ROWS // 4, BACK_ROWS // 3
EPS = 1e-06
ROOT = math.sqrt(2.0 / math.pi)
CUBE = 0.044715
BF = jnp.bfloat16
F32 = jnp.float32
SEQ = ("z", "xl", "y")
CHIPS = ("xh", "z", "xl", "y")


def mm(left, right):
    return lax.dot_general(left, right, (((1,), (0,)), ((), ())), preferred_element_type=F32)


def mm_nt(left, right):
    return lax.dot_general(left, right, (((1,), (1,)), ((), ())), preferred_element_type=F32)


def mm_tn(left, right):
    return lax.dot_general(left, right, (((0,), (0,)), ((), ())), preferred_element_type=F32)


def swap(pairs_ref):
    rows = lax.broadcasted_iota(jnp.int32, (C, C), 0)
    return (rows == pairs_ref[...]).astype(F32).astype(BF)


def scale_of(wide):
    return lax.rsqrt(jnp.mean(wide * wide, axis=-1, keepdims=True) + EPS)


def lay(dst, top, mid, bot):
    start = 0
    for piece in (top, mid, bot):
        rows = piece.shape[0]
        dst[start : start + rows, :] = piece.astype(dst.dtype)
        start += rows


def shift(cells, dil, start, before, after):
    rows = before.shape[0]
    base = pl.multiple_of(start + PAD, 16)

    @pl.when(dil >= 16)
    def _():
        for sign, ref in ((-1, before), (1, after)):
            ref[...] = cells[pl.ds(pl.multiple_of(base + sign * dil, 16), rows), :]

    for small in (1, 2, 4, 8):

        @pl.when(dil == small)
        def _():
            window = cells[pl.ds(pl.multiple_of(base - 16, 16), rows + 32), :].astype(F32)
            before[...] = window[16 - small : 16 - small + rows].astype(BF)
            after[...] = window[16 + small : 16 + small + rows].astype(BF)


def centre(cells, start, rows):
    return cells[pl.ds(pl.multiple_of(start + PAD, 16), rows), :]


def conv(first, last, mid, weight, product=mm):
    rows = mid.shape[0]
    rows_a = jnp.concatenate([first[:, :B], mid[:, :B], last[:, :B]], axis=1)
    rows_b = jnp.concatenate([last[:, B:], mid[:, B:], first[:, B:]], axis=1)
    both = product(jnp.concatenate([rows_a, rows_b], axis=0), weight)
    return jnp.concatenate([both[:rows], both[rows:]], axis=1)


def conv_back(first, last, mid, weight):
    beside = jnp.concatenate([weight[k] for k in range(3)], axis=1)
    return conv(first, last, mid, beside, mm_nt)


def inside(block, start, values):
    rows = lax.broadcasted_iota(jnp.int32, (values.shape[0], 1), 0) + (block * ROWS + start)
    return jnp.where((rows >= 0) & (rows < BLOCKS * ROWS), values, 0.0)


def gelu_both(pre):
    sq = pre * pre
    t = jnp.tanh(pre * (ROOT + (ROOT * CUBE) * sq))
    half = 0.5 + 0.5 * t
    act = pre * half
    return act, half + (act * (1.0 - t)) * (ROOT + (3.0 * CUBE * ROOT) * sq)


def k_enter(pairs, down, up, x, dcat, upcat, normed, inner):
    @pl.when(pl.program_id(0) == 0)
    def _():
        s = swap(pairs)
        for layer in range(2):
            dcat[layer, :, :B] = down[layer]
            dcat[layer, :, B:] = mm(s, down[layer]).astype(BF)
            upcat[layer, :B, :] = up[layer]
            upcat[layer, B:, :] = mm(up[layer], s).astype(BF)

    wide = x[...].astype(F32)
    n = (wide * scale_of(wide)).astype(BF)
    normed[...] = n
    inner[...] = mm(n, dcat[0]).astype(BF)


def k_middle(dil, block, mid, x, top, bot, dcat0, weight, upcat, dcat,
             act, slope, tm, tp, stream, normed, inner, pad, field):
    start = pl.program_id(0) * MID_TILE

    @pl.when(pl.program_id(0) == 0)
    def _():
        lay(field, top[PAD : 4 * PAD, :], x[...], bot[: 3 * PAD, :])
        ends = []
        for halo in (top, bot):
            wide = halo[...].astype(F32)
            ends.append(mm((wide * scale_of(wide)).astype(BF), dcat0[...]).astype(BF))
        lay(pad, ends[0], mid[...], ends[1])

    shift(pad, dil[0], start, tm, tp)
    m = centre(pad, start, MID_TILE)
    g, s = gelu_both(conv(tm[...], tp[...], m, weight[...].reshape(3 * B, B)))
    g = g.astype(BF)
    act[...] = g
    slope[...] = s.astype(BF)
    rows = pl.ds(pl.multiple_of(start, 16), MID_TILE)
    out = (field[rows, :].astype(F32) + mm(g, upcat[...])).astype(BF)
    stream[...] = out
    wide = out.astype(F32)
    n = (wide * scale_of(wide)).astype(BF)
    normed[...] = n
    inner[...] = inside(block[0], start - 3 * PAD, mm(n, dcat[...])).astype(BF)


def k_top(dil, mid, cot, top, bot, weight, upcat, act, d_pre, tm, tp, grad):
    start = pl.program_id(0) * TOP_TILE

    @pl.when(pl.program_id(0) == 0)
    def _():
        lay(grad, top[...], cot[...], bot[...])

    shift(mid, dil[1], start, tm, tp)
    m = centre(mid, start, TOP_TILE)
    rows = pl.ds(pl.multiple_of(start, 16), TOP_TILE)
    d_act = mm_nt(grad[rows, :], upcat[...])
    g, s = gelu_both(conv(tm[...], tp[...], m, weight[...].reshape(3 * B, B)))
    act[...] = g.astype(BF)
    d_pre[...] = (d_act * s).astype(BF)


def put(ref, start, value):
    rows, cols = value.shape
    for i in range(cols // LANES):
        ref[start + i * rows : start + (i + 1) * rows, :] = value[:, i * LANES : (i + 1) * LANES].astype(BF)


def take(ref, start, rows, cols):
    pieces = [ref[start + i * rows : start + (i + 1) * rows, :] for i in range(cols // LANES)]
    return jnp.concatenate(pieces, axis=1).astype(F32)


def own(ref, before):
    return ref[before : before + ROWS, :]


def weight_sums(factor, pairs, act, cot, taps, d_pre, rest):
    up = mm_tn(act, cot) * factor
    put(rest, 0, up[:B] + mm(up[B:].astype(BF), swap(pairs)))
    rows_a = jnp.concatenate([tap[:, :B] for tap in taps], axis=1)
    rows_b = jnp.concatenate([tap[:, B:] for tap in taps[::-1]], axis=1)
    total = (mm_tn(d_pre[:, :B], rows_a) + mm_tn(d_pre[:, B:], rows_b)) * factor
    for k in range(3):
        put(rest, UP + k * 3 * B, total[:, k * B : (k + 1) * B].T)
    rest[REST - LANES :, :] = jnp.zeros((LANES, LANES), BF)


def sort_out(core, lower, upper, send, keep):
    @pl.when(core[0] == 0)
    def _():
        send[...] = upper[...]
        keep[...] = lower[...]

    @pl.when(core[0] != 0)
    def _():
        send[...] = lower[...]
        keep[...] = upper[...]


def k_sums_top(factor, pairs, act, cot, tm, tc, tp, d_pre, rest):
    taps = [own(tm, 2 * PAD), own(tc, 3 * PAD), own(tp, 2 * PAD)]
    weight_sums(factor, pairs, own(act, 2 * PAD), cot[...], taps, own(d_pre, 2 * PAD), rest)


def k_sums(factor, core, pairs, act, cot, tm, tc, tp, d_pre, upper, send, keep, rest):
    taps = [own(tm, 3 * PAD), tc[...], own(tp, 3 * PAD)]
    weight_sums(factor, pairs, own(act, 3 * PAD), own(cot, PAD), taps, own(d_pre, PAD), rest)
    sort_out(core, rest, upper, send, keep)


def down_sum(factor, pairs, normed, d_inner, down):
    total = mm_tn(normed, d_inner) * factor
    put(down, 0, total[:, :B] + mm(swap(pairs), total[:, B:].astype(BF)))


def k_join(keep_a, got_a, keep_b, got_b, out):
    out[:REST, :] = (keep_a[...].astype(F32) + got_a[...].astype(F32)).astype(BF)
    out[REST:, :] = (keep_b[...].astype(F32) + got_b[...].astype(F32)).astype(BF)


def k_share(parts, out):
    share = jnp.sum(parts[...].astype(F32), axis=0).astype(BF)
    out[...] = jnp.broadcast_to(share[None], out.shape)


def k_finish(layer, ref, *rest):
    down, kern, up = rest[-3:]
    up[0] = take(ref, 0, B, C)
    for k in range(3):
        kern[0, k] = take(ref, UP + k * 3 * B, B, B)
    down[0] = take(ref, REST, C, B)


def write_layer(layer, total, outs):
    dims = ((C, B), (3, B, B), (B, C))
    blocks = [pl.BlockSpec((1,) + d, lambda i, n, d=d: (n[0],) + (0,) * len(d)) for d in dims]
    return pl.pallas_call(
        k_finish,
        grid_spec=pltpu.PrefetchScalarGridSpec(
            num_scalar_prefetch=1,
            grid=(1,),
            in_specs=[pl.BlockSpec(total.shape, lambda i, n: (0, 0))] + [pl.BlockSpec(memory_space=pl.ANY)] * len(outs),
            out_specs=blocks,
        ),
        out_shape=[shape(2, *d, kind=F32) for d in dims],
        input_output_aliases={2 + i: i for i in range(len(outs))},
        compiler_params=pltpu.CompilerParams(vmem_limit_bytes=20 * 1024 * 1024),
        name="finish",
    )(layer, total, *outs)


def norm_back(v, d_norm):
    wide = v.astype(F32)
    scale = scale_of(wide)
    mixed = jnp.mean(d_norm * wide, axis=-1, keepdims=True)
    return scale * d_norm - wide * (scale * scale * scale * mixed)


def k_back(factor, dil, block, pairs, mid, weight, normed, stream, cot, top, bot, dcat, upcat, slope,
           grad, d_pre, down, before, after, d_inner, given):
    start = pl.program_id(0) * BACK_TILE

    @pl.when(pl.program_id(0) == 0)
    def _():
        lay(given, top[PAD:, :], cot[...], bot[:PAD, :])

    shift(mid, dil[1], start, before, after)
    di = conv_back(after[...], before[...], centre(mid, start, BACK_TILE), weight).astype(BF)
    rows = pl.ds(pl.multiple_of(start, 16), BACK_TILE)
    saved = pl.ds(pl.multiple_of(start + 2 * PAD, 16), BACK_TILE)
    d_inner[rows, :] = di
    g = given[rows, :].astype(F32) + norm_back(stream[saved, :], mm_nt(di, dcat[...]))
    g = inside(block[0], start - PAD, g).astype(BF)
    grad[...] = g
    d_pre[...] = (mm_nt(g, upcat[...]) * slope[saved, :].astype(F32)).astype(BF)

    @pl.when(pl.program_id(0) == pl.num_programs(0) - 1)
    def _():
        down_sum(factor, pairs, own(normed, 3 * PAD), own(d_inner, PAD), down)


def k_last(factor, core, dil, pairs, mid, weight, normed, upper, send, keep, d_inner, before, after, down):
    start = pl.program_id(0) * TILE

    shift(mid, dil[0], start, before, after)
    di = conv_back(after[...], before[...], centre(mid, start, TILE), weight).astype(BF)
    d_inner[pl.ds(pl.multiple_of(start, 16), TILE), :] = di

    @pl.when(pl.program_id(0) == pl.num_programs(0) - 1)
    def _():
        down_sum(factor, pairs, normed[...], d_inner[...], down)
        sort_out(core, down, upper, send, keep)


def k_out(act, stream, upcat, out):
    step = pl.program_id(0) * TILE
    rows = pl.ds(pl.multiple_of(step + 2 * PAD, 16), TILE)
    base = pl.ds(pl.multiple_of(step + 3 * PAD, 16), TILE)
    out[...] = (stream[base, :].astype(F32) + mm(act[rows, :], upcat[...])).astype(BF)


def k_input(d_inner, x, cot, dcat, out):
    rows = pl.ds(pl.multiple_of(pl.program_id(0) * TILE + PAD, 16), TILE)
    out[...] = (cot[rows, :].astype(F32) + norm_back(x[...], mm_nt(d_inner[...], dcat[...]))).astype(BF)


def tile(rows=TILE):
    return pl.BlockSpec((rows, C), lambda i: (i, 0))


def whole(*shape):
    return pl.BlockSpec(shape, lambda i: (0,) * len(shape), pipeline_mode=pl.Buffered(1))


def scalar():
    return pl.BlockSpec(memory_space=pltpu.SMEM)


def shape(*dims, kind=BF):
    return jax.ShapeDtypeStruct(dims, kind)


def call(body, steps, ins, outs, scratch, flops, name, limit=20):
    size = lambda s: 2 * math.prod(s.shape)
    return pl.pallas_call(
        body,
        grid=(steps,),
        in_specs=ins,
        out_specs=[spec for spec, _ in outs],
        out_shape=[form for _, form in outs],
        scratch_shapes=scratch,
        compiler_params=pltpu.CompilerParams(vmem_limit_bytes=limit * 1024 * 1024),
        cost_estimate=pl.CostEstimate(
            flops=int(flops), bytes_accessed=2 * sum(size(f) for _, f in outs), transcendentals=0
        ),
        name=name,
    )


LANES = 128
UP = 6 * B
REST = UP + 9 * B + LANES
DOWN = 6 * B
UNIT = 2 * ROWS * C * C
FULL = (tile(), shape(ROWS, C))


def store(rows, kind=BF):
    return pltpu.VMEM((rows, C), kind)


def edges(cells, rows):
    top = lax.ppermute(cells[ROWS - rows :], SEQ, [(i, i + 1) for i in range(BLOCKS - 1)])
    bot = lax.ppermute(cells[:rows], SEQ, [(i + 1, i) for i in range(BLOCKS - 1)])
    return top, bot


SWAP = [(0, 1), (1, 0)]
SHARES = (64, (REST + DOWN) // 64, LANES)


def exchange(parts):
    return lax.all_to_all(parts, CHIPS, 0, 0, tiled=True)


def other_core(cells):
    return lax.ppermute(cells, "core", SWAP)


def local(features, cotangent, strand_pairs, dilations, down_weight, conv_weight, up_weight):
    x = features[0]
    cot = cotangent[0]
    pairs = strand_pairs.reshape(1, C)
    factor = 1.0 / math.sqrt(131072.0)
    block = lax.axis_index(SEQ).reshape(1)
    resident = whole(ROWS, C)
    taps_w = [pl.BlockSpec((None, 3, B, B), lambda i, n=n: (n, 0, 0, 0), pipeline_mode=pl.Buffered(1)) for n in range(2)]
    square_of = [pl.BlockSpec((None, C, C), lambda i, n=n: (n, 0, 0), pipeline_mode=pl.Buffered(1)) for n in range(2)]
    halo, c_halo = whole(4 * PAD, C), whole(2 * PAD, C)

    top, bot = edges(x, 4 * PAD)
    ctop, cbot = edges(cot, 2 * PAD)
    squares = (whole(2, C, C), shape(2, C, C))
    dcat, upcat, normed0, inner0 = call(
        k_enter, STEPS, [whole(1, C), whole(2, C, B), whole(2, B, C), tile()],
        [squares] * 2 + [FULL, FULL], [], 3 * UNIT, "enter",
    )(pairs, down_weight, up_weight, x)
    mid = (tile(MID_TILE), shape(MID_ROWS, C))
    act0, slope0, tm0, tp0, stream1, normed1, inner1 = call(
        k_middle, 4,
        [scalar(), scalar(), resident, resident, halo, halo, square_of[0], taps_w[0], square_of[0], square_of[1]],
        [mid] * 7, [store(ROWS + 8 * PAD), store(MID_ROWS)], 6 * UNIT, "middle",
    )(dilations, block, inner0, x, top, bot, dcat, conv_weight, upcat, dcat)
    upper = (tile(TOP_TILE), shape(TOP_ROWS, C))
    act1, d_pre1, tm1, tp1 = call(
        k_top, 4, [scalar(), whole(MID_ROWS, C), resident, c_halo, c_halo, taps_w[1], square_of[1]],
        [upper] * 4, [store(TOP_ROWS)], 3 * UNIT, "top",
    )(dilations, inner1, cot, ctop, cbot, conv_weight, upcat)
    core = lax.axis_index("core").reshape(1)
    sums = (whole(REST, LANES), shape(REST, LANES))
    downs = (whole(DOWN, LANES), shape(DOWN, LANES))
    joined = (whole(REST + DOWN, LANES), shape(REST + DOWN, LANES))
    shares = (whole(*SHARES), shape(*SHARES))
    wide_top, wide_mid, wide_back = whole(TOP_ROWS, C), whole(MID_ROWS, C), whole(BACK_ROWS, C)
    (rest1,) = call(
        functools.partial(k_sums_top, factor), 1,
        [whole(1, C), wide_top, resident, wide_top, wide_mid, wide_top, wide_top],
        [sums], [], 3 * UNIT, "sums_top",
    )(pairs, act1, cot, tm1, inner1, tp1, d_pre1)
    back = (tile(BACK_TILE), shape(BACK_ROWS, C))
    grad, d_pre0, down1 = call(
        functools.partial(k_back, factor), 3,
        [scalar(), scalar(), whole(1, C), wide_top, taps_w[1], wide_mid, wide_mid, resident, c_halo, c_halo,
         square_of[1], square_of[0], wide_mid],
        [back, back, downs],
        [store(BACK_TILE), store(BACK_TILE), store(BACK_ROWS), store(BACK_ROWS)],
        5 * UNIT, "back",
    )(dilations, block, pairs, d_pre1, conv_weight, normed1, stream1, cot, ctop, cbot, dcat, upcat, slope0)
    send_a, keep_a = call(
        functools.partial(k_sums, factor), 1,
        [scalar(), whole(1, C), wide_mid, wide_back, wide_mid, resident, wide_mid, wide_back, sums[0]],
        [sums, sums], [pltpu.VMEM((REST, LANES), BF)], 3 * UNIT, "sums",
    )(core, pairs, act0, grad, tm0, inner0, tp0, d_pre0, rest1)
    send_b, keep_b, d_inner0 = call(
        functools.partial(k_last, factor), STEPS,
        [scalar(), scalar(), whole(1, C), wide_back, taps_w[0], resident, downs[0]],
        [downs, downs, (resident, shape(ROWS, C))],
        [store(TILE), store(TILE), pltpu.VMEM((DOWN, LANES), BF)],
        3 * UNIT, "last",
    )(core, dilations, pairs, d_pre0, conv_weight, normed0, down1)
    (parts,) = call(
        k_join, 1, [sums[0], sums[0], downs[0], downs[0]], [joined], [], 0, "join",
    )(keep_a, other_core(send_a), keep_b, other_core(send_b))
    parts, act1, d_inner0 = lax.optimization_barrier((parts, act1, d_inner0))
    (out,) = call(
        k_out, STEPS, [wide_top, wide_mid, square_of[1]], [FULL], [], UNIT, "out",
    )(act1, stream1, upcat)
    (input_grad,) = call(
        k_input, STEPS, [tile(), tile(), wide_back, square_of[0]], [FULL], [], UNIT, "input",
    )(d_inner0, x, grad, dcat)
    parts = exchange(parts.reshape(SHARES))
    parts, out, input_grad = lax.optimization_barrier((parts, out, input_grad))
    (shared,) = call(k_share, 1, [shares[0]], [shares], [], 0, "share")(parts)
    mine = exchange(shared).reshape(REST + DOWN, LANES)
    other = other_core(mine)
    grads = write_layer(core, mine, ())
    grads = write_layer(1 - core, other, grads)
    return (out[None], input_grad[None], *grads)


def solution(mesh):
    fine = Mesh(mesh.devices.reshape(2, 2, 4, 2, 4), ("xh", "core", "z", "xl", "y"))
    rows = P(("xh", "core"), SEQ, None)
    in_specs = (rows, rows, P(), P(), P(), P(), P())
    out_specs = (rows, rows, P(), P(), P())
    return jax.shard_map(local, mesh=fine, in_specs=in_specs, out_specs=out_specs, check_vma=False)
```

```python
import functools
import math

import jax
import jax.numpy as jnp
from jax import lax
from jax.experimental import pallas as pl
from jax.experimental.pallas import tpu as pltpu
from jax.sharding import Mesh, PartitionSpec as P

C = 768
B = 384
PAD = 64
ROWS = 1024
TILE = 256
STEPS = ROWS // TILE
BLOCKS = 32
MID_ROWS, TOP_ROWS, BACK_ROWS = ROWS + 6 * PAD, ROWS + 4 * PAD, ROWS + 2 * PAD
MID_TILE, TOP_TILE, BACK_TILE = 2 * PAD, TOP_ROWS // 4, BACK_ROWS // 3
EPS = 1e-06
ROOT = math.sqrt(2.0 / math.pi)
CUBE = 0.044715
BF = jnp.bfloat16
F32 = jnp.float32
SEQ = ("z", "xl", "y")
CHIPS = ("xh", "z", "xl", "y")


def mm(left, right):
    return lax.dot_general(left, right, (((1,), (0,)), ((), ())), preferred_element_type=F32)


def mm_nt(left, right):
    return lax.dot_general(left, right, (((1,), (1,)), ((), ())), preferred_element_type=F32)


def mm_tn(left, right):
    return lax.dot_general(left, right, (((0,), (0,)), ((), ())), preferred_element_type=F32)


def swap(pairs_ref):
    rows = lax.broadcasted_iota(jnp.int32, (C, C), 0)
    return (rows == pairs_ref[...]).astype(F32).astype(BF)


def scale_of(wide):
    return lax.rsqrt(jnp.mean(wide * wide, axis=-1, keepdims=True) + EPS)


def lay(dst, top, mid, bot):
    start = 0
    for piece in (top, mid, bot):
        rows = piece.shape[0]
        dst[start : start + rows, :] = piece.astype(dst.dtype)
        start += rows


def shift(cells, dil, start, before, after):
    rows = before.shape[0]
    base = pl.multiple_of(start + PAD, 16)

    @pl.when(dil >= 16)
    def _():
        for sign, ref in ((-1, before), (1, after)):
            ref[...] = cells[pl.ds(pl.multiple_of(base + sign * dil, 16), rows), :]

    for small in (1, 2, 4, 8):

        @pl.when(dil == small)
        def _():
            window = cells[pl.ds(pl.multiple_of(base - 16, 16), rows + 32), :].astype(F32)
            before[...] = window[16 - small : 16 - small + rows].astype(BF)
            after[...] = window[16 + small : 16 + small + rows].astype(BF)


def centre(cells, start, rows):
    return cells[pl.ds(pl.multiple_of(start + PAD, 16), rows), :]


def conv(first, last, mid, weight, product=mm):
    rows = mid.shape[0]
    rows_a = jnp.concatenate([first[:, :B], mid[:, :B], last[:, :B]], axis=1)
    rows_b = jnp.concatenate([last[:, B:], mid[:, B:], first[:, B:]], axis=1)
    both = product(jnp.concatenate([rows_a, rows_b], axis=0), weight)
    return jnp.concatenate([both[:rows], both[rows:]], axis=1)


def conv_back(first, last, mid, weight):
    beside = jnp.concatenate([weight[k] for k in range(3)], axis=1)
    return conv(first, last, mid, beside, mm_nt)


def inside(block, start, values):
    rows = lax.broadcasted_iota(jnp.int32, (values.shape[0], 1), 0) + (block * ROWS + start)
    return jnp.where((rows >= 0) & (rows < BLOCKS * ROWS), values, 0.0)


def gelu_both(pre):
    sq = pre * pre
    t = jnp.tanh(pre * (ROOT + (ROOT * CUBE) * sq))
    half = 0.5 + 0.5 * t
    act = pre * half
    return act, half + (act * (1.0 - t)) * (ROOT + (3.0 * CUBE * ROOT) * sq)


def k_enter(pairs, down, up, x, dcat, upcat, normed, inner):
    @pl.when(pl.program_id(0) == 0)
    def _():
        s = swap(pairs)
        for layer in range(2):
            dcat[layer, :, :B] = down[layer]
            dcat[layer, :, B:] = mm(s, down[layer]).astype(BF)
            upcat[layer, :B, :] = up[layer]
            upcat[layer, B:, :] = mm(up[layer], s).astype(BF)

    wide = x[...].astype(F32)
    n = (wide * scale_of(wide)).astype(BF)
    normed[...] = n
    inner[...] = mm(n, dcat[0]).astype(BF)


def middle_rows(m, x, weight, upcat, dcat, act, slope, tm, tp, stream, normed):
    g, s = gelu_both(conv(tm[...], tp[...], m, weight[...].reshape(3 * B, B)))
    g = g.astype(BF)
    act[...] = g
    slope[...] = s.astype(BF)
    out = (x.astype(F32) + mm(g, upcat[...])).astype(BF)
    stream[...] = out
    wide = out.astype(F32)
    n = (wide * scale_of(wide)).astype(BF)
    normed[...] = n
    return mm(n, dcat[...])


def k_within(dil, mid, x, weight, upcat, dcat, act, slope, tm, tp, stream, normed, inner):
    start = pl.program_id(0) * MID_TILE
    shift(mid, dil[0], start, tm, tp)
    rows = centre(x, start, MID_TILE)
    m = centre(mid, start, MID_TILE)
    inner[...] = middle_rows(m, rows, weight, upcat, dcat, act, slope, tm, tp, stream, normed).astype(BF)


def k_around(dil, block, mid, x, top, bot, dcat0, weight, upcat, dcat, *rest):
    act, slope, tm, tp, stream, normed, inner, pad, field = rest[7:]
    step = pl.program_id(0)

    @pl.when(step == 0)
    def _():
        field[: 3 * PAD, :] = top[PAD : 4 * PAD, :]
        field[3 * PAD : 4 * PAD, :] = x[:PAD, :]
        field[4 * PAD : 5 * PAD, :] = x[ROWS - PAD :, :]
        field[5 * PAD :, :] = bot[: 3 * PAD, :]
        ends = []
        for halo in (top, bot):
            wide = halo[: 4 * PAD, :].astype(F32)
            ends.append(mm((wide * scale_of(wide)).astype(BF), dcat0[...]).astype(BF))
        pad[: 4 * PAD, :] = ends[0]
        pad[4 * PAD : 6 * PAD, :] = mid[: 2 * PAD, :]
        pad[6 * PAD : 8 * PAD, :] = mid[ROWS - 2 * PAD :, :]
        pad[8 * PAD :, :] = ends[1]

    start = pl.multiple_of((step + step // 2) * MID_TILE, MID_TILE)
    shift(pad, dil[0], start, tm, tp)
    m = centre(pad, start, MID_TILE)
    rows = field[pl.ds(pl.multiple_of(step * MID_TILE, MID_TILE), MID_TILE), :]
    values = middle_rows(m, rows, weight, upcat, dcat, act, slope, tm, tp, stream, normed)
    inner[...] = inside(block[0], around(step) * MID_TILE - 3 * PAD, values).astype(BF)


def around(step):
    return step + 7 * (step // 2)


def k_top(dil, mid, cot, top, bot, weight, upcat, act, d_pre, tm, tp, grad):
    start = pl.program_id(0) * TOP_TILE

    @pl.when(pl.program_id(0) == 0)
    def _():
        lay(grad, top[4 * PAD :, :], cot[...], bot[4 * PAD :, :])

    shift(mid, dil[1], start, tm, tp)
    m = centre(mid, start, TOP_TILE)
    rows = pl.ds(pl.multiple_of(start, 16), TOP_TILE)
    d_act = mm_nt(grad[rows, :], upcat[...])
    g, s = gelu_both(conv(tm[...], tp[...], m, weight[...].reshape(3 * B, B)))
    act[...] = g.astype(BF)
    d_pre[...] = (d_act * s).astype(BF)


def put(ref, start, value):
    rows, cols = value.shape
    for i in range(cols // LANES):
        ref[start + i * rows : start + (i + 1) * rows, :] = value[:, i * LANES : (i + 1) * LANES].astype(BF)


def take(ref, start, rows, cols):
    pieces = [ref[start + i * rows : start + (i + 1) * rows, :] for i in range(cols // LANES)]
    return jnp.concatenate(pieces, axis=1).astype(F32)


def own(ref, before):
    return ref[before : before + ROWS, :]


def weight_sums(factor, pairs, act, cot, taps, d_pre, rest):
    up = mm_tn(act, cot) * factor
    put(rest, 0, up[:B] + mm(up[B:].astype(BF), swap(pairs)))
    rows_a = jnp.concatenate([tap[:, :B] for tap in taps], axis=1)
    rows_b = jnp.concatenate([tap[:, B:] for tap in taps[::-1]], axis=1)
    total = (mm_tn(d_pre[:, :B], rows_a) + mm_tn(d_pre[:, B:], rows_b)) * factor
    for k in range(3):
        put(rest, UP + k * 3 * B, total[:, k * B : (k + 1) * B].T)
    rest[REST - LANES :, :] = jnp.zeros((LANES, LANES), BF)


def sort_out(core, lower, upper, send, keep):
    @pl.when(core[0] == 0)
    def _():
        send[...] = upper[...]
        keep[...] = lower[...]

    @pl.when(core[0] != 0)
    def _():
        send[...] = lower[...]
        keep[...] = upper[...]


def k_sums_top(factor, pairs, act, cot, tm, tc, tp, d_pre, rest):
    taps = [own(tm, 2 * PAD), own(tc, 3 * PAD), own(tp, 2 * PAD)]
    weight_sums(factor, pairs, own(act, 2 * PAD), cot[...], taps, own(d_pre, 2 * PAD), rest)


def k_sums(factor, core, pairs, act, cot, tm, tc, tp, d_pre, upper, send, keep, rest):
    taps = [own(tm, 3 * PAD), tc[...], own(tp, 3 * PAD)]
    weight_sums(factor, pairs, own(act, 3 * PAD), own(cot, PAD), taps, own(d_pre, PAD), rest)
    sort_out(core, rest, upper, send, keep)


def down_sum(factor, pairs, normed, d_inner, down):
    total = mm_tn(normed, d_inner) * factor
    put(down, 0, total[:, :B] + mm(swap(pairs), total[:, B:].astype(BF)))


def k_join(keep_a, got_a, keep_b, got_b, out):
    out[:REST, :] = (keep_a[...].astype(F32) + got_a[...].astype(F32)).astype(BF)
    out[REST:, :] = (keep_b[...].astype(F32) + got_b[...].astype(F32)).astype(BF)


def k_share(parts, out):
    share = jnp.sum(parts[...].astype(F32), axis=0).astype(BF)
    out[...] = jnp.broadcast_to(share[None], out.shape)


def k_finish(layer, ref, *rest):
    down, kern, up = rest[-3:]
    up[0] = take(ref, 0, B, C)
    for k in range(3):
        kern[0, k] = take(ref, UP + k * 3 * B, B, B)
    down[0] = take(ref, REST, C, B)


def write_layer(layer, total, outs):
    dims = ((C, B), (3, B, B), (B, C))
    blocks = [pl.BlockSpec((1,) + d, lambda i, n, d=d: (n[0],) + (0,) * len(d)) for d in dims]
    return pl.pallas_call(
        k_finish,
        grid_spec=pltpu.PrefetchScalarGridSpec(
            num_scalar_prefetch=1,
            grid=(1,),
            in_specs=[pl.BlockSpec(total.shape, lambda i, n: (0, 0))] + [pl.BlockSpec(memory_space=pl.ANY)] * len(outs),
            out_specs=blocks,
        ),
        out_shape=[shape(2, *d, kind=F32) for d in dims],
        input_output_aliases={2 + i: i for i in range(len(outs))},
        compiler_params=pltpu.CompilerParams(vmem_limit_bytes=20 * 1024 * 1024),
        name="finish",
    )(layer, total, *outs)


def norm_back(v, d_norm):
    wide = v.astype(F32)
    scale = scale_of(wide)
    mixed = jnp.mean(d_norm * wide, axis=-1, keepdims=True)
    return scale * d_norm - wide * (scale * scale * scale * mixed)


def k_back(factor, dil, block, pairs, mid, weight, normed, stream, cot, top, bot, dcat, upcat, slope,
           grad, d_pre, down, before, after, d_inner, given):
    start = pl.program_id(0) * BACK_TILE

    @pl.when(pl.program_id(0) == 0)
    def _():
        lay(given, top[5 * PAD :, :], cot[...], bot[4 * PAD : 5 * PAD, :])

    shift(mid, dil[1], start, before, after)
    di = conv_back(after[...], before[...], centre(mid, start, BACK_TILE), weight).astype(BF)
    rows = pl.ds(pl.multiple_of(start, 16), BACK_TILE)
    saved = pl.ds(pl.multiple_of(start + 2 * PAD, 16), BACK_TILE)
    d_inner[rows, :] = di
    g = given[rows, :].astype(F32) + norm_back(stream[saved, :], mm_nt(di, dcat[...]))
    g = inside(block[0], start - PAD, g).astype(BF)
    grad[...] = g
    d_pre[...] = (mm_nt(g, upcat[...]) * slope[saved, :].astype(F32)).astype(BF)

    @pl.when(pl.program_id(0) == pl.num_programs(0) - 1)
    def _():
        down_sum(factor, pairs, own(normed, 3 * PAD), own(d_inner, PAD), down)


def k_last(factor, core, dil, pairs, mid, weight, normed, upper, send, keep, d_inner, before, after, down):
    start = pl.program_id(0) * TILE

    shift(mid, dil[0], start, before, after)
    di = conv_back(after[...], before[...], centre(mid, start, TILE), weight).astype(BF)
    d_inner[pl.ds(pl.multiple_of(start, 16), TILE), :] = di

    @pl.when(pl.program_id(0) == pl.num_programs(0) - 1)
    def _():
        down_sum(factor, pairs, normed[...], d_inner[...], down)
        sort_out(core, down, upper, send, keep)


def k_out(act, stream, upcat, out):
    step = pl.program_id(0) * TILE
    rows = pl.ds(pl.multiple_of(step + 2 * PAD, 16), TILE)
    base = pl.ds(pl.multiple_of(step + 3 * PAD, 16), TILE)
    out[...] = (stream[base, :].astype(F32) + mm(act[rows, :], upcat[...])).astype(BF)


def k_input(d_inner, x, cot, dcat, out):
    rows = pl.ds(pl.multiple_of(pl.program_id(0) * TILE + PAD, 16), TILE)
    out[...] = (cot[rows, :].astype(F32) + norm_back(x[...], mm_nt(d_inner[...], dcat[...]))).astype(BF)


def tile(rows=TILE):
    return pl.BlockSpec((rows, C), lambda i: (i, 0))


def whole(*shape):
    return pl.BlockSpec(shape, lambda i: (0,) * len(shape), pipeline_mode=pl.Buffered(1))


def scalar():
    return pl.BlockSpec(memory_space=pltpu.SMEM)


def shape(*dims, kind=BF):
    return jax.ShapeDtypeStruct(dims, kind)


def call(body, steps, ins, outs, scratch, flops, name, limit=20, aliases=None):
    size = lambda s: 2 * math.prod(s.shape)
    return pl.pallas_call(
        body,
        grid=(steps,),
        in_specs=ins,
        out_specs=[spec for spec, _ in outs],
        out_shape=[form for _, form in outs],
        scratch_shapes=scratch,
        input_output_aliases=aliases or {},
        compiler_params=pltpu.CompilerParams(vmem_limit_bytes=limit * 1024 * 1024),
        cost_estimate=pl.CostEstimate(
            flops=int(flops), bytes_accessed=2 * sum(size(f) for _, f in outs), transcendentals=0
        ),
        name=name,
    )


LANES = 128
UP = 6 * B
REST = UP + 9 * B + LANES
DOWN = 6 * B
UNIT = 2 * ROWS * C * C
FULL = (tile(), shape(ROWS, C))


def store(rows, kind=BF):
    return pltpu.VMEM((rows, C), kind)


def edges(x, cot):
    last = jnp.concatenate([x[ROWS - 4 * PAD :], cot[ROWS - 2 * PAD :]], axis=0)
    first = jnp.concatenate([x[: 4 * PAD], cot[: 2 * PAD]], axis=0)
    top = lax.ppermute(last, SEQ, [(i, i + 1) for i in range(BLOCKS - 1)])
    bot = lax.ppermute(first, SEQ, [(i + 1, i) for i in range(BLOCKS - 1)])
    return top, bot


SWAP = [(0, 1), (1, 0)]
SHARES = (64, (REST + DOWN) // 64, LANES)


def exchange(parts):
    return lax.all_to_all(parts, CHIPS, 0, 0, tiled=True)


def other_core(cells):
    return lax.ppermute(cells, "core", SWAP)


def local(features, cotangent, strand_pairs, dilations, down_weight, conv_weight, up_weight):
    x = features[0]
    cot = cotangent[0]
    pairs = strand_pairs.reshape(1, C)
    factor = 1.0 / math.sqrt(131072.0)
    block = lax.axis_index(SEQ).reshape(1)
    resident = whole(ROWS, C)
    taps_w = [pl.BlockSpec((None, 3, B, B), lambda i, n=n: (n, 0, 0, 0), pipeline_mode=pl.Buffered(1)) for n in range(2)]
    square_of = [pl.BlockSpec((None, C, C), lambda i, n=n: (n, 0, 0), pipeline_mode=pl.Buffered(1)) for n in range(2)]
    halo = whole(6 * PAD, C)

    top, bot = edges(x, cot)
    squares = (whole(2, C, C), shape(2, C, C))
    dcat, upcat, normed0, inner0 = call(
        k_enter, STEPS, [whole(1, C), whole(2, C, B), whole(2, B, C), tile()],
        [squares] * 2 + [FULL, FULL], [], 3 * UNIT, "enter",
    )(pairs, down_weight, up_weight, x)
    form = shape(MID_ROWS, C)
    held = call(
        k_within, 7, [scalar(), resident, resident, taps_w[0], square_of[0], square_of[1]],
        [(pl.BlockSpec((MID_TILE, C), lambda i: (i + 2, 0)), form)] * 7, [], 3 * UNIT, "within",
    )(dilations, inner0, x, conv_weight, upcat, dcat)
    act0, slope0, tm0, tp0, stream1, normed1, inner1 = call(
        k_around, 4,
        [scalar(), scalar(), resident, resident, halo, halo, square_of[0], taps_w[0], square_of[0], square_of[1]]
        + [pl.BlockSpec(memory_space=pl.ANY)] * 7,
        [(pl.BlockSpec((MID_TILE, C), lambda i: (around(i), 0)), form)] * 7,
        [store(12 * PAD), store(8 * PAD)], 3 * UNIT, "around", aliases={10 + i: i for i in range(7)},
    )(dilations, block, inner0, x, top, bot, dcat, conv_weight, upcat, dcat, *held)
    upper = (tile(TOP_TILE), shape(TOP_ROWS, C))
    act1, d_pre1, tm1, tp1 = call(
        k_top, 4, [scalar(), whole(MID_ROWS, C), resident, halo, halo, taps_w[1], square_of[1]],
        [upper] * 4, [store(TOP_ROWS)], 3 * UNIT, "top",
    )(dilations, inner1, cot, top, bot, conv_weight, upcat)
    core = lax.axis_index("core").reshape(1)
    sums = (whole(REST, LANES), shape(REST, LANES))
    downs = (whole(DOWN, LANES), shape(DOWN, LANES))
    joined = (whole(REST + DOWN, LANES), shape(REST + DOWN, LANES))
    shares = (whole(*SHARES), shape(*SHARES))
    wide_top, wide_mid, wide_back = whole(TOP_ROWS, C), whole(MID_ROWS, C), whole(BACK_ROWS, C)
    (rest1,) = call(
        functools.partial(k_sums_top, factor), 1,
        [whole(1, C), wide_top, resident, wide_top, wide_mid, wide_top, wide_top],
        [sums], [], 3 * UNIT, "sums_top",
    )(pairs, act1, cot, tm1, inner1, tp1, d_pre1)
    back = (tile(BACK_TILE), shape(BACK_ROWS, C))
    grad, d_pre0, down1 = call(
        functools.partial(k_back, factor), 3,
        [scalar(), scalar(), whole(1, C), wide_top, taps_w[1], wide_mid, wide_mid, resident, halo, halo,
         square_of[1], square_of[0], wide_mid],
        [back, back, downs],
        [store(BACK_TILE), store(BACK_TILE), store(BACK_ROWS), store(BACK_ROWS)],
        5 * UNIT, "back",
    )(dilations, block, pairs, d_pre1, conv_weight, normed1, stream1, cot, top, bot, dcat, upcat, slope0)
    send_a, keep_a = call(
        functools.partial(k_sums, factor), 1,
        [scalar(), whole(1, C), wide_mid, wide_back, wide_mid, resident, wide_mid, wide_back, sums[0]],
        [sums, sums], [pltpu.VMEM((REST, LANES), BF)], 3 * UNIT, "sums",
    )(core, pairs, act0, grad, tm0, inner0, tp0, d_pre0, rest1)
    send_b, keep_b, d_inner0 = call(
        functools.partial(k_last, factor), STEPS,
        [scalar(), scalar(), whole(1, C), wide_back, taps_w[0], resident, downs[0]],
        [downs, downs, (resident, shape(ROWS, C))],
        [store(TILE), store(TILE), pltpu.VMEM((DOWN, LANES), BF)],
        3 * UNIT, "last",
    )(core, dilations, pairs, d_pre0, conv_weight, normed0, down1)
    (parts,) = call(
        k_join, 1, [sums[0], sums[0], downs[0], downs[0]], [joined], [], 0, "join",
    )(keep_a, other_core(send_a), keep_b, other_core(send_b))
    parts, act1, d_inner0 = lax.optimization_barrier((parts, act1, d_inner0))
    (out,) = call(
        k_out, STEPS, [wide_top, wide_mid, square_of[1]], [FULL], [], UNIT, "out",
    )(act1, stream1, upcat)
    (input_grad,) = call(
        k_input, STEPS, [tile(), tile(), wide_back, square_of[0]], [FULL], [], UNIT, "input",
    )(d_inner0, x, grad, dcat)
    parts = exchange(parts.reshape(SHARES))
    parts, out, input_grad = lax.optimization_barrier((parts, out, input_grad))
    (shared,) = call(k_share, 1, [shares[0]], [shares], [], 0, "share")(parts)
    mine = exchange(shared).reshape(REST + DOWN, LANES)
    other = other_core(mine)
    grads = write_layer(core, mine, ())
    grads = write_layer(1 - core, other, grads)
    return (out[None], input_grad[None], *grads)


def solution(mesh):
    fine = Mesh(mesh.devices.reshape(2, 2, 4, 2, 4), ("xh", "core", "z", "xl", "y"))
    rows = P(("xh", "core"), SEQ, None)
    in_specs = (rows, rows, P(), P(), P(), P(), P())
    out_specs = (rows, rows, P(), P(), P())
    return jax.shard_map(local, mesh=fine, in_specs=in_specs, out_specs=out_specs, check_vma=False)
```

```python
import functools
import math

import jax
import jax.numpy as jnp
from jax import lax
from jax.experimental import pallas as pl
from jax.experimental.pallas import tpu as pltpu
from jax.sharding import Mesh, PartitionSpec as P

C = 768
B = 384
PAD = 64
ROWS = 1024
TILE = 256
STEPS = ROWS // TILE
BLOCKS = 32
MID_ROWS, TOP_ROWS, BACK_ROWS = ROWS + 6 * PAD, ROWS + 4 * PAD, ROWS + 2 * PAD
MID_TILE, TOP_TILE, BACK_TILE = 2 * PAD, TOP_ROWS // 4, BACK_ROWS // 3
EPS = 1e-06
ROOT = math.sqrt(2.0 / math.pi)
CUBE = 0.044715
BF = jnp.bfloat16
F32 = jnp.float32
SEQ = ("z", "xl", "y")
CHIPS = ("xh", "z", "xl", "y")


def mm(left, right):
    return lax.dot_general(left, right, (((1,), (0,)), ((), ())), preferred_element_type=F32)


def mm_nt(left, right):
    return lax.dot_general(left, right, (((1,), (1,)), ((), ())), preferred_element_type=F32)


def mm_tn(left, right):
    return lax.dot_general(left, right, (((0,), (0,)), ((), ())), preferred_element_type=F32)


def swap(pairs_ref):
    rows = lax.broadcasted_iota(jnp.int32, (C, C), 0)
    return (rows == pairs_ref[...]).astype(F32).astype(BF)


def scale_of(wide):
    return lax.rsqrt(jnp.mean(wide * wide, axis=-1, keepdims=True) + EPS)


def lay(dst, top, mid, bot):
    start = 0
    for piece in (top, mid, bot):
        rows = piece.shape[0]
        dst[start : start + rows, :] = piece.astype(dst.dtype)
        start += rows


def shift(cells, dil, start, before, after):
    rows = before.shape[0]
    base = pl.multiple_of(start + PAD, 16)

    @pl.when(dil >= 16)
    def _():
        for sign, ref in ((-1, before), (1, after)):
            ref[...] = cells[pl.ds(pl.multiple_of(base + sign * dil, 16), rows), :]

    for small in (1, 2, 4, 8):

        @pl.when(dil == small)
        def _():
            window = cells[pl.ds(pl.multiple_of(base - 16, 16), rows + 32), :].astype(F32)
            before[...] = window[16 - small : 16 - small + rows].astype(BF)
            after[...] = window[16 + small : 16 + small + rows].astype(BF)


def centre(cells, start, rows):
    return cells[pl.ds(pl.multiple_of(start + PAD, 16), rows), :]


def conv(first, last, mid, weight, product=mm):
    rows = mid.shape[0]
    rows_a = jnp.concatenate([first[:, :B], mid[:, :B], last[:, :B]], axis=1)
    rows_b = jnp.concatenate([last[:, B:], mid[:, B:], first[:, B:]], axis=1)
    both = product(jnp.concatenate([rows_a, rows_b], axis=0), weight)
    return jnp.concatenate([both[:rows], both[rows:]], axis=1)


def conv_back(first, last, mid, weight):
    beside = jnp.concatenate([weight[k] for k in range(3)], axis=1)
    return conv(first, last, mid, beside, mm_nt)


def inside(block, start, values):
    rows = lax.broadcasted_iota(jnp.int32, (values.shape[0], 1), 0) + (block * ROWS + start)
    return jnp.where((rows >= 0) & (rows < BLOCKS * ROWS), values, 0.0)


def gelu_both(pre):
    sq = pre * pre
    t = jnp.tanh(pre * (ROOT + (ROOT * CUBE) * sq))
    half = 0.5 + 0.5 * t
    act = pre * half
    return act, half + (act * (1.0 - t)) * (ROOT + (3.0 * CUBE * ROOT) * sq)


def k_enter(pairs, down, up, x, dcat, upcat, normed, inner):
    @pl.when(pl.program_id(0) == 0)
    def _():
        s = swap(pairs)
        for layer in range(2):
            dcat[layer, :, :B] = down[layer]
            dcat[layer, :, B:] = mm(s, down[layer]).astype(BF)
            upcat[layer, :B, :] = up[layer]
            upcat[layer, B:, :] = mm(up[layer], s).astype(BF)

    wide = x[...].astype(F32)
    n = (wide * scale_of(wide)).astype(BF)
    normed[...] = n
    inner[...] = mm(n, dcat[0]).astype(BF)


def middle_rows(m, x, weight, upcat, dcat, act, slope, tm, tp, stream, normed):
    g, s = gelu_both(conv(tm[...], tp[...], m, weight[...].reshape(3 * B, B)))
    g = g.astype(BF)
    act[...] = g
    slope[...] = s.astype(BF)
    out = (x.astype(F32) + mm(g, upcat[...])).astype(BF)
    stream[...] = out
    wide = out.astype(F32)
    n = (wide * scale_of(wide)).astype(BF)
    normed[...] = n
    return mm(n, dcat[...])


def k_within(dil, mid, x, weight, upcat, dcat, act, slope, tm, tp, stream, normed, inner):
    start = pl.program_id(0) * MID_TILE
    shift(mid, dil[0], start, tm, tp)
    rows = centre(x, start, MID_TILE)
    m = centre(mid, start, MID_TILE)
    inner[...] = middle_rows(m, rows, weight, upcat, dcat, act, slope, tm, tp, stream, normed).astype(BF)


def k_around(dil, block, mid, x, top, bot, dcat0, weight, upcat, dcat, *rest):
    act, slope, tm, tp, stream, normed, inner, pad, field = rest[7:]
    step = pl.program_id(0)

    @pl.when(step == 0)
    def _():
        field[: 3 * PAD, :] = top[PAD : 4 * PAD, :]
        field[3 * PAD : 4 * PAD, :] = x[:PAD, :]
        field[4 * PAD : 5 * PAD, :] = x[ROWS - PAD :, :]
        field[5 * PAD :, :] = bot[: 3 * PAD, :]
        ends = []
        for halo in (top, bot):
            wide = halo[: 4 * PAD, :].astype(F32)
            ends.append(mm((wide * scale_of(wide)).astype(BF), dcat0[...]).astype(BF))
        pad[: 4 * PAD, :] = ends[0]
        pad[4 * PAD : 6 * PAD, :] = mid[: 2 * PAD, :]
        pad[6 * PAD : 8 * PAD, :] = mid[ROWS - 2 * PAD :, :]
        pad[8 * PAD :, :] = ends[1]

    start = pl.multiple_of((step + step // 2) * MID_TILE, MID_TILE)
    shift(pad, dil[0], start, tm, tp)
    m = centre(pad, start, MID_TILE)
    rows = field[pl.ds(pl.multiple_of(step * MID_TILE, MID_TILE), MID_TILE), :]
    values = middle_rows(m, rows, weight, upcat, dcat, act, slope, tm, tp, stream, normed)
    inner[...] = inside(block[0], around(step) * MID_TILE - 3 * PAD, values).astype(BF)


def around(step):
    return step + 7 * (step // 2)


def k_top(dil, mid, cot, top, bot, weight, upcat, act, d_pre, tm, tp, grad):
    start = pl.program_id(0) * TOP_TILE

    @pl.when(pl.program_id(0) == 0)
    def _():
        lay(grad, top[4 * PAD :, :], cot[...], bot[4 * PAD :, :])

    shift(mid, dil[1], start, tm, tp)
    m = centre(mid, start, TOP_TILE)
    rows = pl.ds(pl.multiple_of(start, 16), TOP_TILE)
    d_act = mm_nt(grad[rows, :], upcat[...])
    g, s = gelu_both(conv(tm[...], tp[...], m, weight[...].reshape(3 * B, B)))
    act[...] = g.astype(BF)
    d_pre[...] = (d_act * s).astype(BF)


def put(ref, start, value):
    rows, cols = value.shape
    for i in range(cols // LANES):
        ref[start + i * rows : start + (i + 1) * rows, :] = value[:, i * LANES : (i + 1) * LANES].astype(BF)


def take(ref, start, rows, cols):
    pieces = [ref[start + i * rows : start + (i + 1) * rows, :] for i in range(cols // LANES)]
    return jnp.concatenate(pieces, axis=1).astype(F32)


def own(ref, before):
    return ref[before : before + ROWS, :]


def weight_sums(factor, pairs, act, cot, taps, d_pre, rest):
    up = mm_tn(act, cot) * factor
    put(rest, 0, up[:B] + mm(up[B:].astype(BF), swap(pairs)))
    rows_a = jnp.concatenate([tap[:, :B] for tap in taps], axis=1)
    rows_b = jnp.concatenate([tap[:, B:] for tap in taps[::-1]], axis=1)
    total = (mm_tn(d_pre[:, :B], rows_a) + mm_tn(d_pre[:, B:], rows_b)) * factor
    for k in range(3):
        put(rest, UP + k * 3 * B, total[:, k * B : (k + 1) * B].T)
    rest[REST - LANES :, :] = jnp.zeros((LANES, LANES), BF)


def sort_out(core, lower, upper, send, keep):
    @pl.when(core[0] == 0)
    def _():
        send[...] = upper[...]
        keep[...] = lower[...]

    @pl.when(core[0] != 0)
    def _():
        send[...] = lower[...]
        keep[...] = upper[...]


def k_sums_top(factor, pairs, act, cot, tm, tc, tp, d_pre, stream, upcat, rest, out):
    out[...] = (own(stream, 3 * PAD).astype(F32) + mm(own(act, 2 * PAD), upcat[...])).astype(BF)
    taps = [own(tm, 2 * PAD), own(tc, 3 * PAD), own(tp, 2 * PAD)]
    weight_sums(factor, pairs, own(act, 2 * PAD), cot[...], taps, own(d_pre, 2 * PAD), rest)


def k_sums(factor, core, pairs, act, cot, tm, tc, tp, d_pre, upper, send, keep, rest):
    taps = [own(tm, 3 * PAD), tc[...], own(tp, 3 * PAD)]
    weight_sums(factor, pairs, own(act, 3 * PAD), own(cot, PAD), taps, own(d_pre, PAD), rest)
    sort_out(core, rest, upper, send, keep)


def down_sum(factor, pairs, normed, d_inner, down):
    total = mm_tn(normed, d_inner) * factor
    put(down, 0, total[:, :B] + mm(swap(pairs), total[:, B:].astype(BF)))


def k_join(keep_a, got_a, keep_b, got_b, out):
    out[:REST, :] = (keep_a[...].astype(F32) + got_a[...].astype(F32)).astype(BF)
    out[REST:, :] = (keep_b[...].astype(F32) + got_b[...].astype(F32)).astype(BF)


def k_share(parts, out):
    share = jnp.sum(parts[...].astype(F32), axis=0).astype(BF)
    out[...] = jnp.broadcast_to(share[None], out.shape)


def k_finish(core, own, other, down, kern, up):
    layer = pl.program_id(0)
    for mine, ref in ((True, own), (False, other)):

        @pl.when((core[0] == layer) == mine)
        def _():
            up[0] = take(ref, 0, B, C)
            for k in range(3):
                kern[0, k] = take(ref, UP + k * 3 * B, B, B)
            down[0] = take(ref, REST, C, B)


def norm_back(v, d_norm):
    wide = v.astype(F32)
    scale = scale_of(wide)
    mixed = jnp.mean(d_norm * wide, axis=-1, keepdims=True)
    return scale * d_norm - wide * (scale * scale * scale * mixed)


def k_back(factor, dil, block, pairs, mid, weight, normed, stream, cot, top, bot, dcat, upcat, slope,
           grad, d_pre, down, before, after, d_inner, given):
    start = pl.program_id(0) * BACK_TILE

    @pl.when(pl.program_id(0) == 0)
    def _():
        lay(given, top[5 * PAD :, :], cot[...], bot[4 * PAD : 5 * PAD, :])

    shift(mid, dil[1], start, before, after)
    di = conv_back(after[...], before[...], centre(mid, start, BACK_TILE), weight).astype(BF)
    rows = pl.ds(pl.multiple_of(start, 16), BACK_TILE)
    saved = pl.ds(pl.multiple_of(start + 2 * PAD, 16), BACK_TILE)
    d_inner[rows, :] = di
    g = given[rows, :].astype(F32) + norm_back(stream[saved, :], mm_nt(di, dcat[...]))
    g = inside(block[0], start - PAD, g).astype(BF)
    grad[...] = g
    d_pre[...] = (mm_nt(g, upcat[...]) * slope[saved, :].astype(F32)).astype(BF)

    @pl.when(pl.program_id(0) == pl.num_programs(0) - 1)
    def _():
        down_sum(factor, pairs, own(normed, 3 * PAD), own(d_inner, PAD), down)


def k_last(factor, core, dil, pairs, mid, weight, normed, upper, send, keep, d_inner, before, after, down):
    start = pl.program_id(0) * TILE

    shift(mid, dil[0], start, before, after)
    di = conv_back(after[...], before[...], centre(mid, start, TILE), weight).astype(BF)
    d_inner[pl.ds(pl.multiple_of(start, 16), TILE), :] = di

    @pl.when(pl.program_id(0) == pl.num_programs(0) - 1)
    def _():
        down_sum(factor, pairs, normed[...], d_inner[...], down)
        sort_out(core, down, upper, send, keep)


def k_input(d_inner, x, cot, dcat, out):
    rows = pl.ds(pl.multiple_of(pl.program_id(0) * TILE + PAD, 16), TILE)
    out[...] = (cot[rows, :].astype(F32) + norm_back(x[...], mm_nt(d_inner[...], dcat[...]))).astype(BF)


def tile(rows=TILE):
    return pl.BlockSpec((rows, C), lambda i: (i, 0))


def whole(*shape):
    return pl.BlockSpec(shape, lambda i: (0,) * len(shape), pipeline_mode=pl.Buffered(1))


def scalar():
    return pl.BlockSpec(memory_space=pltpu.SMEM)


def shape(*dims, kind=BF):
    return jax.ShapeDtypeStruct(dims, kind)


def call(body, steps, ins, outs, scratch, flops, name, limit=16, aliases=None):
    size = lambda s: 2 * math.prod(s.shape)
    return pl.pallas_call(
        body,
        grid=(steps,),
        in_specs=ins,
        out_specs=[spec for spec, _ in outs],
        out_shape=[form for _, form in outs],
        scratch_shapes=scratch,
        input_output_aliases=aliases or {},
        compiler_params=pltpu.CompilerParams(vmem_limit_bytes=limit * 1024 * 1024),
        cost_estimate=pl.CostEstimate(
            flops=int(flops), bytes_accessed=2 * sum(size(f) for _, f in outs), transcendentals=0
        ),
        name=name,
    )


LANES = 128
UP = 6 * B
REST = UP + 9 * B + LANES
DOWN = 6 * B
UNIT = 2 * ROWS * C * C
FULL = (tile(), shape(ROWS, C))


def store(rows, kind=BF):
    return pltpu.VMEM((rows, C), kind)


def edges(x, cot):
    last = jnp.concatenate([x[ROWS - 4 * PAD :], cot[ROWS - 2 * PAD :]], axis=0)
    first = jnp.concatenate([x[: 4 * PAD], cot[: 2 * PAD]], axis=0)
    top = lax.ppermute(last, SEQ, [(i, i + 1) for i in range(BLOCKS - 1)])
    bot = lax.ppermute(first, SEQ, [(i + 1, i) for i in range(BLOCKS - 1)])
    return top, bot


SWAP = [(0, 1), (1, 0)]
SHARES = (64, (REST + DOWN) // 64, LANES)


def exchange(parts):
    return lax.all_to_all(parts, CHIPS, 0, 0, tiled=True)


def other_core(cells):
    return lax.ppermute(cells, "core", SWAP)


def local(features, cotangent, strand_pairs, dilations, down_weight, conv_weight, up_weight):
    x = features[0]
    cot = cotangent[0]
    pairs = strand_pairs.reshape(1, C)
    factor = 1.0 / math.sqrt(131072.0)
    block = lax.axis_index(SEQ).reshape(1)
    resident = whole(ROWS, C)
    taps_w = [pl.BlockSpec((None, 3, B, B), lambda i, n=n: (n, 0, 0, 0), pipeline_mode=pl.Buffered(1)) for n in range(2)]
    square_of = [pl.BlockSpec((None, C, C), lambda i, n=n: (n, 0, 0), pipeline_mode=pl.Buffered(1)) for n in range(2)]
    halo = whole(6 * PAD, C)

    top, bot = edges(x, cot)
    squares = (whole(2, C, C), shape(2, C, C))
    dcat, upcat, normed0, inner0 = call(
        k_enter, STEPS, [whole(1, C), whole(2, C, B), whole(2, B, C), tile()],
        [squares] * 2 + [FULL, FULL], [], 3 * UNIT, "enter",
    )(pairs, down_weight, up_weight, x)
    form = shape(MID_ROWS, C)
    held = call(
        k_within, 7, [scalar(), resident, resident, taps_w[0], square_of[0], square_of[1]],
        [(pl.BlockSpec((MID_TILE, C), lambda i: (i + 2, 0)), form)] * 7, [], 3 * UNIT, "within",
    )(dilations, inner0, x, conv_weight, upcat, dcat)
    act0, slope0, tm0, tp0, stream1, normed1, inner1 = call(
        k_around, 4,
        [scalar(), scalar(), resident, resident, halo, halo, square_of[0], taps_w[0], square_of[0], square_of[1]]
        + [pl.BlockSpec(memory_space=pl.ANY)] * 7,
        [(pl.BlockSpec((MID_TILE, C), lambda i: (around(i), 0)), form)] * 7,
        [store(12 * PAD), store(8 * PAD)], 3 * UNIT, "around", aliases={10 + i: i for i in range(7)},
    )(dilations, block, inner0, x, top, bot, dcat, conv_weight, upcat, dcat, *held)
    upper = (tile(TOP_TILE), shape(TOP_ROWS, C))
    act1, d_pre1, tm1, tp1 = call(
        k_top, 4, [scalar(), whole(MID_ROWS, C), resident, halo, halo, taps_w[1], square_of[1]],
        [upper] * 4, [store(TOP_ROWS)], 3 * UNIT, "top",
    )(dilations, inner1, cot, top, bot, conv_weight, upcat)
    core = lax.axis_index("core").reshape(1)
    sums = (whole(REST, LANES), shape(REST, LANES))
    downs = (whole(DOWN, LANES), shape(DOWN, LANES))
    joined = (whole(REST + DOWN, LANES), shape(REST + DOWN, LANES))
    shares = (whole(*SHARES), shape(*SHARES))
    wide_top, wide_mid, wide_back = whole(TOP_ROWS, C), whole(MID_ROWS, C), whole(BACK_ROWS, C)
    rest1, out = call(
        functools.partial(k_sums_top, factor), 1,
        [whole(1, C), wide_top, resident, wide_top, wide_mid, wide_top, wide_top, wide_mid, square_of[1]],
        [sums, (resident, shape(ROWS, C))], [], 3 * UNIT, "sums_top",
    )(pairs, act1, cot, tm1, inner1, tp1, d_pre1, stream1, upcat)
    back = (tile(BACK_TILE), shape(BACK_ROWS, C))
    grad, d_pre0, down1 = call(
        functools.partial(k_back, factor), 3,
        [scalar(), scalar(), whole(1, C), wide_top, taps_w[1], wide_mid, wide_mid, resident, halo, halo,
         square_of[1], square_of[0], wide_mid],
        [back, back, downs],
        [store(BACK_TILE), store(BACK_TILE), store(BACK_ROWS), store(BACK_ROWS)],
        5 * UNIT, "back",
    )(dilations, block, pairs, d_pre1, conv_weight, normed1, stream1, cot, top, bot, dcat, upcat, slope0)
    send_a, keep_a = call(
        functools.partial(k_sums, factor), 1,
        [scalar(), whole(1, C), wide_mid, wide_back, wide_mid, resident, wide_mid, wide_back, sums[0]],
        [sums, sums], [pltpu.VMEM((REST, LANES), BF)], 3 * UNIT, "sums",
    )(core, pairs, act0, grad, tm0, inner0, tp0, d_pre0, rest1)
    send_b, keep_b, d_inner0 = call(
        functools.partial(k_last, factor), STEPS,
        [scalar(), scalar(), whole(1, C), wide_back, taps_w[0], resident, downs[0]],
        [downs, downs, (resident, shape(ROWS, C))],
        [store(TILE), store(TILE), pltpu.VMEM((DOWN, LANES), BF)],
        3 * UNIT, "last",
    )(core, dilations, pairs, d_pre0, conv_weight, normed0, down1)
    (parts,) = call(
        k_join, 1, [sums[0], sums[0], downs[0], downs[0]], [joined], [], 0, "join",
    )(keep_a, other_core(send_a), keep_b, other_core(send_b))
    (input_grad,) = call(
        k_input, STEPS, [tile(), tile(), wide_back, square_of[0]], [FULL], [], UNIT, "input",
    )(d_inner0, x, grad, dcat)
    parts = exchange(parts.reshape(SHARES))
    (shared,) = call(k_share, 1, [shares[0]], [shares], [], 0, "share")(parts)
    mine = exchange(shared).reshape(REST + DOWN, LANES)
    layered = lambda *dims: (
        pl.BlockSpec((1,) + dims, lambda i: (i,) + (0,) * len(dims)), shape(2, *dims, kind=F32)
    )
    grads = call(
        k_finish, 2, [scalar()] + [joined[0]] * 2,
        [layered(C, B), layered(3, B, B), layered(B, C)], [], 0, "finish",
    )(core, mine, other_core(mine))
    return (out[None], input_grad[None], *grads)


def solution(mesh):
    fine = Mesh(mesh.devices.reshape(2, 2, 4, 2, 4), ("xh", "core", "z", "xl", "y"))
    rows = P(("xh", "core"), SEQ, None)
    in_specs = (rows, rows, P(), P(), P(), P(), P())
    out_specs = (rows, rows, P(), P(), P())
    return jax.shard_map(local, mesh=fine, in_specs=in_specs, out_specs=out_specs, check_vma=False)
```

```python
import functools
import math

import jax
import jax.numpy as jnp
from jax import lax
from jax.experimental import pallas as pl
from jax.experimental.pallas import tpu as pltpu
from jax.sharding import Mesh, PartitionSpec as P

C = 768
B = 384
PAD = 64
ROWS = 1024
TILE = 512
STEPS = ROWS // TILE
BLOCKS = 32
MID_ROWS, TOP_ROWS, BACK_ROWS = ROWS + 6 * PAD, ROWS + 4 * PAD, ROWS + 2 * PAD
MID_TILE, TOP_TILE, BACK_TILE = MID_ROWS // 4, TOP_ROWS // 2, BACK_ROWS // 2
EPS = 1e-06
ROOT = math.sqrt(2.0 / math.pi)
CUBE = 0.044715
BF = jnp.bfloat16
F32 = jnp.float32
SEQ = ("z", "xl", "y")
CHIPS = ("xh", "z", "xl", "y")


def mm(left, right):
    return lax.dot_general(left, right, (((1,), (0,)), ((), ())), preferred_element_type=F32)


def mm_nt(left, right):
    return lax.dot_general(left, right, (((1,), (1,)), ((), ())), preferred_element_type=F32)


def mm_tn(left, right):
    return lax.dot_general(left, right, (((0,), (0,)), ((), ())), preferred_element_type=F32)


def swap(pairs_ref):
    rows = lax.broadcasted_iota(jnp.int32, (C, C), 0)
    return (rows == pairs_ref[...]).astype(F32).astype(BF)


def scale_of(wide):
    return lax.rsqrt(jnp.mean(wide * wide, axis=-1, keepdims=True) + EPS)


def lay(dst, top, mid, bot):
    start = 0
    for piece in (top, mid, bot):
        rows = piece.shape[0]
        dst[start : start + rows, :] = piece.astype(dst.dtype)
        start += rows


def shift(cells, dil, start, before, after):
    rows = before.shape[0]
    base = pl.multiple_of(start + PAD, 16)

    @pl.when(dil >= 16)
    def _():
        for sign, ref in ((-1, before), (1, after)):
            ref[...] = cells[pl.ds(pl.multiple_of(base + sign * dil, 16), rows), :]

    for small in (1, 2, 4, 8):

        @pl.when(dil == small)
        def _():
            window = cells[pl.ds(pl.multiple_of(base - 16, 16), rows + 32), :].astype(F32)
            before[...] = window[16 - small : 16 - small + rows].astype(BF)
            after[...] = window[16 + small : 16 + small + rows].astype(BF)


def centre(cells, start, rows):
    return cells[pl.ds(pl.multiple_of(start + PAD, 16), rows), :]


def conv(first, last, mid, weight, product=mm):
    rows = mid.shape[0]
    rows_a = jnp.concatenate([first[:, :B], mid[:, :B], last[:, :B]], axis=1)
    rows_b = jnp.concatenate([last[:, B:], mid[:, B:], first[:, B:]], axis=1)
    both = product(jnp.concatenate([rows_a, rows_b], axis=0), weight)
    return jnp.concatenate([both[:rows], both[rows:]], axis=1)


def conv_back(first, last, mid, weight):
    beside = jnp.concatenate([weight[k] for k in range(3)], axis=1)
    return conv(first, last, mid, beside, mm_nt)


def inside(block, start, values):
    rows = lax.broadcasted_iota(jnp.int32, (values.shape[0], 1), 0) + (block * ROWS + start)
    return jnp.where((rows >= 0) & (rows < BLOCKS * ROWS), values, 0.0)


def gelu_both(pre):
    sq = pre * pre
    t = jnp.tanh(pre * (ROOT + (ROOT * CUBE) * sq))
    half = 0.5 + 0.5 * t
    act = pre * half
    return act, half + (act * (1.0 - t)) * (ROOT + (3.0 * CUBE * ROOT) * sq)


def k_enter(pairs, down, up, x, dcat, upcat, normed, inner):
    @pl.when(pl.program_id(0) == 0)
    def _():
        s = swap(pairs)
        for layer in range(2):
            dcat[layer, :, :B] = down[layer]
            dcat[layer, :, B:] = mm(s, down[layer]).astype(BF)
            upcat[layer, :B, :] = up[layer]
            upcat[layer, B:, :] = mm(up[layer], s).astype(BF)

    wide = x[...].astype(F32)
    n = (wide * scale_of(wide)).astype(BF)
    normed[...] = n
    inner[...] = mm(n, dcat[0]).astype(BF)


def k_middle(dil, block, mid, x, top, bot, dcat0, weight, upcat, dcat,
             act, slope, tm, tp, stream, normed, inner, pad, field):
    start = pl.program_id(0) * MID_TILE

    @pl.when(pl.program_id(0) == 0)
    def _():
        lay(field, top[PAD : 4 * PAD, :], x[...], bot[: 3 * PAD, :])
        ends = []
        for halo in (top, bot):
            wide = halo[...].astype(F32)
            ends.append(mm((wide * scale_of(wide)).astype(BF), dcat0[...]).astype(BF))
        lay(pad, ends[0], mid[...], ends[1])

    shift(pad, dil[0], start, tm, tp)
    m = centre(pad, start, MID_TILE)
    g, s = gelu_both(conv(tm[...], tp[...], m, weight[...].reshape(3 * B, B)))
    g = g.astype(BF)
    act[...] = g
    slope[...] = s.astype(BF)
    rows = pl.ds(pl.multiple_of(start, 16), MID_TILE)
    out = (field[rows, :].astype(F32) + mm(g, upcat[...])).astype(BF)
    stream[...] = out
    wide = out.astype(F32)
    n = (wide * scale_of(wide)).astype(BF)
    normed[...] = n
    inner[...] = inside(block[0], start - 3 * PAD, mm(n, dcat[...])).astype(BF)


def k_top(dil, mid, cot, top, bot, weight, upcat, act, d_pre, tm, tp, grad):
    start = pl.program_id(0) * TOP_TILE

    @pl.when(pl.program_id(0) == 0)
    def _():
        lay(grad, top[...], cot[...], bot[...])

    shift(mid, dil[1], start, tm, tp)
    m = centre(mid, start, TOP_TILE)
    rows = pl.ds(pl.multiple_of(start, 16), TOP_TILE)
    d_act = mm_nt(grad[rows, :], upcat[...])
    g, s = gelu_both(conv(tm[...], tp[...], m, weight[...].reshape(3 * B, B)))
    act[...] = g.astype(BF)
    d_pre[...] = (d_act * s).astype(BF)


def put(ref, start, value):
    rows, cols = value.shape
    for i in range(cols // LANES):
        ref[start + i * rows : start + (i + 1) * rows, :] = value[:, i * LANES : (i + 1) * LANES].astype(BF)


def take(ref, start, rows, cols):
    pieces = [ref[start + i * rows : start + (i + 1) * rows, :] for i in range(cols // LANES)]
    return jnp.concatenate(pieces, axis=1).astype(F32)


def own(ref, before):
    return ref[before : before + ROWS, :]


def weight_sums(factor, pairs, act, cot, taps, d_pre, rest):
    up = mm_tn(act, cot) * factor
    put(rest, 0, up[:B] + mm(up[B:].astype(BF), swap(pairs)))
    rows_a = jnp.concatenate([tap[:, :B] for tap in taps], axis=1)
    rows_b = jnp.concatenate([tap[:, B:] for tap in taps[::-1]], axis=1)
    total = (mm_tn(d_pre[:, :B], rows_a) + mm_tn(d_pre[:, B:], rows_b)) * factor
    for k in range(3):
        put(rest, UP + k * 3 * B, total[:, k * B : (k + 1) * B].T)
    rest[REST - LANES :, :] = jnp.zeros((LANES, LANES), BF)


def sort_out(core, lower, upper, send, keep):
    @pl.when(core[0] == 0)
    def _():
        send[...] = upper[...]
        keep[...] = lower[...]

    @pl.when(core[0] != 0)
    def _():
        send[...] = lower[...]
        keep[...] = upper[...]


def k_sums_top(factor, pairs, act, cot, tm, tc, tp, d_pre, rest):
    taps = [own(tm, 2 * PAD), own(tc, 3 * PAD), own(tp, 2 * PAD)]
    weight_sums(factor, pairs, own(act, 2 * PAD), cot[...], taps, own(d_pre, 2 * PAD), rest)


def k_sums(factor, core, pairs, act, cot, tm, tc, tp, d_pre, upper, send, keep, rest):
    taps = [own(tm, 3 * PAD), tc[...], own(tp, 3 * PAD)]
    weight_sums(factor, pairs, own(act, 3 * PAD), own(cot, PAD), taps, own(d_pre, PAD), rest)
    sort_out(core, rest, upper, send, keep)


def down_sum(factor, pairs, normed, d_inner, down):
    total = mm_tn(normed, d_inner) * factor
    put(down, 0, total[:, :B] + mm(swap(pairs), total[:, B:].astype(BF)))


def k_join(keep_a, got_a, keep_b, got_b, out):
    out[:REST, :] = (keep_a[...].astype(F32) + got_a[...].astype(F32)).astype(BF)
    out[REST:, :] = (keep_b[...].astype(F32) + got_b[...].astype(F32)).astype(BF)


def k_share(parts, out):
    share = jnp.sum(parts[...].astype(F32), axis=0).astype(BF)
    out[...] = jnp.broadcast_to(share[None], out.shape)


def k_finish(layer, ref, *rest):
    down, kern, up = rest[-3:]
    up[0] = take(ref, 0, B, C)
    for k in range(3):
        kern[0, k] = take(ref, UP + k * 3 * B, B, B)
    down[0] = take(ref, REST, C, B)


def write_layer(layer, total, outs):
    dims = ((C, B), (3, B, B), (B, C))
    blocks = [pl.BlockSpec((1,) + d, lambda i, n, d=d: (n[0],) + (0,) * len(d)) for d in dims]
    return pl.pallas_call(
        k_finish,
        grid_spec=pltpu.PrefetchScalarGridSpec(
            num_scalar_prefetch=1,
            grid=(1,),
            in_specs=[pl.BlockSpec(total.shape, lambda i, n: (0, 0))] + [pl.BlockSpec(memory_space=pl.ANY)] * len(outs),
            out_specs=blocks,
        ),
        out_shape=[shape(2, *d, kind=F32) for d in dims],
        input_output_aliases={2 + i: i for i in range(len(outs))},
        compiler_params=pltpu.CompilerParams(vmem_limit_bytes=20 * 1024 * 1024),
        name="finish",
    )(layer, total, *outs)


def norm_back(v, d_norm):
    wide = v.astype(F32)
    scale = scale_of(wide)
    mixed = jnp.mean(d_norm * wide, axis=-1, keepdims=True)
    return scale * d_norm - wide * (scale * scale * scale * mixed)


def k_back(factor, dil, block, pairs, mid, weight, normed, stream, cot, top, bot, dcat, upcat, slope,
           grad, d_pre, down, before, after, d_inner, given):
    start = pl.program_id(0) * BACK_TILE

    @pl.when(pl.program_id(0) == 0)
    def _():
        lay(given, top[PAD:, :], cot[...], bot[:PAD, :])

    shift(mid, dil[1], start, before, after)
    di = conv_back(after[...], before[...], centre(mid, start, BACK_TILE), weight).astype(BF)
    rows = pl.ds(pl.multiple_of(start, 16), BACK_TILE)
    saved = pl.ds(pl.multiple_of(start + 2 * PAD, 16), BACK_TILE)
    d_inner[rows, :] = di
    g = given[rows, :].astype(F32) + norm_back(stream[saved, :], mm_nt(di, dcat[...]))
    g = inside(block[0], start - PAD, g).astype(BF)
    grad[...] = g
    d_pre[...] = (mm_nt(g, upcat[...]) * slope[saved, :].astype(F32)).astype(BF)

    @pl.when(pl.program_id(0) == pl.num_programs(0) - 1)
    def _():
        down_sum(factor, pairs, own(normed, 3 * PAD), own(d_inner, PAD), down)


def k_last(factor, core, dil, pairs, mid, weight, normed, upper, send, keep, d_inner, before, after, down):
    start = pl.program_id(0) * TILE

    shift(mid, dil[0], start, before, after)
    di = conv_back(after[...], before[...], centre(mid, start, TILE), weight).astype(BF)
    d_inner[pl.ds(pl.multiple_of(start, 16), TILE), :] = di

    @pl.when(pl.program_id(0) == pl.num_programs(0) - 1)
    def _():
        down_sum(factor, pairs, normed[...], d_inner[...], down)
        sort_out(core, down, upper, send, keep)


def k_out(act, stream, upcat, out):
    step = pl.program_id(0) * TILE
    rows = pl.ds(pl.multiple_of(step + 2 * PAD, 16), TILE)
    base = pl.ds(pl.multiple_of(step + 3 * PAD, 16), TILE)
    out[...] = (stream[base, :].astype(F32) + mm(act[rows, :], upcat[...])).astype(BF)


def k_input(d_inner, x, cot, dcat, out):
    rows = pl.ds(pl.multiple_of(pl.program_id(0) * TILE + PAD, 16), TILE)
    out[...] = (cot[rows, :].astype(F32) + norm_back(x[...], mm_nt(d_inner[...], dcat[...]))).astype(BF)


def tile(rows=TILE):
    return pl.BlockSpec((rows, C), lambda i: (i, 0))


def whole(*shape):
    return pl.BlockSpec(shape, lambda i: (0,) * len(shape), pipeline_mode=pl.Buffered(1))


def scalar():
    return pl.BlockSpec(memory_space=pltpu.SMEM)


def shape(*dims, kind=BF):
    return jax.ShapeDtypeStruct(dims, kind)


def call(body, steps, ins, outs, scratch, flops, name, limit=20):
    size = lambda s: 2 * math.prod(s.shape)
    return pl.pallas_call(
        body,
        grid=(steps,),
        in_specs=ins,
        out_specs=[spec for spec, _ in outs],
        out_shape=[form for _, form in outs],
        scratch_shapes=scratch,
        compiler_params=pltpu.CompilerParams(vmem_limit_bytes=limit * 1024 * 1024),
        cost_estimate=pl.CostEstimate(
            flops=int(flops), bytes_accessed=2 * sum(size(f) for _, f in outs), transcendentals=0
        ),
        name=name,
    )


LANES = 128
UP = 6 * B
REST = UP + 9 * B + LANES
DOWN = 6 * B
UNIT = 2 * ROWS * C * C
FULL = (tile(), shape(ROWS, C))


def store(rows, kind=BF):
    return pltpu.VMEM((rows, C), kind)


def edges(cells, rows):
    top = lax.ppermute(cells[ROWS - rows :], SEQ, [(i, i + 1) for i in range(BLOCKS - 1)])
    bot = lax.ppermute(cells[:rows], SEQ, [(i + 1, i) for i in range(BLOCKS - 1)])
    return top, bot


SWAP = [(0, 1), (1, 0)]
SHARES = (64, (REST + DOWN) // 64, LANES)


def exchange(parts):
    return lax.all_to_all(parts, CHIPS, 0, 0, tiled=True)


def other_core(cells):
    return lax.ppermute(cells, "core", SWAP)


def local(features, cotangent, strand_pairs, dilations, down_weight, conv_weight, up_weight):
    x = features[0]
    cot = cotangent[0]
    pairs = strand_pairs.reshape(1, C)
    factor = 1.0 / math.sqrt(131072.0)
    block = lax.axis_index(SEQ).reshape(1)
    resident = whole(ROWS, C)
    taps_w = [pl.BlockSpec((None, 3, B, B), lambda i, n=n: (n, 0, 0, 0), pipeline_mode=pl.Buffered(1)) for n in range(2)]
    square_of = [pl.BlockSpec((None, C, C), lambda i, n=n: (n, 0, 0), pipeline_mode=pl.Buffered(1)) for n in range(2)]
    halo, c_halo = whole(4 * PAD, C), whole(2 * PAD, C)

    top, bot = edges(x, 4 * PAD)
    ctop, cbot = edges(cot, 2 * PAD)
    squares = (whole(2, C, C), shape(2, C, C))
    dcat, upcat, normed0, inner0 = call(
        k_enter, STEPS, [whole(1, C), whole(2, C, B), whole(2, B, C), tile()],
        [squares] * 2 + [FULL, FULL], [], 3 * UNIT, "enter",
    )(pairs, down_weight, up_weight, x)
    mid = (tile(MID_TILE), shape(MID_ROWS, C))
    act0, slope0, tm0, tp0, stream1, normed1, inner1 = call(
        k_middle, 4,
        [scalar(), scalar(), resident, resident, halo, halo, square_of[0], taps_w[0], square_of[0], square_of[1]],
        [mid] * 7, [store(ROWS + 8 * PAD), store(MID_ROWS)], 6 * UNIT, "middle",
    )(dilations, block, inner0, x, top, bot, dcat, conv_weight, upcat, dcat)
    upper = (tile(TOP_TILE), shape(TOP_ROWS, C))
    act1, d_pre1, tm1, tp1 = call(
        k_top, 2, [scalar(), whole(MID_ROWS, C), resident, c_halo, c_halo, taps_w[1], square_of[1]],
        [upper] * 4, [store(TOP_ROWS)], 3 * UNIT, "top",
    )(dilations, inner1, cot, ctop, cbot, conv_weight, upcat)
    core = lax.axis_index("core").reshape(1)
    sums = (whole(REST, LANES), shape(REST, LANES))
    downs = (whole(DOWN, LANES), shape(DOWN, LANES))
    joined = (whole(REST + DOWN, LANES), shape(REST + DOWN, LANES))
    shares = (whole(*SHARES), shape(*SHARES))
    wide_top, wide_mid, wide_back = whole(TOP_ROWS, C), whole(MID_ROWS, C), whole(BACK_ROWS, C)
    (rest1,) = call(
        functools.partial(k_sums_top, factor), 1,
        [whole(1, C), wide_top, resident, wide_top, wide_mid, wide_top, wide_top],
        [sums], [], 3 * UNIT, "sums_top",
    )(pairs, act1, cot, tm1, inner1, tp1, d_pre1)
    back = (tile(BACK_TILE), shape(BACK_ROWS, C))
    grad, d_pre0, down1 = call(
        functools.partial(k_back, factor), 2,
        [scalar(), scalar(), whole(1, C), wide_top, taps_w[1], wide_mid, wide_mid, resident, c_halo, c_halo,
         square_of[1], square_of[0], wide_mid],
        [back, back, downs],
        [store(BACK_TILE), store(BACK_TILE), store(BACK_ROWS), store(BACK_ROWS)],
        5 * UNIT, "back",
    )(dilations, block, pairs, d_pre1, conv_weight, normed1, stream1, cot, ctop, cbot, dcat, upcat, slope0)
    send_a, keep_a = call(
        functools.partial(k_sums, factor), 1,
        [scalar(), whole(1, C), wide_mid, wide_back, wide_mid, resident, wide_mid, wide_back, sums[0]],
        [sums, sums], [pltpu.VMEM((REST, LANES), BF)], 3 * UNIT, "sums",
    )(core, pairs, act0, grad, tm0, inner0, tp0, d_pre0, rest1)
    send_b, keep_b, d_inner0 = call(
        functools.partial(k_last, factor), STEPS,
        [scalar(), scalar(), whole(1, C), wide_back, taps_w[0], resident, downs[0]],
        [downs, downs, (resident, shape(ROWS, C))],
        [store(TILE), store(TILE), pltpu.VMEM((DOWN, LANES), BF)],
        3 * UNIT, "last",
    )(core, dilations, pairs, d_pre0, conv_weight, normed0, down1)
    (parts,) = call(
        k_join, 1, [sums[0], sums[0], downs[0], downs[0]], [joined], [], 0, "join",
    )(keep_a, other_core(send_a), keep_b, other_core(send_b))
    parts, act1, d_inner0 = lax.optimization_barrier((parts, act1, d_inner0))
    (out,) = call(
        k_out, STEPS, [wide_top, wide_mid, square_of[1]], [FULL], [], UNIT, "out",
    )(act1, stream1, upcat)
    (input_grad,) = call(
        k_input, STEPS, [tile(), tile(), wide_back, square_of[0]], [FULL], [], UNIT, "input",
    )(d_inner0, x, grad, dcat)
    parts = exchange(parts.reshape(SHARES))
    parts, out, input_grad = lax.optimization_barrier((parts, out, input_grad))
    (shared,) = call(k_share, 1, [shares[0]], [shares], [], 0, "share")(parts)
    mine = exchange(shared).reshape(REST + DOWN, LANES)
    other = other_core(mine)
    grads = write_layer(core, mine, ())
    grads = write_layer(1 - core, other, grads)
    return (out[None], input_grad[None], *grads)


def solution(mesh):
    fine = Mesh(mesh.devices.reshape(2, 2, 4, 2, 4), ("xh", "core", "z", "xl", "y"))
    rows = P(("xh", "core"), SEQ, None)
    in_specs = (rows, rows, P(), P(), P(), P(), P())
    out_specs = (rows, rows, P(), P(), P())
    return jax.shard_map(local, mesh=fine, in_specs=in_specs, out_specs=out_specs, check_vma=False)
```

```python
import functools
import math

import jax
import jax.numpy as jnp
from jax import lax
from jax.experimental import pallas as pl
from jax.experimental.pallas import tpu as pltpu
from jax.sharding import Mesh, PartitionSpec as P

C = 768
B = 384
PAD = 64
ROWS = 1024
TILE = 512
STEPS = ROWS // TILE
BLOCKS = 32
MID_ROWS, TOP_ROWS, BACK_ROWS = ROWS + 6 * PAD, ROWS + 4 * PAD, ROWS + 2 * PAD
MID_TILE, TOP_TILE, BACK_TILE = MID_ROWS // 2, TOP_ROWS // 2, BACK_ROWS // 2
EPS = 1e-06
ROOT = math.sqrt(2.0 / math.pi)
CUBE = 0.044715
BF = jnp.bfloat16
F32 = jnp.float32
SEQ = ("z", "xl", "y")
CHIPS = ("xh", "z", "xl", "y")


def mm(left, right):
    return lax.dot_general(left, right, (((1,), (0,)), ((), ())), preferred_element_type=F32)


def mm_nt(left, right):
    return lax.dot_general(left, right, (((1,), (1,)), ((), ())), preferred_element_type=F32)


def mm_tn(left, right):
    return lax.dot_general(left, right, (((0,), (0,)), ((), ())), preferred_element_type=F32)


def swap(pairs_ref):
    rows = lax.broadcasted_iota(jnp.int32, (C, C), 0)
    return (rows == pairs_ref[...]).astype(F32).astype(BF)


def scale_of(wide):
    return lax.rsqrt(jnp.mean(wide * wide, axis=-1, keepdims=True) + EPS)


def lay(dst, top, mid, bot):
    start = 0
    for piece in (top, mid, bot):
        rows = piece.shape[0]
        dst[start : start + rows, :] = piece.astype(dst.dtype)
        start += rows


def shift(cells, dil, start, before, after):
    rows = before.shape[0]
    base = pl.multiple_of(start + PAD, 16)

    @pl.when(dil >= 16)
    def _():
        for sign, ref in ((-1, before), (1, after)):
            ref[...] = cells[pl.ds(pl.multiple_of(base + sign * dil, 16), rows), :]

    for small in (1, 2, 4, 8):

        @pl.when(dil == small)
        def _():
            window = cells[pl.ds(pl.multiple_of(base - 16, 16), rows + 32), :].astype(F32)
            before[...] = window[16 - small : 16 - small + rows].astype(BF)
            after[...] = window[16 + small : 16 + small + rows].astype(BF)


def centre(cells, start, rows):
    return cells[pl.ds(pl.multiple_of(start + PAD, 16), rows), :]


def conv(first, last, mid, weight, product=mm):
    rows = mid.shape[0]
    rows_a = jnp.concatenate([first[:, :B], mid[:, :B], last[:, :B]], axis=1)
    rows_b = jnp.concatenate([last[:, B:], mid[:, B:], first[:, B:]], axis=1)
    both = product(jnp.concatenate([rows_a, rows_b], axis=0), weight)
    return jnp.concatenate([both[:rows], both[rows:]], axis=1)


def conv_back(first, last, mid, weight):
    beside = jnp.concatenate([weight[k] for k in range(3)], axis=1)
    return conv(first, last, mid, beside, mm_nt)


def inside(block, start, values):
    rows = lax.broadcasted_iota(jnp.int32, (values.shape[0], 1), 0) + (block * ROWS + start)
    return jnp.where((rows >= 0) & (rows < BLOCKS * ROWS), values, 0.0)


def gelu_both(pre):
    sq = pre * pre
    t = jnp.tanh(pre * (ROOT + (ROOT * CUBE) * sq))
    half = 0.5 + 0.5 * t
    act = pre * half
    return act, half + (act * (1.0 - t)) * (ROOT + (3.0 * CUBE * ROOT) * sq)


def k_enter(pairs, down, up, x, dcat, upcat, normed, inner):
    @pl.when(pl.program_id(0) == 0)
    def _():
        s = swap(pairs)
        for layer in range(2):
            dcat[layer, :, :B] = down[layer]
            dcat[layer, :, B:] = mm(s, down[layer]).astype(BF)
            upcat[layer, :B, :] = up[layer]
            upcat[layer, B:, :] = mm(up[layer], s).astype(BF)

    wide = x[...].astype(F32)
    n = (wide * scale_of(wide)).astype(BF)
    normed[...] = n
    inner[...] = mm(n, dcat[0]).astype(BF)


def k_middle(dil, block, mid, x, top, bot, dcat0, weight, upcat, dcat,
             act, slope, tm, tp, stream, normed, inner, pad, field):
    start = pl.program_id(0) * MID_TILE

    @pl.when(pl.program_id(0) == 0)
    def _():
        lay(field, top[PAD : 4 * PAD, :], x[...], bot[: 3 * PAD, :])
        ends = []
        for halo in (top, bot):
            wide = halo[...].astype(F32)
            ends.append(mm((wide * scale_of(wide)).astype(BF), dcat0[...]).astype(BF))
        lay(pad, ends[0], mid[...], ends[1])

    shift(pad, dil[0], start, tm, tp)
    m = centre(pad, start, MID_TILE)
    g, s = gelu_both(conv(tm[...], tp[...], m, weight[...].reshape(3 * B, B)))
    g = g.astype(BF)
    act[...] = g
    slope[...] = s.astype(BF)
    rows = pl.ds(pl.multiple_of(start, 16), MID_TILE)
    out = (field[rows, :].astype(F32) + mm(g, upcat[...])).astype(BF)
    stream[...] = out
    wide = out.astype(F32)
    n = (wide * scale_of(wide)).astype(BF)
    normed[...] = n
    inner[...] = inside(block[0], start - 3 * PAD, mm(n, dcat[...])).astype(BF)


def k_top(dil, mid, cot, top, bot, weight, upcat, act, d_pre, tm, tp, grad):
    start = pl.program_id(0) * TOP_TILE

    @pl.when(pl.program_id(0) == 0)
    def _():
        lay(grad, top[...], cot[...], bot[...])

    shift(mid, dil[1], start, tm, tp)
    m = centre(mid, start, TOP_TILE)
    rows = pl.ds(pl.multiple_of(start, 16), TOP_TILE)
    d_act = mm_nt(grad[rows, :], upcat[...])
    g, s = gelu_both(conv(tm[...], tp[...], m, weight[...].reshape(3 * B, B)))
    act[...] = g.astype(BF)
    d_pre[...] = (d_act * s).astype(BF)


def put(ref, start, value):
    rows, cols = value.shape
    for i in range(cols // LANES):
        ref[start + i * rows : start + (i + 1) * rows, :] = value[:, i * LANES : (i + 1) * LANES].astype(BF)


def take(ref, start, rows, cols):
    pieces = [ref[start + i * rows : start + (i + 1) * rows, :] for i in range(cols // LANES)]
    return jnp.concatenate(pieces, axis=1).astype(F32)


def own(ref, before):
    return ref[before : before + ROWS, :]


def weight_sums(factor, pairs, act, cot, taps, d_pre, rest):
    up = mm_tn(act, cot) * factor
    put(rest, 0, up[:B] + mm(up[B:].astype(BF), swap(pairs)))
    rows_a = jnp.concatenate([tap[:, :B] for tap in taps], axis=1)
    rows_b = jnp.concatenate([tap[:, B:] for tap in taps[::-1]], axis=1)
    total = (mm_tn(d_pre[:, :B], rows_a) + mm_tn(d_pre[:, B:], rows_b)) * factor
    for k in range(3):
        put(rest, UP + k * 3 * B, total[:, k * B : (k + 1) * B].T)
    rest[REST - LANES :, :] = jnp.zeros((LANES, LANES), BF)


def sort_out(core, lower, upper, send, keep):
    @pl.when(core[0] == 0)
    def _():
        send[...] = upper[...]
        keep[...] = lower[...]

    @pl.when(core[0] != 0)
    def _():
        send[...] = lower[...]
        keep[...] = upper[...]


def k_sums_top(factor, pairs, act, cot, tm, tc, tp, d_pre, rest):
    taps = [own(tm, 2 * PAD), own(tc, 3 * PAD), own(tp, 2 * PAD)]
    weight_sums(factor, pairs, own(act, 2 * PAD), cot[...], taps, own(d_pre, 2 * PAD), rest)


def k_sums(factor, core, pairs, act, cot, tm, tc, tp, d_pre, upper, send, keep, rest):
    taps = [own(tm, 3 * PAD), tc[...], own(tp, 3 * PAD)]
    weight_sums(factor, pairs, own(act, 3 * PAD), own(cot, PAD), taps, own(d_pre, PAD), rest)
    sort_out(core, rest, upper, send, keep)


def down_sum(factor, pairs, normed, d_inner, down):
    total = mm_tn(normed, d_inner) * factor
    put(down, 0, total[:, :B] + mm(swap(pairs), total[:, B:].astype(BF)))


def k_join(keep_a, got_a, keep_b, got_b, out):
    out[:REST, :] = (keep_a[...].astype(F32) + got_a[...].astype(F32)).astype(BF)
    out[REST:, :] = (keep_b[...].astype(F32) + got_b[...].astype(F32)).astype(BF)


def k_share(parts, out):
    share = jnp.sum(parts[...].astype(F32), axis=0).astype(BF)
    out[...] = jnp.broadcast_to(share[None], out.shape)


def k_finish(layer, ref, *rest):
    down, kern, up = rest[-3:]
    up[0] = take(ref, 0, B, C)
    for k in range(3):
        kern[0, k] = take(ref, UP + k * 3 * B, B, B)
    down[0] = take(ref, REST, C, B)


def write_layer(layer, total, outs):
    dims = ((C, B), (3, B, B), (B, C))
    blocks = [pl.BlockSpec((1,) + d, lambda i, n, d=d: (n[0],) + (0,) * len(d)) for d in dims]
    return pl.pallas_call(
        k_finish,
        grid_spec=pltpu.PrefetchScalarGridSpec(
            num_scalar_prefetch=1,
            grid=(1,),
            in_specs=[pl.BlockSpec(total.shape, lambda i, n: (0, 0))] + [pl.BlockSpec(memory_space=pl.ANY)] * len(outs),
            out_specs=blocks,
        ),
        out_shape=[shape(2, *d, kind=F32) for d in dims],
        input_output_aliases={2 + i: i for i in range(len(outs))},
        compiler_params=pltpu.CompilerParams(vmem_limit_bytes=20 * 1024 * 1024),
        name="finish",
    )(layer, total, *outs)


def norm_back(v, d_norm):
    wide = v.astype(F32)
    scale = scale_of(wide)
    mixed = jnp.mean(d_norm * wide, axis=-1, keepdims=True)
    return scale * d_norm - wide * (scale * scale * scale * mixed)


def k_back(factor, dil, block, pairs, mid, weight, normed, stream, cot, top, bot, dcat, upcat, slope,
           grad, d_pre, down, before, after, d_inner, given):
    start = pl.program_id(0) * BACK_TILE

    @pl.when(pl.program_id(0) == 0)
    def _():
        lay(given, top[PAD:, :], cot[...], bot[:PAD, :])

    shift(mid, dil[1], start, before, after)
    di = conv_back(after[...], before[...], centre(mid, start, BACK_TILE), weight).astype(BF)
    rows = pl.ds(pl.multiple_of(start, 16), BACK_TILE)
    saved = pl.ds(pl.multiple_of(start + 2 * PAD, 16), BACK_TILE)
    d_inner[rows, :] = di
    g = given[rows, :].astype(F32) + norm_back(stream[saved, :], mm_nt(di, dcat[...]))
    g = inside(block[0], start - PAD, g).astype(BF)
    grad[...] = g
    d_pre[...] = (mm_nt(g, upcat[...]) * slope[saved, :].astype(F32)).astype(BF)

    @pl.when(pl.program_id(0) == pl.num_programs(0) - 1)
    def _():
        down_sum(factor, pairs, own(normed, 3 * PAD), own(d_inner, PAD), down)


def k_last(factor, core, dil, pairs, mid, weight, normed, upper, send, keep, d_inner, before, after, down):
    start = pl.program_id(0) * TILE

    shift(mid, dil[0], start, before, after)
    di = conv_back(after[...], before[...], centre(mid, start, TILE), weight).astype(BF)
    d_inner[pl.ds(pl.multiple_of(start, 16), TILE), :] = di

    @pl.when(pl.program_id(0) == pl.num_programs(0) - 1)
    def _():
        down_sum(factor, pairs, normed[...], d_inner[...], down)
        sort_out(core, down, upper, send, keep)


def k_out(act, stream, upcat, out):
    step = pl.program_id(0) * TILE
    rows = pl.ds(pl.multiple_of(step + 2 * PAD, 16), TILE)
    base = pl.ds(pl.multiple_of(step + 3 * PAD, 16), TILE)
    out[...] = (stream[base, :].astype(F32) + mm(act[rows, :], upcat[...])).astype(BF)


def k_input(d_inner, x, cot, dcat, out):
    rows = pl.ds(pl.multiple_of(pl.program_id(0) * TILE + PAD, 16), TILE)
    out[...] = (cot[rows, :].astype(F32) + norm_back(x[...], mm_nt(d_inner[...], dcat[...]))).astype(BF)


def tile(rows=TILE):
    return pl.BlockSpec((rows, C), lambda i: (i, 0))


def whole(*shape):
    return pl.BlockSpec(shape, lambda i: (0,) * len(shape), pipeline_mode=pl.Buffered(1))


def scalar():
    return pl.BlockSpec(memory_space=pltpu.SMEM)


def shape(*dims, kind=BF):
    return jax.ShapeDtypeStruct(dims, kind)


def call(body, steps, ins, outs, scratch, flops, name, limit=20):
    size = lambda s: 2 * math.prod(s.shape)
    return pl.pallas_call(
        body,
        grid=(steps,),
        in_specs=ins,
        out_specs=[spec for spec, _ in outs],
        out_shape=[form for _, form in outs],
        scratch_shapes=scratch,
        compiler_params=pltpu.CompilerParams(vmem_limit_bytes=limit * 1024 * 1024),
        cost_estimate=pl.CostEstimate(
            flops=int(flops), bytes_accessed=2 * sum(size(f) for _, f in outs), transcendentals=0
        ),
        name=name,
    )


LANES = 128
UP = 6 * B
REST = UP + 9 * B + LANES
DOWN = 6 * B
UNIT = 2 * ROWS * C * C
FULL = (tile(), shape(ROWS, C))


def store(rows, kind=BF):
    return pltpu.VMEM((rows, C), kind)


def edges(cells, rows):
    top = lax.ppermute(cells[ROWS - rows :], SEQ, [(i, i + 1) for i in range(BLOCKS - 1)])
    bot = lax.ppermute(cells[:rows], SEQ, [(i + 1, i) for i in range(BLOCKS - 1)])
    return top, bot


SWAP = [(0, 1), (1, 0)]
SHARES = (64, (REST + DOWN) // 64, LANES)


def exchange(parts):
    return lax.all_to_all(parts, CHIPS, 0, 0, tiled=True)


def other_core(cells):
    return lax.ppermute(cells, "core", SWAP)


def local(features, cotangent, strand_pairs, dilations, down_weight, conv_weight, up_weight):
    x = features[0]
    cot = cotangent[0]
    pairs = strand_pairs.reshape(1, C)
    factor = 1.0 / math.sqrt(131072.0)
    block = lax.axis_index(SEQ).reshape(1)
    resident = whole(ROWS, C)
    taps_w = [pl.BlockSpec((None, 3, B, B), lambda i, n=n: (n, 0, 0, 0), pipeline_mode=pl.Buffered(1)) for n in range(2)]
    square_of = [pl.BlockSpec((None, C, C), lambda i, n=n: (n, 0, 0), pipeline_mode=pl.Buffered(1)) for n in range(2)]
    halo, c_halo = whole(4 * PAD, C), whole(2 * PAD, C)

    top, bot = edges(x, 4 * PAD)
    ctop, cbot = edges(cot, 2 * PAD)
    squares = (whole(2, C, C), shape(2, C, C))
    dcat, upcat, normed0, inner0 = call(
        k_enter, STEPS, [whole(1, C), whole(2, C, B), whole(2, B, C), tile()],
        [squares] * 2 + [FULL, FULL], [], 3 * UNIT, "enter",
    )(pairs, down_weight, up_weight, x)
    mid = (tile(MID_TILE), shape(MID_ROWS, C))
    act0, slope0, tm0, tp0, stream1, normed1, inner1 = call(
        k_middle, 2,
        [scalar(), scalar(), resident, resident, halo, halo, square_of[0], taps_w[0], square_of[0], square_of[1]],
        [mid] * 7, [store(ROWS + 8 * PAD), store(MID_ROWS)], 6 * UNIT, "middle",
    )(dilations, block, inner0, x, top, bot, dcat, conv_weight, upcat, dcat)
    upper = (tile(TOP_TILE), shape(TOP_ROWS, C))
    act1, d_pre1, tm1, tp1 = call(
        k_top, 2, [scalar(), whole(MID_ROWS, C), resident, c_halo, c_halo, taps_w[1], square_of[1]],
        [upper] * 4, [store(TOP_ROWS)], 3 * UNIT, "top",
    )(dilations, inner1, cot, ctop, cbot, conv_weight, upcat)
    core = lax.axis_index("core").reshape(1)
    sums = (whole(REST, LANES), shape(REST, LANES))
    downs = (whole(DOWN, LANES), shape(DOWN, LANES))
    joined = (whole(REST + DOWN, LANES), shape(REST + DOWN, LANES))
    shares = (whole(*SHARES), shape(*SHARES))
    wide_top, wide_mid, wide_back = whole(TOP_ROWS, C), whole(MID_ROWS, C), whole(BACK_ROWS, C)
    (rest1,) = call(
        functools.partial(k_sums_top, factor), 1,
        [whole(1, C), wide_top, resident, wide_top, wide_mid, wide_top, wide_top],
        [sums], [], 3 * UNIT, "sums_top",
    )(pairs, act1, cot, tm1, inner1, tp1, d_pre1)
    back = (tile(BACK_TILE), shape(BACK_ROWS, C))
    grad, d_pre0, down1 = call(
        functools.partial(k_back, factor), 2,
        [scalar(), scalar(), whole(1, C), wide_top, taps_w[1], wide_mid, wide_mid, resident, c_halo, c_halo,
         square_of[1], square_of[0], wide_mid],
        [back, back, downs],
        [store(BACK_TILE), store(BACK_TILE), store(BACK_ROWS), store(BACK_ROWS)],
        5 * UNIT, "back",
    )(dilations, block, pairs, d_pre1, conv_weight, normed1, stream1, cot, ctop, cbot, dcat, upcat, slope0)
    send_a, keep_a = call(
        functools.partial(k_sums, factor), 1,
        [scalar(), whole(1, C), wide_mid, wide_back, wide_mid, resident, wide_mid, wide_back, sums[0]],
        [sums, sums], [pltpu.VMEM((REST, LANES), BF)], 3 * UNIT, "sums",
    )(core, pairs, act0, grad, tm0, inner0, tp0, d_pre0, rest1)
    send_b, keep_b, d_inner0 = call(
        functools.partial(k_last, factor), STEPS,
        [scalar(), scalar(), whole(1, C), wide_back, taps_w[0], resident, downs[0]],
        [downs, downs, (resident, shape(ROWS, C))],
        [store(TILE), store(TILE), pltpu.VMEM((DOWN, LANES), BF)],
        3 * UNIT, "last",
    )(core, dilations, pairs, d_pre0, conv_weight, normed0, down1)
    (parts,) = call(
        k_join, 1, [sums[0], sums[0], downs[0], downs[0]], [joined], [], 0, "join",
    )(keep_a, other_core(send_a), keep_b, other_core(send_b))
    parts, act1, d_inner0 = lax.optimization_barrier((parts, act1, d_inner0))
    (out,) = call(
        k_out, STEPS, [wide_top, wide_mid, square_of[1]], [FULL], [], UNIT, "out",
    )(act1, stream1, upcat)
    (input_grad,) = call(
        k_input, STEPS, [tile(), tile(), wide_back, square_of[0]], [FULL], [], UNIT, "input",
    )(d_inner0, x, grad, dcat)
    parts = exchange(parts.reshape(SHARES))
    parts, out, input_grad = lax.optimization_barrier((parts, out, input_grad))
    (shared,) = call(k_share, 1, [shares[0]], [shares], [], 0, "share")(parts)
    mine = exchange(shared).reshape(REST + DOWN, LANES)
    other = other_core(mine)
    grads = write_layer(core, mine, ())
    grads = write_layer(1 - core, other, grads)
    return (out[None], input_grad[None], *grads)


def solution(mesh):
    fine = Mesh(mesh.devices.reshape(2, 2, 4, 2, 4), ("xh", "core", "z", "xl", "y"))
    rows = P(("xh", "core"), SEQ, None)
    in_specs = (rows, rows, P(), P(), P(), P(), P())
    out_specs = (rows, rows, P(), P(), P())
    return jax.shard_map(local, mesh=fine, in_specs=in_specs, out_specs=out_specs, check_vma=False)
```
